32 devices in a mesh: rhs: 8 (over z, x), clus: 4 (over y, core).
Axes of the slice: x: 2, y: 2, z: 4, core: 2. Of those that a mesh axis runs over, the one named last changes fastest.
Arguments:
- incident: bfloat16 [832, 32768], P('rhs', 'clus'), may hold values from -6 to 6
- v_factors: bfloat16 [20, 2048, 128], P('clus', 'rhs'), may hold values from -0.125 to 0.125
- u_factors: bfloat16 [40, 2048, 128], P('clus', 'rhs'), may hold values from -0.5 to 0.5
- block_source: int32 [20], P('clus'), may hold values from 0 to 3
- block_rank: int32 [20], P('clus'), may hold values from 16 to 128
- block_slot: int32 [20], P('clus'), may hold values from 0 to 39, as said below
- slot_target: int32 [40], P('clus'), may hold values from 0 to 3
Outputs:
- scattered: bfloat16 [832, 32768], P('rhs', 'clus')
The draws below stay inside these ranges and needn't reach their ends.
Inputs may be any that keep to these rules, and one draw needn't show every extreme that they name: `block_slot`: every value is a slot number, all 20 values are distinct, and slot v belongs to index v // 10 of clus. The 5 blocks of one index of clus name at most 3 slots of any one index, and in every draw some index sends exactly 3 to one index and some index of clus receives exactly 10 blocks. Which slots stay empty varies.
All inputs are finite; a program needn't handle non-finite values.
Results may differ from the reference program's by a relative error of at most 0.0049.
Values may be sent and summed in bfloat16 or wider, within the bound.
No kernel may reach another device: no remote copies, remote signals or barrier semaphores. Data moves between devices by JAX's collectives and lax.ppermute only.
A program may use at most 64 MiB of HBM per device.

```python
import jax
import jax.numpy as jnp
from jax import lax

CL = 2048
R = 128
CLUS_DEV = 4
BLK_DEV = 5
CLUSTERS = 16
ORDER = 32768
COLS = 832
NB = 20
RCAP = 10
CAP = 3
N_CLUS = 4


def draw_block_slot(key, part):
    subkeys = jax.random.split(key, 5)
    hottest = jax.random.randint(subkeys[0], (), 0, N_CLUS)
    sequence = jax.random.permutation(subkeys[1], N_CLUS)
    weights = jax.random.randint(subkeys[2], (N_CLUS,), 1, 5)
    slot_scores = jax.random.randint(subkeys[3], (N_CLUS, RCAP), 0, 1 << 20) * RCAP + lax.broadcasted_iota(jnp.int32, (N_CLUS, RCAP), 1)
    shuffles = jnp.argsort(slot_scores, axis=1, stable=True).astype(jnp.int32)
    receiver_ids = jnp.arange(N_CLUS, dtype=jnp.int32)

    def sender_step(sender_turn, state):
        chosen_slots, received = state
        sender = sequence[sender_turn]

        def block_step(block_turn, inner):
            chosen_slots, received, sent_here = inner
            allowed = (sent_here < CAP) & (received < RCAP)
            jitter = jax.random.randint(jax.random.fold_in(subkeys[4], sender_turn * BLK_DEV + block_turn), (N_CLUS,), 0, 1 << 16)
            scores = jnp.where(allowed, jitter * weights * N_CLUS + receiver_ids, -1)
            receiver = jnp.where(allowed[hottest], hottest, jnp.argmax(scores)).astype(jnp.int32)
            slot_value = receiver * RCAP + shuffles[receiver, received[receiver]]
            chosen_slots = chosen_slots.at[sender, block_turn].set(slot_value)
            received = received.at[receiver].add(1)
            sent_here = sent_here.at[receiver].add(1)
            return (chosen_slots, received, sent_here)
        chosen_slots, received, sent_here = lax.fori_loop(0, BLK_DEV, block_step, (chosen_slots, received, jnp.zeros((N_CLUS,), jnp.int32)))
        return (chosen_slots, received)
    chosen_slots, received = lax.fori_loop(0, N_CLUS, sender_step, (jnp.zeros((N_CLUS, BLK_DEV), jnp.int32), jnp.zeros((N_CLUS,), jnp.int32)))
    return chosen_slots.reshape(-1)


def place_ends(array, own_key, least, largest):
    longest = array.shape.index(max(array.shape))
    spots = []
    for shift in (0, 1):
        where = [jax.random.randint(jax.random.fold_in(own_key, axis), (), 0, length) for axis, length in enumerate(array.shape)]
        where[longest] = (where[longest] + shift) % array.shape[longest]
        spots.append(tuple(where))
    return array.at[spots[0]].set(least).at[spots[1]].set(largest)


def block_scale(own_key, shape, pieces, smallest, top_value):
    loudness, own = 1.0, jax.random.fold_in(own_key, 6)
    for dim, parts in pieces:
        heights = jnp.exp(jax.random.uniform(jax.random.fold_in(own, dim), (parts,), jnp.float32, smallest / len(pieces), top_value / len(pieces)))
        loudness = loudness * jnp.repeat(heights, shape[dim] // parts).reshape([-1 if axis == dim else 1 for axis in range(len(shape))])
    return loudness


def centred(own_key, shape, deviation, most, cuts=(), kind=jnp.bfloat16):
    drawn = jax.random.normal(own_key, shape, jnp.float32) * deviation
    if len(cuts) > 0:
        drawn = block_scale(own_key, shape, cuts, -0.22, 0.18) * drawn
    return jnp.clip(drawn, min=-most, max=most).astype(kind)


def setup_inputs(seed: int = 0) -> dict:
    splits = jax.random.split(jax.random.key(seed), 8)
    return {
        "incident": centred(splits[0], (COLS, ORDER), 1.0, 6.0, ((0, 8), (1, 4))),
        "v_factors": centred(splits[1], (NB, CL, R), CL ** -0.5, 0.125, ((0, 4), (1, 8))),
        "u_factors": centred(splits[2], (N_CLUS * RCAP, CL, R), R ** -0.5, 0.5, ((0, 4), (1, 8))),
        "block_source": place_ends(jax.random.randint(splits[3], (NB,), 0, CLUS_DEV), jax.random.fold_in(splits[3], 1), 0, CLUS_DEV - 1).astype(jnp.int32),
        "block_rank": place_ends(jax.random.randint(splits[4], (NB,), R // 8, R + 1), jax.random.fold_in(splits[4], 1), R // 8, R).astype(jnp.int32),
        "block_slot": draw_block_slot(jax.random.fold_in(splits[7], 71), 0),
        "slot_target": place_ends(jax.random.randint(splits[6], (N_CLUS * RCAP,), 0, CLUS_DEV), jax.random.fold_in(splits[6], 1), 0, CLUS_DEV - 1).astype(jnp.int32),
    }


def reference(incident, v_factors, u_factors, block_source, block_rank, block_slot, slot_target):
    columns = incident.shape[0]
    sources = incident.reshape(columns, CLUSTERS, CL)
    rank_range = jnp.arange(R, dtype=jnp.int32)

    def project(block_index):
        cluster = (block_index // BLK_DEV) * CLUS_DEV + block_source[block_index]
        window = lax.dynamic_index_in_dim(sources, cluster, axis=1, keepdims=False)
        product = jnp.dot(window, v_factors[block_index], preferred_element_type=jnp.float32)
        masked = jnp.where(rank_range[None, :] < block_rank[block_index], product, jnp.zeros_like(product))
        return masked.astype(jnp.bfloat16)

    compressed = lax.map(project, jnp.arange(NB, dtype=jnp.int32))
    slot_rows = jnp.zeros((N_CLUS * RCAP, columns, R), jnp.bfloat16).at[block_slot].set(compressed)
    cluster_range = jnp.arange(CLUS_DEV, dtype=jnp.int32)

    def expand(device):
        def add_slot(running, local_slot):
            slot_index = device * RCAP + local_slot
            product = jnp.dot(slot_rows[slot_index], u_factors[slot_index].T, preferred_element_type=jnp.float32)
            owner = (cluster_range == slot_target[slot_index]).astype(jnp.float32)
            return running + owner[None, :, None] * product[:, None, :], None

        running, _unused = lax.scan(add_slot, jnp.zeros((columns, CLUS_DEV, CL), jnp.float32), jnp.arange(RCAP, dtype=jnp.int32))
        return running.astype(jnp.bfloat16)

    per_device = lax.map(expand, jnp.arange(N_CLUS, dtype=jnp.int32))
    return jnp.transpose(per_device, (1, 0, 2, 3)).reshape(columns, ORDER)
```

```python
import functools

import jax
import jax.numpy as jnp
from jax import lax
from jax.experimental import pallas as pl
from jax.experimental.pallas import tpu as pltpu
from jax.sharding import PartitionSpec as P

VMEM = pl.BlockSpec(memory_space=pltpu.VMEM)
SMEM = pl.BlockSpec(memory_space=pltpu.SMEM)
LIMIT = 32 * 1024 * 1024


def call(body, out_shape, in_specs, name, flops=0, moved=0, scratch=()):
    out_specs = [VMEM] * len(out_shape) if isinstance(out_shape, list) else VMEM
    return pl.pallas_call(
        body,
        out_shape=out_shape,
        in_specs=in_specs,
        out_specs=out_specs,
        scratch_shapes=list(scratch),
        compiler_params=pltpu.CompilerParams(vmem_limit_bytes=LIMIT),
        cost_estimate=pl.CostEstimate(flops=flops, bytes_accessed=moved, transcendentals=0),
        name=name,
    )


def pack_body(seg, pos_ref, x_ref, out_ref):
    half = 1 - pos_ref[0]
    for piece in range(out_ref.shape[1] // seg):
        start = pl.multiple_of((2 * piece + half) * seg, seg)
        out_ref[:, piece * seg : (piece + 1) * seg] = x_ref[:, pl.ds(start, seg)]


def compress_body(seg, outer, pos_ref, source_ref, x_ref, xn_ref, *refs):
    shards, out_ref = refs[:-1], refs[-1]
    half, mine = pos_ref[0], pos_ref[1]
    for block in range(out_ref.shape[0]):
        source = source_ref[block]
        own = jnp.zeros(out_ref.shape[2:], jnp.float32)
        other = jnp.zeros(out_ref.shape[2:], jnp.float32)
        for shift, shard in enumerate(shards):
            place = lax.rem(mine - shift + outer, outer)
            here = pl.multiple_of(((source * outer + place) * 2 + half) * seg, seg)
            there = pl.multiple_of((source * outer + place) * seg, seg)
            rows = shard[block]
            own += jnp.dot(x_ref[:, pl.ds(here, seg)], rows, preferred_element_type=jnp.float32)
            other += jnp.dot(xn_ref[:, pl.ds(there, seg)], rows, preferred_element_type=jnp.float32)
        out_ref[block, half] = own
        out_ref[block, 1 - half] = other


def expand_body(seg, pos_ref, index_ref, target_ref, comp_ref, u_ref, own_ref, other_ref, acc):
    half = pos_ref[0]
    acc[...] = jnp.zeros_like(acc)
    for slot in range(u_ref.shape[0]):
        block = index_ref[slot]

        @pl.when(block >= 0)
        def _():
            target = target_ref[slot]
            rows = u_ref[slot]
            for side in range(2):
                acc[target, side] += lax.dot_general(
                    comp_ref[block, side],
                    rows,
                    (((1,), (1,)), ((), ())),
                    preferred_element_type=jnp.float32,
                )

    for target in range(acc.shape[0]):
        span = slice(target * seg, (target + 1) * seg)
        own_ref[:, span] = acc[target, half].astype(own_ref.dtype)
        other_ref[:, span] = acc[target, 1 - half].astype(other_ref.dtype)


def join_body(seg, outer, clusters, pos_ref, *refs):
    out_ref = refs[-1]
    half, mine = pos_ref[0], pos_ref[1]
    for shift in range(outer):
        place = lax.rem(mine - shift + outer, outer)
        for target in range(clusters):
            span = slice(target * seg, (target + 1) * seg)
            base = (target * outer + place) * 2
            here = pl.multiple_of((base + half) * seg, seg)
            there = pl.multiple_of((base + 1 - half) * seg, seg)
            out_ref[:, pl.ds(here, seg)] = refs[shift][:, span]
            out_ref[:, pl.ds(there, seg)] = refs[outer + shift][:, span]


def after(value, *first):
    return lax.optimization_barrier((value, *first))[0]


def paired(incident, v_factors, u_factors, block_source, block_rank, block_slot, slot_target):
    columns, width = incident.shape
    blocks, seg, rank_max = v_factors.shape
    capacity = u_factors.shape[0]
    places, owners = lax.axis_size("rhs"), lax.axis_size("clus")
    outer = places // 2
    clusters = width // (seg * places)
    me, owner = lax.axis_index("rhs"), lax.axis_index("clus")
    position = jnp.stack([me % 2, me // 2]).astype(jnp.int32)

    across = [(p, p ^ 1) for p in range(places)]

    def along(array, shift):
        return lax.ppermute(
            array,
            "rhs",
            [(p, (p // 2 + shift) % outer * 2 + p % 2) for p in range(places)],
        )

    def to_owner(array, shift):
        return lax.ppermute(array, "clus", [(p, (p + shift) % owners) for p in range(owners)])

    v_shards = [v_factors] + [along(v_factors, s) for s in range(1, outer)]
    packed = call(
        functools.partial(pack_body, seg),
        jax.ShapeDtypeStruct((columns, width // 2), incident.dtype),
        [SMEM, VMEM],
        "pack",
        moved=3 * columns * width,
    )(position, incident)
    x_other = lax.ppermute(packed, "rhs", across)
    slots = jnp.concatenate([block_slot] + [to_owner(block_slot, s) for s in range(1, owners)])
    u_shards = [u_factors] + [along(after(u_factors, v_shards[s]), s) for s in range(1, outer)]

    partial = call(
        functools.partial(compress_body, seg, outer),
        jax.ShapeDtypeStruct((blocks, 2, columns, rank_max), jnp.float32),
        [SMEM, SMEM] + [VMEM] * (2 + outer),
        "compress",
        flops=4 * blocks * columns * seg * outer * rank_max,
        moved=3 * columns * width + 2 * outer * v_factors.size,
    )(position, block_source, incident, x_other, *v_shards)
    rank_index = lax.broadcasted_iota(jnp.int32, (blocks, 1, 1, rank_max), 3)
    compressed = jnp.where(
        rank_index < block_rank[:, None, None, None],
        partial + lax.ppermute(partial, "rhs", across),
        0.0,
    ).astype(jnp.bfloat16)
    gathered = jnp.concatenate(
        [compressed] + [to_owner(compressed, s) for s in range(1, owners)], axis=0
    )
    wanted = owner * capacity + lax.broadcasted_iota(jnp.int32, (capacity, slots.shape[0]), 0)
    order = lax.broadcasted_iota(jnp.int32, (capacity, slots.shape[0]), 1)
    feeding = jnp.max(jnp.where(wanted == slots[None, :], order, -1), axis=1)

    chunk = jax.ShapeDtypeStruct((columns, clusters * seg), jnp.bfloat16)
    own_parts, other_parts = [], []
    for shard in u_shards:
        own, other = call(
            functools.partial(expand_body, seg),
            [chunk, chunk],
            [SMEM, SMEM, SMEM, VMEM, VMEM],
            "expand",
            flops=4 * capacity * columns * seg * rank_max,
            moved=2 * shard.size + 2 * gathered.size + 4 * columns * clusters * seg,
            scratch=[pltpu.VMEM((clusters, 2, columns, seg), jnp.float32)],
        )(position, feeding, slot_target, gathered, shard)
        own_parts.append(own)
        other_parts.append(lax.ppermute(other, "rhs", across))
    return call(
        functools.partial(join_body, seg, outer, clusters),
        jax.ShapeDtypeStruct((columns, width), jnp.bfloat16),
        [SMEM] + [VMEM] * (2 * outer),
        "join",
        moved=4 * columns * width,
    )(position, *own_parts, *other_parts)


def gathered_plan(
    incident, v_factors, u_factors, block_source, block_rank, block_slot, slot_target
):
    columns = incident.shape[0]
    blocks = v_factors.shape[0]
    rank_max = v_factors.shape[2]
    capacity = u_factors.shape[0]
    devices = lax.axis_size("clus")
    cluster_len = v_factors.shape[1] * lax.axis_size("rhs")
    local_clusters = incident.shape[1] // cluster_len
    per_peer = max(1, (2 * blocks + devices - 1) // devices)
    sources = jnp.take(incident.reshape(columns, local_clusters, cluster_len), block_source, axis=1)
    compressed = jnp.einsum(
        "cbr,brk->bck",
        sources,
        lax.all_gather(v_factors, "rhs", axis=1, tiled=True),
        preferred_element_type=jnp.float32,
    )
    rank_index = lax.broadcasted_iota(jnp.int32, (blocks, 1, rank_max), 2)
    compressed = jnp.where(rank_index < block_rank[:, None, None], compressed, 0.0).astype(
        jnp.bfloat16
    )
    target_dev = block_slot // capacity
    target_pos = block_slot % capacity
    later_index = lax.broadcasted_iota(jnp.int32, (blocks, blocks), 0)
    earlier_index = lax.broadcasted_iota(jnp.int32, (blocks, blocks), 1)
    same_target = target_dev[None, :] == target_dev[:, None]
    before = jnp.sum((same_target & (earlier_index < later_index)).astype(jnp.int32), axis=1)
    position = target_dev * per_peer + before
    places = lax.broadcasted_iota(jnp.int32, (blocks, devices * per_peer), 1)
    placed = position[:, None] == places
    outgoing = jnp.einsum(
        "bp,bck->pck", placed.astype(jnp.bfloat16), compressed, preferred_element_type=jnp.float32
    ).astype(jnp.bfloat16)
    labels = jnp.sum(jnp.where(placed, target_pos[:, None] + 1, 0), axis=0) - 1
    arrived, arrived_labels = (
        lax.all_to_all(outgoing, "clus", split_axis=0, concat_axis=0, tiled=True),
        lax.all_to_all(labels, "clus", split_axis=0, concat_axis=0, tiled=True),
    )
    slot_ids = lax.broadcasted_iota(jnp.int32, (devices * per_peer, capacity), 1)
    landing = (arrived_labels[:, None] == slot_ids).astype(jnp.bfloat16)
    slot_rows = jnp.einsum(
        "pj,pck->jck", landing, arrived, preferred_element_type=jnp.float32
    ).astype(jnp.bfloat16)
    cluster_ids = lax.broadcasted_iota(jnp.int32, (capacity, local_clusters), 1)
    owners = (slot_target[:, None] == cluster_ids).astype(jnp.float32)
    products = jnp.einsum(
        "jck,jrk->jcr",
        slot_rows,
        lax.all_gather(u_factors, "rhs", axis=1, tiled=True),
        preferred_element_type=jnp.float32,
    )
    summed = jnp.einsum("jt,jcr->ctr", owners, products, precision=lax.Precision.HIGHEST)
    return summed.reshape(columns, local_clusters * cluster_len).astype(jnp.bfloat16)


def local(incident, v_factors, *rest):
    plan = paired if v_factors.shape[1] % 128 == 0 else gathered_plan
    return plan(incident, v_factors, *rest)


def solution(mesh):
    placed = (
        P("rhs", "clus"),
        P("clus", "rhs", None),
        P("clus", "rhs", None),
        P("clus"),
        P("clus"),
        P("clus"),
        P("clus"),
    )
    return jax.shard_map(
        local, mesh=mesh, in_specs=placed, out_specs=P("rhs", "clus"), check_vma=False
    )
```

```python
import functools

import jax
import jax.numpy as jnp
from jax import lax
from jax.experimental import pallas as pl
from jax.experimental.pallas import tpu as pltpu
from jax.sharding import PartitionSpec as P

VMEM = pl.BlockSpec(memory_space=pltpu.VMEM)
SMEM = pl.BlockSpec(memory_space=pltpu.SMEM)
LIMIT = 32 * 1024 * 1024


def call(body, out_shape, in_specs, name, flops=0, moved=0, scratch=()):
    out_specs = [VMEM] * len(out_shape) if isinstance(out_shape, list) else VMEM
    return pl.pallas_call(
        body,
        out_shape=out_shape,
        in_specs=in_specs,
        out_specs=out_specs,
        scratch_shapes=list(scratch),
        compiler_params=pltpu.CompilerParams(vmem_limit_bytes=LIMIT),
        cost_estimate=pl.CostEstimate(flops=flops, bytes_accessed=moved, transcendentals=0),
        name=name,
    )


def pack_body(seg, pos_ref, x_ref, out_ref):
    half = 1 - pos_ref[0]
    for piece in range(out_ref.shape[1] // seg):
        start = pl.multiple_of((2 * piece + half) * seg, seg)
        out_ref[:, piece * seg : (piece + 1) * seg] = x_ref[:, pl.ds(start, seg)]


def compress_body(seg, pos_ref, source_ref, x_ref, xn_ref, v0, v1, v2, v3, v4, out_ref, send_ref):
    half, mine = pos_ref[0], pos_ref[1]
    columns = x_ref.shape[0]
    out_ref[...] = jnp.zeros_like(out_ref)

    def run(shards):
        for block in range(out_ref.shape[0]):
            source = source_ref[block]
            own = other = 0.0
            for step, shard in enumerate(shards):
                piece = source * PLACES + jnp.bitwise_xor(mine, step)
                here = pl.multiple_of((piece * 2 + half) * seg, seg)
                there = pl.multiple_of(piece * seg, seg)
                rows = shard[block]
                own += jnp.dot(x_ref[:, pl.ds(here, seg)], rows, preferred_element_type=jnp.float32)
                other += jnp.dot(
                    xn_ref[:, pl.ds(there, seg)], rows, preferred_element_type=jnp.float32
                )
            out_ref[block, half, :columns] = own
            out_ref[block, 1 - half, :columns] = other

    inner = (mine == 1) | (mine == 2)

    @pl.when(inner)
    def _():
        run((v0, v1, v2, v3))

    @pl.when(jnp.logical_not(inner))
    def _():
        run((v0, v1, v2, v4))

    send_ref[...] = out_ref[...].astype(send_ref.dtype)


def land_body(index_ref, target_ref, comp_ref, rows_ref):
    clusters, rank_max = rows_ref.shape[0], comp_ref.shape[3]
    for slot in range(rows_ref.shape[3] // rank_max):
        block, target = index_ref[slot], target_ref[slot]
        found = comp_ref[jnp.maximum(block, 0)]
        for cluster in range(clusters):
            wanted = (block >= 0) & (target == cluster)
            kept = jnp.where(wanted, found, jnp.zeros_like(found))
            rows_ref[cluster, :, :, slot * rank_max : (slot + 1) * rank_max] = kept


def expand_body(seg, columns, choices, pos_ref, rows_ref, *refs):
    own_ref, other_ref, acc = refs[-3:]
    half, mine = pos_ref[0], pos_ref[1]
    clusters, sides, padded, depth = rows_ref.shape

    def run(choice):
        slots = [refs[index][slot] for index in choice for slot in range(refs[index].shape[0])]
        factor = jnp.concatenate(slots, axis=1)
        product = lax.dot_general(
            rows_ref[...].reshape(clusters * sides * padded, depth),
            factor,
            (((1,), (1,)), ((), ())),
            preferred_element_type=jnp.float32,
        )
        acc[...] = product.reshape(clusters, sides, padded, seg)

    if len(choices) == 1:
        run(choices[0])
    else:
        inner = (mine == 1) | (mine == 2)

        @pl.when(inner)
        def _():
            run(choices[0])

        @pl.when(jnp.logical_not(inner))
        def _():
            run(choices[1])

    for target in range(clusters):
        span = slice(target * seg, (target + 1) * seg)
        own_ref[:, span] = acc[target, half, :columns].astype(own_ref.dtype)
        other_ref[:, span] = acc[target, 1 - half, :columns].astype(other_ref.dtype)


def join_body(seg, clusters, pos_ref, *refs):
    out_ref = refs[-1]
    half, mine = pos_ref[0], pos_ref[1]
    for step in range(PLACES):
        place = jnp.bitwise_xor(mine, step)
        for target in range(clusters):
            span = slice(target * seg, (target + 1) * seg)
            base = (target * PLACES + place) * 2
            here = pl.multiple_of((base + half) * seg, seg)
            there = pl.multiple_of((base + 1 - half) * seg, seg)
            out_ref[:, pl.ds(here, seg)] = refs[step][:, span]
            out_ref[:, pl.ds(there, seg)] = refs[PLACES + step][:, span]


def after(value, *first):
    return lax.optimization_barrier((value, *first))[0]


PLACES = 4


def paired(incident, v_factors, u_factors, block_source, block_rank, block_slot, slot_target):
    columns, width = incident.shape
    padded = -(-columns // 16) * 16
    blocks, seg, rank_max = v_factors.shape
    capacity = u_factors.shape[0]
    owners = lax.axis_size("clus")
    clusters = width // (seg * 2 * PLACES)
    me, owner = lax.axis_index("rhs"), lax.axis_index("clus")
    position = jnp.stack([me % 2, me // 2]).astype(jnp.int32)

    def move(array, pairs):
        return lax.ppermute(array, "rhs", [(2 * a + i, 2 * b + i) for a, b in pairs for i in (0, 1)])

    def across(array):
        return lax.ppermute(array, "rhs", [(p, p ^ 1) for p in range(2 * PLACES)])

    far = [(p, p ^ 2) for p in range(PLACES)]
    near = [(p, p ^ 1) for p in range(PLACES)]
    middle = [(1, 2), (2, 1)]
    early = capacity // 2
    ends = [(1, 0), (2, 3)]

    def spread(array):
        stages, stage = [], 1
        while stage < owners:
            stages, stage = [stage] + stages, 2 * stage
        for stage in stages:
            other = lax.ppermute(array, "clus", [(p, p ^ stage) for p in range(owners)])
            array = jnp.concatenate([array, other], axis=0)
        return array

    v_far, v_near, v_middle = (
        move(v_factors, far),
        move(v_factors, near),
        move(v_factors, middle),
    )
    packed = call(
        functools.partial(pack_body, seg),
        jax.ShapeDtypeStruct((columns, width // 2), incident.dtype),
        [SMEM, VMEM],
        "pack",
        moved=3 * columns * width,
    )(position, incident)
    x_other = across(packed)
    slots = spread(block_slot)
    v_far, slots = lax.optimization_barrier((v_far, slots))
    v_ends = move(v_far, ends)
    u_first = after(u_factors, v_far)
    u_far = [move(u_first[part], far) for part in (slice(0, early), slice(early, capacity))]
    u_near, u_middle = move(u_first, near), move(u_first, middle)
    u_ends = [move(part, ends) for part in u_far]

    partial, sent = call(
        functools.partial(compress_body, seg),
        [
            jax.ShapeDtypeStruct((blocks, 2, padded, rank_max), jnp.float32),
            jax.ShapeDtypeStruct((blocks, 2, padded, rank_max), jnp.bfloat16),
        ],
        [SMEM, SMEM] + [VMEM] * 7,
        "compress",
        flops=4 * blocks * columns * seg * PLACES * rank_max,
        moved=3 * columns * width + 2 * PLACES * v_factors.size,
    )(position, block_source, incident, x_other, v_factors, v_near, v_far, v_middle, v_ends)
    rank_index = lax.broadcasted_iota(jnp.int32, (blocks, 1, 1, rank_max), 3)
    compressed = jnp.where(
        rank_index < block_rank[:, None, None, None],
        partial + across(sent).astype(jnp.float32),
        0.0,
    ).astype(jnp.bfloat16)
    gathered = spread(after(compressed, u_far[0]))
    wanted = owner * capacity + lax.broadcasted_iota(jnp.int32, (capacity, slots.shape[0]), 0)
    order = lax.broadcasted_iota(jnp.int32, (capacity, slots.shape[0]), 1)
    feeding = jnp.max(jnp.where(wanted == slots[None, :], order, -1), axis=1)
    slot_rows = call(
        land_body,
        jax.ShapeDtypeStruct((clusters, 2, padded, capacity * rank_max), jnp.bfloat16),
        [SMEM, SMEM, VMEM],
        "land",
        moved=2 * gathered.size * (1 + clusters),
    )(feeding, slot_target, after(gathered, u_far[1]))

    chunk = jax.ShapeDtypeStruct((columns, clusters * seg), jnp.bfloat16)
    own_parts, other_parts = [None] * PLACES, [None] * PLACES
    arrivals = {
        0: ([u_factors], [[0]]),
        2: (u_far, [[0, 1]]),
        1: ([u_near], [[0]]),
        3: ([u_middle, *u_ends], [[0], [1, 2]]),
    }
    finished = []
    for step, (shards, choices) in arrivals.items():
        if finished:
            slot_rows = after(slot_rows, own_parts[finished[-1]])
        if len(finished) > 1:
            slot_rows = after(slot_rows, other_parts[finished[-2]])
        own, other = call(
            functools.partial(expand_body, seg, columns, choices),
            [chunk, chunk],
            [SMEM, VMEM] + [VMEM] * len(shards),
            "expand",
            flops=4 * clusters * capacity * columns * seg * rank_max,
            moved=2 * u_factors.size + 2 * slot_rows.size + 4 * columns * clusters * seg,
            scratch=[pltpu.VMEM((clusters, 2, padded, seg), jnp.float32)],
        )(position, slot_rows, *shards)
        own_parts[step], other_parts[step] = own, across(other)
        finished.append(step)
    return call(
        functools.partial(join_body, seg, clusters),
        jax.ShapeDtypeStruct((columns, width), jnp.bfloat16),
        [SMEM] + [VMEM] * (2 * PLACES),
        "join",
        moved=4 * columns * width,
    )(position, *own_parts, *other_parts)


def gathered_plan(
    incident, v_factors, u_factors, block_source, block_rank, block_slot, slot_target
):
    columns = incident.shape[0]
    blocks = v_factors.shape[0]
    rank_max = v_factors.shape[2]
    capacity = u_factors.shape[0]
    devices = lax.axis_size("clus")
    cluster_len = v_factors.shape[1] * lax.axis_size("rhs")
    local_clusters = incident.shape[1] // cluster_len
    per_peer = max(1, (2 * blocks + devices - 1) // devices)
    sources = jnp.take(incident.reshape(columns, local_clusters, cluster_len), block_source, axis=1)
    compressed = jnp.einsum(
        "cbr,brk->bck",
        sources,
        lax.all_gather(v_factors, "rhs", axis=1, tiled=True),
        preferred_element_type=jnp.float32,
    )
    rank_index = lax.broadcasted_iota(jnp.int32, (blocks, 1, rank_max), 2)
    compressed = jnp.where(rank_index < block_rank[:, None, None], compressed, 0.0).astype(
        jnp.bfloat16
    )
    target_dev = block_slot // capacity
    target_pos = block_slot % capacity
    later_index = lax.broadcasted_iota(jnp.int32, (blocks, blocks), 0)
    earlier_index = lax.broadcasted_iota(jnp.int32, (blocks, blocks), 1)
    same_target = target_dev[None, :] == target_dev[:, None]
    before = jnp.sum((same_target & (earlier_index < later_index)).astype(jnp.int32), axis=1)
    position = target_dev * per_peer + before
    places = lax.broadcasted_iota(jnp.int32, (blocks, devices * per_peer), 1)
    placed = position[:, None] == places
    outgoing = jnp.einsum(
        "bp,bck->pck", placed.astype(jnp.bfloat16), compressed, preferred_element_type=jnp.float32
    ).astype(jnp.bfloat16)
    labels = jnp.sum(jnp.where(placed, target_pos[:, None] + 1, 0), axis=0) - 1
    arrived, arrived_labels = (
        lax.all_to_all(outgoing, "clus", split_axis=0, concat_axis=0, tiled=True),
        lax.all_to_all(labels, "clus", split_axis=0, concat_axis=0, tiled=True),
    )
    slot_ids = lax.broadcasted_iota(jnp.int32, (devices * per_peer, capacity), 1)
    landing = (arrived_labels[:, None] == slot_ids).astype(jnp.bfloat16)
    slot_rows = jnp.einsum(
        "pj,pck->jck", landing, arrived, preferred_element_type=jnp.float32
    ).astype(jnp.bfloat16)
    cluster_ids = lax.broadcasted_iota(jnp.int32, (capacity, local_clusters), 1)
    owners = (slot_target[:, None] == cluster_ids).astype(jnp.float32)
    products = jnp.einsum(
        "jck,jrk->jcr",
        slot_rows,
        lax.all_gather(u_factors, "rhs", axis=1, tiled=True),
        preferred_element_type=jnp.float32,
    )
    summed = jnp.einsum("jt,jcr->ctr", owners, products, precision=lax.Precision.HIGHEST)
    return summed.reshape(columns, local_clusters * cluster_len).astype(jnp.bfloat16)


def local(incident, v_factors, *rest):
    owners = lax.axis_size("clus")
    fits = (
        lax.axis_size("rhs") == 2 * PLACES
        and v_factors.shape[1] % 128 == 0
        and owners & (owners - 1) == 0
    )
    return (paired if fits else gathered_plan)(incident, v_factors, *rest)


def solution(mesh):
    placed = (
        P("rhs", "clus"),
        P("clus", "rhs", None),
        P("clus", "rhs", None),
        P("clus"),
        P("clus"),
        P("clus"),
        P("clus"),
    )
    return jax.shard_map(
        local, mesh=mesh, in_specs=placed, out_specs=P("rhs", "clus"), check_vma=False
    )
```

```python
import functools

import jax
import jax.numpy as jnp
from jax import lax
from jax.experimental import pallas as pl
from jax.experimental.pallas import tpu as pltpu
from jax.sharding import PartitionSpec as P

VMEM = pl.BlockSpec(memory_space=pltpu.VMEM)
SMEM = pl.BlockSpec(memory_space=pltpu.SMEM)
LIMIT = 32 * 1024 * 1024


def call(body, out_shape, in_specs, name, flops=0, moved=0, scratch=()):
    out_specs = [VMEM] * len(out_shape) if isinstance(out_shape, list) else VMEM
    return pl.pallas_call(
        body,
        out_shape=out_shape,
        in_specs=in_specs,
        out_specs=out_specs,
        scratch_shapes=list(scratch),
        compiler_params=pltpu.CompilerParams(vmem_limit_bytes=LIMIT),
        cost_estimate=pl.CostEstimate(flops=flops, bytes_accessed=moved, transcendentals=0),
        name=name,
    )


def pack_body(seg, pos_ref, x_ref, out_ref):
    half = 1 - pos_ref[0]
    for piece in range(out_ref.shape[1] // seg):
        start = pl.multiple_of((2 * piece + half) * seg, seg)
        out_ref[:, piece * seg : (piece + 1) * seg] = x_ref[:, pl.ds(start, seg)]


def compress_body(seg, pos_ref, source_ref, x_ref, xn_ref, v0, v1, v2, v3, v4, out_ref, send_ref):
    half, mine = pos_ref[0], pos_ref[1]
    columns = x_ref.shape[0]
    out_ref[...] = jnp.zeros_like(out_ref)

    def run(shards):
        for block in range(out_ref.shape[0]):
            source = source_ref[block]
            own = other = 0.0
            for step, shard in enumerate(shards):
                piece = source * PLACES + jnp.bitwise_xor(mine, step)
                here = pl.multiple_of((piece * 2 + half) * seg, seg)
                there = pl.multiple_of(piece * seg, seg)
                rows = shard[block]
                own += jnp.dot(x_ref[:, pl.ds(here, seg)], rows, preferred_element_type=jnp.float32)
                other += jnp.dot(
                    xn_ref[:, pl.ds(there, seg)], rows, preferred_element_type=jnp.float32
                )
            out_ref[block, half, :columns] = own
            out_ref[block, 1 - half, :columns] = other

    inner = (mine == 1) | (mine == 2)

    @pl.when(inner)
    def _():
        run((v0, v1, v2, v3))

    @pl.when(jnp.logical_not(inner))
    def _():
        run((v0, v1, v2, v4))

    send_ref[...] = out_ref[...].astype(send_ref.dtype)


def land_body(index_ref, target_ref, comp_ref, rows_ref):
    clusters, rank_max = rows_ref.shape[0], comp_ref.shape[3]
    for slot in range(rows_ref.shape[3] // rank_max):
        block, target = index_ref[slot], target_ref[slot]
        found = comp_ref[jnp.maximum(block, 0)]
        for cluster in range(clusters):
            wanted = (block >= 0) & (target == cluster)
            kept = jnp.where(wanted, found, jnp.zeros_like(found))
            rows_ref[cluster, :, :, slot * rank_max : (slot + 1) * rank_max] = kept


def expand_body(seg, columns, choices, pos_ref, rows_ref, *refs):
    own_ref, other_ref, acc = refs[-3:]
    half, mine = pos_ref[0], pos_ref[1]
    clusters, sides, padded, depth = rows_ref.shape

    def run(choice):
        slots = [refs[index][slot] for index in choice for slot in range(refs[index].shape[0])]
        factor = jnp.concatenate(slots, axis=1)
        product = lax.dot_general(
            rows_ref[...].reshape(clusters * sides * padded, depth),
            factor,
            (((1,), (1,)), ((), ())),
            preferred_element_type=jnp.float32,
        )
        acc[...] = product.reshape(clusters, sides, padded, seg)

    if len(choices) == 1:
        run(choices[0])
    else:
        inner = (mine == 1) | (mine == 2)

        @pl.when(inner)
        def _():
            run(choices[0])

        @pl.when(jnp.logical_not(inner))
        def _():
            run(choices[1])

    for target in range(clusters):
        span = slice(target * seg, (target + 1) * seg)
        own_ref[:, span] = acc[target, half, :columns].astype(own_ref.dtype)
        other_ref[:, span] = acc[target, 1 - half, :columns].astype(other_ref.dtype)


def join_body(seg, clusters, pos_ref, *refs):
    out_ref = refs[-1]
    half, mine = pos_ref[0], pos_ref[1]
    for step in range(PLACES):
        place = jnp.bitwise_xor(mine, step)
        for target in range(clusters):
            span = slice(target * seg, (target + 1) * seg)
            base = (target * PLACES + place) * 2
            here = pl.multiple_of((base + half) * seg, seg)
            there = pl.multiple_of((base + 1 - half) * seg, seg)
            out_ref[:, pl.ds(here, seg)] = refs[step][:, span]
            out_ref[:, pl.ds(there, seg)] = refs[PLACES + step][:, span]


def after(value, *first):
    return lax.optimization_barrier((value, *first))[0]


PLACES = 4


def paired(incident, v_factors, u_factors, block_source, block_rank, block_slot, slot_target):
    columns, width = incident.shape
    padded = -(-columns // 16) * 16
    blocks, seg, rank_max = v_factors.shape
    capacity = u_factors.shape[0]
    owners = lax.axis_size("clus")
    clusters = width // (seg * 2 * PLACES)
    me, owner = lax.axis_index("rhs"), lax.axis_index("clus")
    position = jnp.stack([me % 2, me // 2]).astype(jnp.int32)

    def move(array, pairs):
        return lax.ppermute(array, "rhs", [(2 * a + i, 2 * b + i) for a, b in pairs for i in (0, 1)])

    def across(array):
        return lax.ppermute(array, "rhs", [(p, p ^ 1) for p in range(2 * PLACES)])

    far = [(p, p ^ 2) for p in range(PLACES)]
    near = [(p, p ^ 1) for p in range(PLACES)]
    middle = [(1, 2), (2, 1)]
    early = capacity // 2
    ends = [(1, 0), (2, 3)]

    stages = [1 << bit for bit in reversed(range((owners - 1).bit_length()))]

    def double(array, stage):
        other = lax.ppermute(array, "clus", [(p, p ^ stage) for p in range(owners)])
        return jnp.concatenate([array, other], axis=0)

    v_far, v_near, v_middle = (
        move(v_factors, far),
        move(v_factors, near),
        move(v_factors, middle),
    )
    packed = call(
        functools.partial(pack_body, seg),
        jax.ShapeDtypeStruct((columns, width // 2), incident.dtype),
        [SMEM, VMEM],
        "pack",
        moved=3 * columns * width,
    )(position, incident)
    x_other = across(packed)
    slots = block_slot
    for stage in stages:
        slots = double(slots, stage)
    v_far, slots = lax.optimization_barrier((v_far, slots))
    v_ends = move(v_far, ends)
    u_first = after(u_factors, v_far)
    u_far = [move(u_first[part], far) for part in (slice(0, early), slice(early, capacity))]
    u_ends = [move(part, ends) for part in u_far]

    partial, sent = call(
        functools.partial(compress_body, seg),
        [
            jax.ShapeDtypeStruct((blocks, 2, padded, rank_max), jnp.float32),
            jax.ShapeDtypeStruct((blocks, 2, padded, rank_max), jnp.bfloat16),
        ],
        [SMEM, SMEM] + [VMEM] * 7,
        "compress",
        flops=4 * blocks * columns * seg * PLACES * rank_max,
        moved=3 * columns * width + 2 * PLACES * v_factors.size,
    )(position, block_source, incident, x_other, v_factors, v_near, v_far, v_middle, v_ends)
    received = across(sent)
    u_next = after(u_factors, received)
    u_near, u_middle = move(u_next, near), move(u_next, middle)

    def chain(_, unused):
        rank_index = lax.broadcasted_iota(jnp.int32, (blocks, 1, 1, rank_max), 3)
        rows = jnp.where(
            rank_index < block_rank[:, None, None, None],
            partial + received.astype(jnp.float32),
            0.0,
        ).astype(jnp.bfloat16)
        for stage in stages:
            rows = double(rows, stage)
        return rows

    rounds = 1 + jnp.minimum(me, 0)
    gathered = lax.fori_loop(
        0, rounds, chain, jnp.zeros((owners * blocks, 2, padded, rank_max), jnp.bfloat16)
    )
    wanted = owner * capacity + lax.broadcasted_iota(jnp.int32, (capacity, slots.shape[0]), 0)
    order = lax.broadcasted_iota(jnp.int32, (capacity, slots.shape[0]), 1)
    feeding = jnp.max(jnp.where(wanted == slots[None, :], order, -1), axis=1)
    slot_rows = call(
        land_body,
        jax.ShapeDtypeStruct((clusters, 2, padded, capacity * rank_max), jnp.bfloat16),
        [SMEM, SMEM, VMEM],
        "land",
        moved=2 * gathered.size * (1 + clusters),
    )(feeding, slot_target, after(gathered, u_far[0]))

    chunk = jax.ShapeDtypeStruct((columns, clusters * seg), jnp.bfloat16)
    own_parts, other_parts = [None] * PLACES, [None] * PLACES
    arrivals = {
        0: ([u_factors], [[0]]),
        2: (u_far, [[0, 1]]),
        1: ([u_near], [[0]]),
        3: ([u_middle, *u_ends], [[0], [1, 2]]),
    }
    finished = []
    for step, (shards, choices) in arrivals.items():
        if finished:
            slot_rows = after(slot_rows, own_parts[finished[-1]])
        if len(finished) > 1:
            slot_rows = after(slot_rows, other_parts[finished[-2]])
        if len(finished) == PLACES - 1:
            slot_rows = after(slot_rows, other_parts[finished[-1]])
        own, other = call(
            functools.partial(expand_body, seg, columns, choices),
            [chunk, chunk],
            [SMEM, VMEM] + [VMEM] * len(shards),
            "expand",
            flops=4 * clusters * capacity * columns * seg * rank_max,
            moved=2 * u_factors.size + 2 * slot_rows.size + 4 * columns * clusters * seg,
            scratch=[pltpu.VMEM((clusters, 2, padded, seg), jnp.float32)],
        )(position, slot_rows, *shards)
        own_parts[step], other_parts[step] = own, across(other)
        finished.append(step)
    return call(
        functools.partial(join_body, seg, clusters),
        jax.ShapeDtypeStruct((columns, width), jnp.bfloat16),
        [SMEM] + [VMEM] * (2 * PLACES),
        "join",
        moved=4 * columns * width,
    )(position, *own_parts, *other_parts)


def gathered_plan(
    incident, v_factors, u_factors, block_source, block_rank, block_slot, slot_target
):
    columns = incident.shape[0]
    blocks = v_factors.shape[0]
    rank_max = v_factors.shape[2]
    capacity = u_factors.shape[0]
    devices = lax.axis_size("clus")
    cluster_len = v_factors.shape[1] * lax.axis_size("rhs")
    local_clusters = incident.shape[1] // cluster_len
    per_peer = max(1, (2 * blocks + devices - 1) // devices)
    sources = jnp.take(incident.reshape(columns, local_clusters, cluster_len), block_source, axis=1)
    compressed = jnp.einsum(
        "cbr,brk->bck",
        sources,
        lax.all_gather(v_factors, "rhs", axis=1, tiled=True),
        preferred_element_type=jnp.float32,
    )
    rank_index = lax.broadcasted_iota(jnp.int32, (blocks, 1, rank_max), 2)
    compressed = jnp.where(rank_index < block_rank[:, None, None], compressed, 0.0).astype(
        jnp.bfloat16
    )
    target_dev = block_slot // capacity
    target_pos = block_slot % capacity
    later_index = lax.broadcasted_iota(jnp.int32, (blocks, blocks), 0)
    earlier_index = lax.broadcasted_iota(jnp.int32, (blocks, blocks), 1)
    same_target = target_dev[None, :] == target_dev[:, None]
    before = jnp.sum((same_target & (earlier_index < later_index)).astype(jnp.int32), axis=1)
    position = target_dev * per_peer + before
    places = lax.broadcasted_iota(jnp.int32, (blocks, devices * per_peer), 1)
    placed = position[:, None] == places
    outgoing = jnp.einsum(
        "bp,bck->pck", placed.astype(jnp.bfloat16), compressed, preferred_element_type=jnp.float32
    ).astype(jnp.bfloat16)
    labels = jnp.sum(jnp.where(placed, target_pos[:, None] + 1, 0), axis=0) - 1
    arrived, arrived_labels = (
        lax.all_to_all(outgoing, "clus", split_axis=0, concat_axis=0, tiled=True),
        lax.all_to_all(labels, "clus", split_axis=0, concat_axis=0, tiled=True),
    )
    slot_ids = lax.broadcasted_iota(jnp.int32, (devices * per_peer, capacity), 1)
    landing = (arrived_labels[:, None] == slot_ids).astype(jnp.bfloat16)
    slot_rows = jnp.einsum(
        "pj,pck->jck", landing, arrived, preferred_element_type=jnp.float32
    ).astype(jnp.bfloat16)
    cluster_ids = lax.broadcasted_iota(jnp.int32, (capacity, local_clusters), 1)
    owners = (slot_target[:, None] == cluster_ids).astype(jnp.float32)
    products = jnp.einsum(
        "jck,jrk->jcr",
        slot_rows,
        lax.all_gather(u_factors, "rhs", axis=1, tiled=True),
        preferred_element_type=jnp.float32,
    )
    summed = jnp.einsum("jt,jcr->ctr", owners, products, precision=lax.Precision.HIGHEST)
    return summed.reshape(columns, local_clusters * cluster_len).astype(jnp.bfloat16)


def local(incident, v_factors, *rest):
    owners = lax.axis_size("clus")
    fits = (
        lax.axis_size("rhs") == 2 * PLACES
        and v_factors.shape[1] % 128 == 0
        and owners > 1
        and owners & (owners - 1) == 0
    )
    return (paired if fits else gathered_plan)(incident, v_factors, *rest)


def solution(mesh):
    placed = (
        P("rhs", "clus"),
        P("clus", "rhs", None),
        P("clus", "rhs", None),
        P("clus"),
        P("clus"),
        P("clus"),
        P("clus"),
    )
    return jax.shard_map(
        local, mesh=mesh, in_specs=placed, out_specs=P("rhs", "clus"), check_vma=False
    )
```

```python
import functools

import jax
import jax.numpy as jnp
from jax import lax
from jax.experimental import pallas as pl
from jax.experimental.pallas import tpu as pltpu
from jax.sharding import PartitionSpec as P

VMEM = pl.BlockSpec(memory_space=pltpu.VMEM)
SMEM = pl.BlockSpec(memory_space=pltpu.SMEM)
LIMIT = 32 * 1024 * 1024


def call(body, out_shape, in_specs, name, flops=0, moved=0, scratch=()):
    out_specs = [VMEM] * len(out_shape) if isinstance(out_shape, list) else VMEM
    return pl.pallas_call(
        body,
        out_shape=out_shape,
        in_specs=in_specs,
        out_specs=out_specs,
        scratch_shapes=list(scratch),
        compiler_params=pltpu.CompilerParams(vmem_limit_bytes=LIMIT),
        cost_estimate=pl.CostEstimate(flops=flops, bytes_accessed=moved, transcendentals=0),
        name=name,
    )


def pack_body(seg, pos_ref, x_ref, *out_refs):
    half = 1 - pos_ref[0]
    pieces = out_refs[0].shape[1] // seg
    for piece in range(pieces * len(out_refs)):
        start = pl.multiple_of((2 * piece + half) * seg, seg)
        place = piece % pieces * seg
        out_refs[piece // pieces][:, place : place + seg] = x_ref[:, pl.ds(start, seg)]


def compress_body(seg, pos_ref, source_ref, x_ref, xl_ref, xh_ref, *refs):
    v0, v1, v2, v3, v4, out_ref, send_ref, xn_ref = refs
    half, mine = pos_ref[0], pos_ref[1]
    columns = x_ref.shape[0]
    xn_ref[:, : xl_ref.shape[1]] = xl_ref[...]
    xn_ref[:, xl_ref.shape[1] :] = xh_ref[...]
    out_ref[...] = jnp.zeros_like(out_ref)

    def run(shards):
        for block in range(out_ref.shape[0]):
            source = source_ref[block]
            own = other = 0.0
            for step, shard in enumerate(shards):
                piece = source * PLACES + jnp.bitwise_xor(mine, step)
                here = pl.multiple_of((piece * 2 + half) * seg, seg)
                there = pl.multiple_of(piece * seg, seg)
                rows = shard[block]
                own += jnp.dot(x_ref[:, pl.ds(here, seg)], rows, preferred_element_type=jnp.float32)
                other += jnp.dot(
                    xn_ref[:, pl.ds(there, seg)], rows, preferred_element_type=jnp.float32
                )
            out_ref[block, half, :columns] = own
            out_ref[block, 1 - half, :columns] = other

    inner = (mine == 1) | (mine == 2)

    @pl.when(inner)
    def _():
        run((v0, v1, v2, v3))

    @pl.when(jnp.logical_not(inner))
    def _():
        run((v0, v1, v2, v4))

    send_ref[...] = out_ref[...].astype(send_ref.dtype)


def land_body(index_ref, target_ref, comp_ref, rows_ref):
    clusters, rank_max = rows_ref.shape[0], comp_ref.shape[3]
    for slot in range(rows_ref.shape[3] // rank_max):
        block, target = index_ref[slot], target_ref[slot]
        found = comp_ref[jnp.maximum(block, 0)]
        for cluster in range(clusters):
            wanted = (block >= 0) & (target == cluster)
            kept = jnp.where(wanted, found, jnp.zeros_like(found))
            rows_ref[cluster, :, :, slot * rank_max : (slot + 1) * rank_max] = kept


def expand_body(seg, columns, choices, pos_ref, rows_ref, *refs):
    own_ref, other_ref, acc = refs[-3:]
    half, mine = pos_ref[0], pos_ref[1]
    clusters, sides, padded, depth = rows_ref.shape

    def run(choice):
        slots = [refs[index][slot] for index in choice for slot in range(refs[index].shape[0])]
        factor = jnp.concatenate(slots, axis=1)
        product = lax.dot_general(
            rows_ref[...].reshape(clusters * sides * padded, depth),
            factor,
            (((1,), (1,)), ((), ())),
            preferred_element_type=jnp.float32,
        )
        acc[...] = product.reshape(clusters, sides, padded, seg)

    if len(choices) == 1:
        run(choices[0])
    else:
        inner = (mine == 1) | (mine == 2)

        @pl.when(inner)
        def _():
            run(choices[0])

        @pl.when(jnp.logical_not(inner))
        def _():
            run(choices[1])

    for target in range(clusters):
        span = slice(target * seg, (target + 1) * seg)
        own_ref[:, span] = acc[target, half, :columns].astype(own_ref.dtype)
        other_ref[:, span] = acc[target, 1 - half, :columns].astype(other_ref.dtype)


def expand_own_body(seg, columns, pos_ref, rows_ref, u_ref, side_ref, out_ref, acc):
    half = pos_ref[0]
    clusters, sides, padded, depth = rows_ref.shape
    rows = rows_ref[:, half].reshape(clusters * padded, depth)
    for shard, place in ((u_ref, half), (side_ref, 1 - half)):
        factor = jnp.concatenate([shard[slot] for slot in range(shard.shape[0])], axis=1)
        product = lax.dot_general(
            rows, factor, (((1,), (1,)), ((), ())), preferred_element_type=jnp.float32
        )
        acc[...] = product.reshape(clusters, padded, seg)
        for target in range(clusters):
            start = pl.multiple_of((2 * target + place) * seg, seg)
            out_ref[:, pl.ds(start, seg)] = acc[target, :columns].astype(out_ref.dtype)


def join_body(seg, clusters, pos_ref, first_ref, *refs):
    out_ref = refs[-1]
    half, mine = pos_ref[0], pos_ref[1]
    for target in range(clusters):
        start = pl.multiple_of((target * PLACES + mine) * 2 * seg, 2 * seg)
        span = slice(2 * target * seg, 2 * (target + 1) * seg)
        out_ref[:, pl.ds(start, 2 * seg)] = first_ref[:, span]
    for step in range(1, PLACES):
        place = jnp.bitwise_xor(mine, step)
        for target in range(clusters):
            span = slice(target * seg, (target + 1) * seg)
            base = (target * PLACES + place) * 2
            here = pl.multiple_of((base + half) * seg, seg)
            there = pl.multiple_of((base + 1 - half) * seg, seg)
            out_ref[:, pl.ds(here, seg)] = refs[step - 1][:, span]
            out_ref[:, pl.ds(there, seg)] = refs[PLACES + step - 2][:, span]


def after(value, *first):
    return lax.optimization_barrier((value, *first))[0]


PLACES = 4


def paired(incident, v_factors, u_factors, block_source, block_rank, block_slot, slot_target):
    columns, width = incident.shape
    padded = -(-columns // 16) * 16
    blocks, seg, rank_max = v_factors.shape
    capacity = u_factors.shape[0]
    owners = lax.axis_size("clus")
    clusters = width // (seg * 2 * PLACES)
    me, owner = lax.axis_index("rhs"), lax.axis_index("clus")
    position = jnp.stack([me % 2, me // 2]).astype(jnp.int32)

    def move(array, pairs):
        return lax.ppermute(array, "rhs", [(2 * a + i, 2 * b + i) for a, b in pairs for i in (0, 1)])

    def across(array):
        return lax.ppermute(array, "rhs", [(p, p ^ 1) for p in range(2 * PLACES)])

    far = [(p, p ^ 2) for p in range(PLACES)]
    near = [(p, p ^ 1) for p in range(PLACES)]
    middle = [(1, 2), (2, 1)]
    early = capacity // 2
    ends = [(1, 0), (2, 3)]

    stages = [1 << bit for bit in reversed(range((owners - 1).bit_length()))]

    def swapped(array, stage):
        return lax.ppermute(array, "clus", [(p, p ^ stage) for p in range(owners)])

    def double(array, stage):
        return jnp.concatenate([array, swapped(array, stage)], axis=0)

    v_far, v_near, v_middle = (
        move(v_factors, far),
        move(v_factors, near),
        move(v_factors, middle),
    )
    packed = call(
        functools.partial(pack_body, seg),
        [jax.ShapeDtypeStruct((columns, width // 4), incident.dtype)] * 2,
        [SMEM, VMEM],
        "pack",
        moved=3 * columns * width,
    )(position, incident)
    x_other = [across(part) for part in packed]
    slots = block_slot
    for stage in stages:
        slots = double(slots, stage)
    v_far, slots = lax.optimization_barrier((v_far, slots))
    v_ends = move(v_far, ends)
    u_first = after(u_factors, v_near, v_middle, v_ends)
    u_side = across(after(u_factors, *x_other))
    u_far = [move(u_first[part], far) for part in (slice(0, early), slice(early, capacity))]
    u_ends = [move(part, ends) for part in u_far]

    partial, sent = call(
        functools.partial(compress_body, seg),
        [
            jax.ShapeDtypeStruct((blocks, 2, padded, rank_max), jnp.float32),
            jax.ShapeDtypeStruct((blocks, 2, padded, rank_max), jnp.bfloat16),
        ],
        [SMEM, SMEM] + [VMEM] * 8,
        "compress",
        flops=4 * blocks * columns * seg * PLACES * rank_max,
        moved=3 * columns * width + 2 * PLACES * v_factors.size,
        scratch=[pltpu.VMEM((columns, width // 2), incident.dtype)],
    )(position, block_source, incident, *x_other, v_factors, v_near, v_far, v_middle, v_ends)
    received = across(sent)
    u_next = after(u_factors, received)
    u_near, u_middle = move(u_next, near), move(u_next, middle)

    rank_index = lax.broadcasted_iota(jnp.int32, (blocks, 1, 1, rank_max), 3)
    rows = jnp.where(
        rank_index < block_rank[:, None, None, None],
        partial + received.astype(jnp.float32),
        0.0,
    ).astype(jnp.bfloat16)

    rounds, gathered = 1 + jnp.minimum(me, 0), rows
    for stage in stages:
        other = lax.fori_loop(
            0, rounds, lambda _, array, stage=stage: swapped(array, stage), gathered
        )
        gathered = jnp.concatenate([gathered, other], axis=0)
    wanted = owner * capacity + lax.broadcasted_iota(jnp.int32, (capacity, slots.shape[0]), 0)
    order = lax.broadcasted_iota(jnp.int32, (capacity, slots.shape[0]), 1)
    feeding = jnp.max(jnp.where(wanted == slots[None, :], order, -1), axis=1)
    slot_rows = call(
        land_body,
        jax.ShapeDtypeStruct((clusters, 2, padded, capacity * rank_max), jnp.bfloat16),
        [SMEM, SMEM, VMEM],
        "land",
        moved=2 * gathered.size * (1 + clusters),
    )(feeding, slot_target, gathered)

    chunk = jax.ShapeDtypeStruct((columns, clusters * seg), jnp.bfloat16)
    own_parts, other_parts = [None] * PLACES, [None] * PLACES
    first = call(
        functools.partial(expand_own_body, seg, columns),
        jax.ShapeDtypeStruct((columns, 2 * clusters * seg), jnp.bfloat16),
        [SMEM] + [VMEM] * 3,
        "expand_own",
        flops=4 * clusters * capacity * columns * seg * rank_max,
        moved=4 * u_factors.size + 2 * slot_rows.size + 4 * columns * clusters * seg,
        scratch=[pltpu.VMEM((clusters, padded, seg), jnp.float32)],
    )(position, slot_rows, u_factors, u_side)
    arrivals = {
        1: ([u_near], [[0]]),
        2: (u_far, [[0, 1]]),
        3: ([u_middle, *u_ends], [[0], [1, 2]]),
    }
    finished = []
    for step, (shards, choices) in arrivals.items():
        if finished:
            slot_rows = after(slot_rows, own_parts[finished[-1]])
        if len(finished) == 2:
            slot_rows = after(slot_rows, first, other_parts[finished[0]])
        own, other = call(
            functools.partial(expand_body, seg, columns, choices),
            [chunk, chunk],
            [SMEM, VMEM] + [VMEM] * len(shards),
            "expand",
            flops=4 * clusters * capacity * columns * seg * rank_max,
            moved=2 * u_factors.size + 2 * slot_rows.size + 4 * columns * clusters * seg,
            scratch=[pltpu.VMEM((clusters, 2, padded, seg), jnp.float32)],
        )(position, slot_rows, *shards)
        own_parts[step], other_parts[step] = own, across(other)
        finished.append(step)
    return call(
        functools.partial(join_body, seg, clusters),
        jax.ShapeDtypeStruct((columns, width), jnp.bfloat16),
        [SMEM] + [VMEM] * (2 * PLACES - 1),
        "join",
        moved=4 * columns * width,
    )(position, first, *own_parts[1:], *other_parts[1:])


def gathered_plan(
    incident, v_factors, u_factors, block_source, block_rank, block_slot, slot_target
):
    columns = incident.shape[0]
    blocks = v_factors.shape[0]
    rank_max = v_factors.shape[2]
    capacity = u_factors.shape[0]
    devices = lax.axis_size("clus")
    cluster_len = v_factors.shape[1] * lax.axis_size("rhs")
    local_clusters = incident.shape[1] // cluster_len
    per_peer = max(1, (2 * blocks + devices - 1) // devices)
    sources = jnp.take(incident.reshape(columns, local_clusters, cluster_len), block_source, axis=1)
    compressed = jnp.einsum(
        "cbr,brk->bck",
        sources,
        lax.all_gather(v_factors, "rhs", axis=1, tiled=True),
        preferred_element_type=jnp.float32,
    )
    rank_index = lax.broadcasted_iota(jnp.int32, (blocks, 1, rank_max), 2)
    compressed = jnp.where(rank_index < block_rank[:, None, None], compressed, 0.0).astype(
        jnp.bfloat16
    )
    target_dev = block_slot // capacity
    target_pos = block_slot % capacity
    later_index = lax.broadcasted_iota(jnp.int32, (blocks, blocks), 0)
    earlier_index = lax.broadcasted_iota(jnp.int32, (blocks, blocks), 1)
    same_target = target_dev[None, :] == target_dev[:, None]
    before = jnp.sum((same_target & (earlier_index < later_index)).astype(jnp.int32), axis=1)
    position = target_dev * per_peer + before
    places = lax.broadcasted_iota(jnp.int32, (blocks, devices * per_peer), 1)
    placed = position[:, None] == places
    outgoing = jnp.einsum(
        "bp,bck->pck", placed.astype(jnp.bfloat16), compressed, preferred_element_type=jnp.float32
    ).astype(jnp.bfloat16)
    labels = jnp.sum(jnp.where(placed, target_pos[:, None] + 1, 0), axis=0) - 1
    arrived, arrived_labels = (
        lax.all_to_all(outgoing, "clus", split_axis=0, concat_axis=0, tiled=True),
        lax.all_to_all(labels, "clus", split_axis=0, concat_axis=0, tiled=True),
    )
    slot_ids = lax.broadcasted_iota(jnp.int32, (devices * per_peer, capacity), 1)
    landing = (arrived_labels[:, None] == slot_ids).astype(jnp.bfloat16)
    slot_rows = jnp.einsum(
        "pj,pck->jck", landing, arrived, preferred_element_type=jnp.float32
    ).astype(jnp.bfloat16)
    cluster_ids = lax.broadcasted_iota(jnp.int32, (capacity, local_clusters), 1)
    owners = (slot_target[:, None] == cluster_ids).astype(jnp.float32)
    products = jnp.einsum(
        "jck,jrk->jcr",
        slot_rows,
        lax.all_gather(u_factors, "rhs", axis=1, tiled=True),
        preferred_element_type=jnp.float32,
    )
    summed = jnp.einsum("jt,jcr->ctr", owners, products, precision=lax.Precision.HIGHEST)
    return summed.reshape(columns, local_clusters * cluster_len).astype(jnp.bfloat16)


def local(incident, v_factors, *rest):
    owners = lax.axis_size("clus")
    fits = (
        lax.axis_size("rhs") == 2 * PLACES
        and v_factors.shape[1] % 128 == 0
        and owners > 1
        and owners & (owners - 1) == 0
    )
    return (paired if fits else gathered_plan)(incident, v_factors, *rest)


def solution(mesh):
    placed = (
        P("rhs", "clus"),
        P("clus", "rhs", None),
        P("clus", "rhs", None),
        P("clus"),
        P("clus"),
        P("clus"),
        P("clus"),
    )
    return jax.shard_map(
        local, mesh=mesh, in_specs=placed, out_specs=P("rhs", "clus"), check_vma=False
    )
```

```python
import functools

import jax
import jax.numpy as jnp
from jax import lax
from jax.experimental import pallas as pl
from jax.experimental.pallas import tpu as pltpu
from jax.sharding import PartitionSpec as P

VMEM = pl.BlockSpec(memory_space=pltpu.VMEM)
SMEM = pl.BlockSpec(memory_space=pltpu.SMEM)
LIMIT = 10 * 1024 * 1024


def call(body, out_shape, in_specs, name, flops=0, moved=0, scratch=()):
    out_specs = [VMEM] * len(out_shape) if isinstance(out_shape, list) else VMEM
    return pl.pallas_call(
        body,
        out_shape=out_shape,
        in_specs=in_specs,
        out_specs=out_specs,
        scratch_shapes=list(scratch),
        compiler_params=pltpu.CompilerParams(vmem_limit_bytes=LIMIT),
        cost_estimate=pl.CostEstimate(flops=flops, bytes_accessed=moved, transcendentals=0),
        name=name,
    )


def pack_body(seg, pos_ref, x_ref, *out_refs):
    half, piece = 1 - pos_ref[0], 0
    for out_ref in out_refs:
        for place in range(0, out_ref.shape[1], seg):
            start = pl.multiple_of((2 * piece + half) * seg, seg)
            out_ref[:, place : place + seg] = x_ref[:, pl.ds(start, seg)]
            piece += 1


def compress_body(seg, pos_ref, source_ref, x_ref, xl_ref, xh_ref, *refs):
    v0, v1, v2, v3, v4, out_ref, send_ref, xn_ref = refs
    half, mine = pos_ref[0], pos_ref[1]
    columns = x_ref.shape[0]
    xn_ref[:, : xl_ref.shape[1]] = xl_ref[...]
    xn_ref[:, xl_ref.shape[1] :] = xh_ref[...]
    out_ref[...] = jnp.zeros_like(out_ref)

    def run(shards):
        for block in range(out_ref.shape[0]):
            source = source_ref[block]
            own = other = 0.0
            for step, shard in enumerate(shards):
                piece = source * PLACES + jnp.bitwise_xor(mine, step)
                here = pl.multiple_of((piece * 2 + half) * seg, seg)
                there = pl.multiple_of(piece * seg, seg)
                rows = shard[block]
                own += jnp.dot(x_ref[:, pl.ds(here, seg)], rows, preferred_element_type=jnp.float32)
                other += jnp.dot(
                    xn_ref[:, pl.ds(there, seg)], rows, preferred_element_type=jnp.float32
                )
            out_ref[block, half, :columns] = own
            out_ref[block, 1 - half, :columns] = other

    inner = (mine == 1) | (mine == 2)

    @pl.when(inner)
    def _():
        run((v0, v1, v2, v3))

    @pl.when(jnp.logical_not(inner))
    def _():
        run((v0, v1, v2, v4))

    send_ref[...] = out_ref[...].astype(send_ref.dtype)


def land_body(index_ref, target_ref, comp_ref, rows_ref):
    clusters, rank_max = rows_ref.shape[0], comp_ref.shape[3]
    for slot in range(rows_ref.shape[3] // rank_max):
        block, target = index_ref[slot], target_ref[slot]
        found = comp_ref[jnp.maximum(block, 0)]
        for cluster in range(clusters):
            wanted = (block >= 0) & (target == cluster)
            kept = jnp.where(wanted, found, jnp.zeros_like(found))
            rows_ref[cluster, :, :, slot * rank_max : (slot + 1) * rank_max] = kept


def expand_body(seg, columns, choices, pos_ref, rows_ref, *refs):
    own_ref, other_ref, acc = refs[-3:]
    half, mine = pos_ref[0], pos_ref[1]
    clusters, sides, padded, depth = rows_ref.shape

    def run(choice):
        slots = [refs[index][slot] for index in choice for slot in range(refs[index].shape[0])]
        factor = jnp.concatenate(slots, axis=1)
        product = lax.dot_general(
            rows_ref[...].reshape(clusters * sides * padded, depth),
            factor,
            (((1,), (1,)), ((), ())),
            preferred_element_type=jnp.float32,
        )
        acc[...] = product.reshape(clusters, sides, padded, seg)

    if len(choices) == 1:
        run(choices[0])
    else:
        inner = (mine == 1) | (mine == 2)

        @pl.when(inner)
        def _():
            run(choices[0])

        @pl.when(jnp.logical_not(inner))
        def _():
            run(choices[1])

    for target in range(clusters):
        span = slice(target * seg, (target + 1) * seg)
        own_ref[:, span] = acc[target, half, :columns].astype(own_ref.dtype)
        other_ref[:, span] = acc[target, 1 - half, :columns].astype(other_ref.dtype)


def expand_own_body(seg, columns, pos_ref, rows_ref, u_ref, side_ref, out_ref, acc):
    half = pos_ref[0]
    clusters, sides, padded, depth = rows_ref.shape
    rows = rows_ref[:, half].reshape(clusters * padded, depth)
    for shard, place in ((u_ref, half), (side_ref, 1 - half)):
        factor = jnp.concatenate([shard[slot] for slot in range(shard.shape[0])], axis=1)
        product = lax.dot_general(
            rows, factor, (((1,), (1,)), ((), ())), preferred_element_type=jnp.float32
        )
        acc[...] = product.reshape(clusters, padded, seg)
        for target in range(clusters):
            start = pl.multiple_of((2 * target + place) * seg, seg)
            out_ref[:, pl.ds(start, seg)] = acc[target, :columns].astype(out_ref.dtype)


def join_body(seg, clusters, pos_ref, first_ref, *refs):
    out_ref = refs[-1]
    half, mine = pos_ref[0], pos_ref[1]
    for target in range(clusters):
        start = pl.multiple_of((target * PLACES + mine) * 2 * seg, 2 * seg)
        span = slice(2 * target * seg, 2 * (target + 1) * seg)
        out_ref[:, pl.ds(start, 2 * seg)] = first_ref[:, span]
    for step in range(1, PLACES):
        place = jnp.bitwise_xor(mine, step)
        for target in range(clusters):
            span = slice(target * seg, (target + 1) * seg)
            base = (target * PLACES + place) * 2
            here = pl.multiple_of((base + half) * seg, seg)
            there = pl.multiple_of((base + 1 - half) * seg, seg)
            out_ref[:, pl.ds(here, seg)] = refs[step - 1][:, span]
            out_ref[:, pl.ds(there, seg)] = refs[PLACES + step - 2][:, span]


def after(value, *first):
    return lax.optimization_barrier((value, *first))[0]


PLACES = 4


def paired(incident, v_factors, u_factors, block_source, block_rank, block_slot, slot_target):
    columns, width = incident.shape
    padded = -(-columns // 16) * 16
    blocks, seg, rank_max = v_factors.shape
    capacity = u_factors.shape[0]
    owners = lax.axis_size("clus")
    clusters = width // (seg * 2 * PLACES)
    me, owner = lax.axis_index("rhs"), lax.axis_index("clus")
    position = jnp.stack([me % 2, me // 2]).astype(jnp.int32)

    def move(array, pairs):
        return lax.ppermute(array, "rhs", [(2 * a + i, 2 * b + i) for a, b in pairs for i in (0, 1)])

    def across(array):
        return lax.ppermute(array, "rhs", [(p, p ^ 1) for p in range(2 * PLACES)])

    far = [(p, p ^ 2) for p in range(PLACES)]
    near = [(p, p ^ 1) for p in range(PLACES)]
    middle = [(1, 2), (2, 1)]
    ends = [(1, 0), (2, 3)]

    stages = [1 << bit for bit in reversed(range((owners - 1).bit_length()))]

    def swapped(array, stage):
        return lax.ppermute(array, "clus", [(p, p ^ stage) for p in range(owners)])

    def double(array, stage):
        return jnp.concatenate([array, swapped(array, stage)], axis=0)

    v_far, v_near, v_middle = (
        move(v_factors, far),
        move(v_factors, near),
        move(v_factors, middle),
    )
    packed = call(
        functools.partial(pack_body, seg),
        [
            jax.ShapeDtypeStruct((columns, count * PLACES * seg), incident.dtype)
            for count in (1, clusters - 1)
        ],
        [SMEM, VMEM],
        "pack",
        moved=3 * columns * width,
    )(position, incident)
    x_other = [across(part) for part in packed]
    slots = block_slot
    for stage in stages:
        slots = double(slots, stage)
    v_far, slots, x_low = lax.optimization_barrier((v_far, slots, x_other[0]))
    v_ends = move(v_far, ends)
    u_first = after(u_factors, v_near, v_middle, v_ends)
    u_far = move(u_first, far)

    partial, sent = call(
        functools.partial(compress_body, seg),
        [
            jax.ShapeDtypeStruct((blocks, 2, padded, rank_max), jnp.float32),
            jax.ShapeDtypeStruct((blocks, 2, padded, rank_max), jnp.bfloat16),
        ],
        [SMEM, SMEM] + [VMEM] * 8,
        "compress",
        flops=4 * blocks * columns * seg * PLACES * rank_max,
        moved=3 * columns * width + 2 * PLACES * v_factors.size,
        scratch=[pltpu.VMEM((columns, width // 2), incident.dtype)],
    )(position, block_source, incident, x_low, x_other[1], v_factors, v_near, v_far, v_middle, v_ends)
    received = across(sent)
    u_side = across(after(u_factors, received))
    u_near, u_middle = move(u_first, near), move(u_first, middle)

    rank_index = lax.broadcasted_iota(jnp.int32, (blocks, 1, 1, rank_max), 3)
    rows = jnp.where(
        rank_index < block_rank[:, None, None, None],
        partial + received.astype(jnp.float32),
        0.0,
    ).astype(jnp.bfloat16)

    rounds, gathered = 1 + jnp.minimum(me, 0), rows
    for stage in stages:
        other = lax.fori_loop(
            0, rounds, lambda _, array, stage=stage: swapped(array, stage), gathered
        )
        gathered = jnp.concatenate([gathered, other], axis=0)
    u_ends = move(after(u_far, gathered), ends)
    wanted = owner * capacity + lax.broadcasted_iota(jnp.int32, (capacity, slots.shape[0]), 0)
    order = lax.broadcasted_iota(jnp.int32, (capacity, slots.shape[0]), 1)
    feeding = jnp.max(jnp.where(wanted == slots[None, :], order, -1), axis=1)
    slot_rows = call(
        land_body,
        jax.ShapeDtypeStruct((clusters, 2, padded, capacity * rank_max), jnp.bfloat16),
        [SMEM, SMEM, VMEM],
        "land",
        moved=2 * gathered.size * (1 + clusters),
    )(feeding, slot_target, gathered)

    chunk = jax.ShapeDtypeStruct((columns, clusters * seg), jnp.bfloat16)
    own_parts, other_parts = [None] * PLACES, [None] * PLACES
    first = call(
        functools.partial(expand_own_body, seg, columns),
        jax.ShapeDtypeStruct((columns, 2 * clusters * seg), jnp.bfloat16),
        [SMEM] + [VMEM] * 3,
        "expand_own",
        flops=4 * clusters * capacity * columns * seg * rank_max,
        moved=4 * u_factors.size + 2 * slot_rows.size + 4 * columns * clusters * seg,
        scratch=[pltpu.VMEM((clusters, padded, seg), jnp.float32)],
    )(position, slot_rows, u_factors, u_side)
    arrivals = {
        1: ([u_near], [[0]]),
        2: ([u_far], [[0]]),
        3: ([u_middle, u_ends], [[0], [1]]),
    }
    finished = []
    for step, (shards, choices) in arrivals.items():
        if finished:
            slot_rows = after(slot_rows, own_parts[finished[-1]])
        if len(finished) == 2:
            slot_rows = after(slot_rows, first, other_parts[finished[0]])
        own, other = call(
            functools.partial(expand_body, seg, columns, choices),
            [chunk, chunk],
            [SMEM, VMEM] + [VMEM] * len(shards),
            "expand",
            flops=4 * clusters * capacity * columns * seg * rank_max,
            moved=2 * u_factors.size + 2 * slot_rows.size + 4 * columns * clusters * seg,
            scratch=[pltpu.VMEM((clusters, 2, padded, seg), jnp.float32)],
        )(position, slot_rows, *shards)
        own_parts[step], other_parts[step] = own, across(other)
        finished.append(step)
    return call(
        functools.partial(join_body, seg, clusters),
        jax.ShapeDtypeStruct((columns, width), jnp.bfloat16),
        [SMEM] + [VMEM] * (2 * PLACES - 1),
        "join",
        moved=4 * columns * width,
    )(position, first, *own_parts[1:], *other_parts[1:])


def gathered_plan(
    incident, v_factors, u_factors, block_source, block_rank, block_slot, slot_target
):
    columns = incident.shape[0]
    blocks = v_factors.shape[0]
    rank_max = v_factors.shape[2]
    capacity = u_factors.shape[0]
    devices = lax.axis_size("clus")
    cluster_len = v_factors.shape[1] * lax.axis_size("rhs")
    local_clusters = incident.shape[1] // cluster_len
    per_peer = max(1, (2 * blocks + devices - 1) // devices)
    sources = jnp.take(incident.reshape(columns, local_clusters, cluster_len), block_source, axis=1)
    compressed = jnp.einsum(
        "cbr,brk->bck",
        sources,
        lax.all_gather(v_factors, "rhs", axis=1, tiled=True),
        preferred_element_type=jnp.float32,
    )
    rank_index = lax.broadcasted_iota(jnp.int32, (blocks, 1, rank_max), 2)
    compressed = jnp.where(rank_index < block_rank[:, None, None], compressed, 0.0).astype(
        jnp.bfloat16
    )
    target_dev = block_slot // capacity
    target_pos = block_slot % capacity
    later_index = lax.broadcasted_iota(jnp.int32, (blocks, blocks), 0)
    earlier_index = lax.broadcasted_iota(jnp.int32, (blocks, blocks), 1)
    same_target = target_dev[None, :] == target_dev[:, None]
    before = jnp.sum((same_target & (earlier_index < later_index)).astype(jnp.int32), axis=1)
    position = target_dev * per_peer + before
    places = lax.broadcasted_iota(jnp.int32, (blocks, devices * per_peer), 1)
    placed = position[:, None] == places
    outgoing = jnp.einsum(
        "bp,bck->pck", placed.astype(jnp.bfloat16), compressed, preferred_element_type=jnp.float32
    ).astype(jnp.bfloat16)
    labels = jnp.sum(jnp.where(placed, target_pos[:, None] + 1, 0), axis=0) - 1
    arrived, arrived_labels = (
        lax.all_to_all(outgoing, "clus", split_axis=0, concat_axis=0, tiled=True),
        lax.all_to_all(labels, "clus", split_axis=0, concat_axis=0, tiled=True),
    )
    slot_ids = lax.broadcasted_iota(jnp.int32, (devices * per_peer, capacity), 1)
    landing = (arrived_labels[:, None] == slot_ids).astype(jnp.bfloat16)
    slot_rows = jnp.einsum(
        "pj,pck->jck", landing, arrived, preferred_element_type=jnp.float32
    ).astype(jnp.bfloat16)
    cluster_ids = lax.broadcasted_iota(jnp.int32, (capacity, local_clusters), 1)
    owners = (slot_target[:, None] == cluster_ids).astype(jnp.float32)
    products = jnp.einsum(
        "jck,jrk->jcr",
        slot_rows,
        lax.all_gather(u_factors, "rhs", axis=1, tiled=True),
        preferred_element_type=jnp.float32,
    )
    summed = jnp.einsum("jt,jcr->ctr", owners, products, precision=lax.Precision.HIGHEST)
    return summed.reshape(columns, local_clusters * cluster_len).astype(jnp.bfloat16)


def local(incident, v_factors, *rest):
    owners = lax.axis_size("clus")
    fits = (
        lax.axis_size("rhs") == 2 * PLACES
        and v_factors.shape[1] % 128 == 0
        and owners > 1
        and incident.shape[1] > v_factors.shape[1] * 2 * PLACES
        and owners & (owners - 1) == 0
    )
    return (paired if fits else gathered_plan)(incident, v_factors, *rest)


def solution(mesh):
    placed = (
        P("rhs", "clus"),
        P("clus", "rhs", None),
        P("clus", "rhs", None),
        P("clus"),
        P("clus"),
        P("clus"),
        P("clus"),
    )
    return jax.shard_map(
        local, mesh=mesh, in_specs=placed, out_specs=P("rhs", "clus"), check_vma=False
    )
```

```python
import functools

import jax
import jax.numpy as jnp
from jax import lax
from jax.experimental import pallas as pl
from jax.experimental.pallas import tpu as pltpu
from jax.sharding import PartitionSpec as P

VMEM = pl.BlockSpec(memory_space=pltpu.VMEM)
SMEM = pl.BlockSpec(memory_space=pltpu.SMEM)
LIMIT = 10 * 1024 * 1024


def call(body, out_shape, in_specs, name, flops=0, moved=0, scratch=()):
    out_specs = [VMEM] * len(out_shape) if isinstance(out_shape, list) else VMEM
    return pl.pallas_call(
        body,
        out_shape=out_shape,
        in_specs=in_specs,
        out_specs=out_specs,
        scratch_shapes=list(scratch),
        compiler_params=pltpu.CompilerParams(vmem_limit_bytes=LIMIT),
        cost_estimate=pl.CostEstimate(flops=flops, bytes_accessed=moved, transcendentals=0),
        name=name,
    )


def pack_body(seg, pos_ref, x_ref, *out_refs):
    half, piece = 1 - pos_ref[0], 0
    for out_ref in out_refs:
        for place in range(0, out_ref.shape[1], seg):
            start = pl.multiple_of((2 * piece + half) * seg, seg)
            out_ref[:, place : place + seg] = x_ref[:, pl.ds(start, seg)]
            piece += 1


def compress_body(seg, pos_ref, source_ref, x_ref, xl_ref, xh_ref, *refs):
    v0, v1, v2, v3, v4, out_ref, send_ref, xn_ref = refs
    half, mine = pos_ref[0], pos_ref[1]
    columns = x_ref.shape[0]
    xn_ref[:, : xl_ref.shape[1]] = xl_ref[...]
    xn_ref[:, xl_ref.shape[1] :] = xh_ref[...]
    out_ref[...] = jnp.zeros_like(out_ref)

    def run(shards):
        for block in range(out_ref.shape[0]):
            source = source_ref[block]
            own = other = 0.0
            for step, shard in enumerate(shards):
                piece = source * PLACES + jnp.bitwise_xor(mine, step)
                here = pl.multiple_of((piece * 2 + half) * seg, seg)
                there = pl.multiple_of(piece * seg, seg)
                rows = shard[block]
                own += jnp.dot(x_ref[:, pl.ds(here, seg)], rows, preferred_element_type=jnp.float32)
                other += jnp.dot(
                    xn_ref[:, pl.ds(there, seg)], rows, preferred_element_type=jnp.float32
                )
            out_ref[block, half, :columns] = own
            out_ref[block, 1 - half, :columns] = other

    inner = (mine == 1) | (mine == 2)

    @pl.when(inner)
    def _():
        run((v0, v1, v2, v3))

    @pl.when(jnp.logical_not(inner))
    def _():
        run((v0, v1, v2, v4))

    send_ref[...] = out_ref[...].astype(send_ref.dtype)


def place_columns(value, offset, store):
    width = value.shape[-1]
    shift = lax.rem(offset, width)
    turned = pltpu.roll(value, shift, value.ndim - 1)
    lane = lax.broadcasted_iota(jnp.int32, value.shape, value.ndim - 1)
    store(offset // width, jnp.where(lane >= shift, turned, 0.0))
    store(offset // width + 1, jnp.where(lane < shift, turned, 0.0))


def squeeze_body(offset_ref, used_ref, u_ref, out_ref, acc):
    acc[...] = jnp.zeros_like(acc)
    for slot in range(u_ref.shape[0]):
        value = u_ref[slot].astype(jnp.float32)
        lane = lax.broadcasted_iota(jnp.int32, value.shape, 1)

        def store(tile, part):
            acc[tile] += part

        place_columns(jnp.where(lane < used_ref[slot], value, 0.0), offset_ref[slot], store)
    out_ref[...] = acc[: out_ref.shape[0]].astype(out_ref.dtype)


def land_body(index_ref, target_ref, offset_ref, comp_ref, rows_ref):
    rows_ref[...] = jnp.zeros_like(rows_ref)
    last = rows_ref.shape[0] - 1
    for slot in range(index_ref.shape[0]):
        block, target = index_ref[slot], target_ref[slot]
        value = comp_ref[jnp.maximum(block, 0)].astype(jnp.float32)
        value = jnp.where(block >= 0, value, 0.0).reshape(rows_ref.shape[2:])

        def store(tile, part):
            rows_ref[jnp.minimum(tile, last), target] += part.astype(rows_ref.dtype)

        place_columns(value, offset_ref[slot], store)


def lined_up(ref, rows):
    return jnp.concatenate([ref[tile].reshape(rows, ref.shape[-1]) for tile in range(ref.shape[0])], axis=1)


def expand_body(seg, columns, pos_ref, rows_ref, *refs):
    own_ref, other_ref, acc = refs[-3:]
    half, mine = pos_ref[0], pos_ref[1]
    clusters, sides, padded = acc.shape[:3]

    def run(shard):
        product = lax.dot_general(
            lined_up(rows_ref, clusters * sides * padded),
            lined_up(shard, seg),
            (((1,), (1,)), ((), ())),
            preferred_element_type=jnp.float32,
        )
        acc[...] = product.reshape(acc.shape)

    if len(refs) == 4:
        run(refs[0])
    else:
        inner = (mine == 1) | (mine == 2)

        @pl.when(inner)
        def _():
            run(refs[0])

        @pl.when(jnp.logical_not(inner))
        def _():
            run(refs[1])

    for target in range(clusters):
        span = slice(target * seg, (target + 1) * seg)
        own_ref[:, span] = acc[target, half, :columns].astype(own_ref.dtype)
        other_ref[:, span] = acc[target, 1 - half, :columns].astype(other_ref.dtype)


def expand_own_body(seg, columns, pos_ref, rows_ref, u_ref, side_ref, out_ref, acc):
    half = pos_ref[0]
    clusters, padded = acc.shape[:2]
    start = pl.multiple_of(half * padded, padded)
    tiles = [
        rows_ref[tile, :, pl.ds(start, padded)].reshape(clusters * padded, rows_ref.shape[3])
        for tile in range(rows_ref.shape[0])
    ]
    rows = jnp.concatenate(tiles, axis=1)
    for shard, place in ((u_ref, half), (side_ref, 1 - half)):
        product = lax.dot_general(
            rows,
            lined_up(shard, seg),
            (((1,), (1,)), ((), ())),
            preferred_element_type=jnp.float32,
        )
        acc[...] = product.reshape(acc.shape)
        for target in range(clusters):
            start = pl.multiple_of((2 * target + place) * seg, seg)
            out_ref[:, pl.ds(start, seg)] = acc[target, :columns].astype(out_ref.dtype)


def join_body(seg, clusters, pos_ref, first_ref, *refs):
    out_ref = refs[-1]
    half, mine = pos_ref[0], pos_ref[1]
    for target in range(clusters):
        start = pl.multiple_of((target * PLACES + mine) * 2 * seg, 2 * seg)
        span = slice(2 * target * seg, 2 * (target + 1) * seg)
        out_ref[:, pl.ds(start, 2 * seg)] = first_ref[:, span]
    for step in range(1, PLACES):
        place = jnp.bitwise_xor(mine, step)
        for target in range(clusters):
            span = slice(target * seg, (target + 1) * seg)
            base = (target * PLACES + place) * 2
            here = pl.multiple_of((base + half) * seg, seg)
            there = pl.multiple_of((base + 1 - half) * seg, seg)
            out_ref[:, pl.ds(here, seg)] = refs[step - 1][:, span]
            out_ref[:, pl.ds(there, seg)] = refs[PLACES + step - 2][:, span]


def after(value, *first):
    return lax.optimization_barrier((value, *first))[0]


PLACES = 4


def paired(incident, v_factors, u_factors, block_source, block_rank, block_slot, slot_target):
    columns, width = incident.shape
    padded = -(-columns // 16) * 16
    blocks, seg, rank_max = v_factors.shape
    capacity = u_factors.shape[0]
    owners = lax.axis_size("clus")
    clusters = width // (seg * 2 * PLACES)
    me, owner = lax.axis_index("rhs"), lax.axis_index("clus")
    position = jnp.stack([me % 2, me // 2]).astype(jnp.int32)

    def move(array, pairs):
        return lax.ppermute(array, "rhs", [(2 * a + i, 2 * b + i) for a, b in pairs for i in (0, 1)])

    def across(array):
        return lax.ppermute(array, "rhs", [(p, p ^ 1) for p in range(2 * PLACES)])

    far = [(p, p ^ 2) for p in range(PLACES)]
    near = [(p, p ^ 1) for p in range(PLACES)]
    middle = [(1, 2), (2, 1)]
    ends = [(1, 0), (2, 3)]

    stages = [1 << bit for bit in reversed(range((owners - 1).bit_length()))]

    def swapped(array, stage):
        return lax.ppermute(array, "clus", [(p, p ^ stage) for p in range(owners)])

    def double(array, stage):
        return jnp.concatenate([array, swapped(array, stage)], axis=0)

    v_far, v_near, v_middle = (
        move(v_factors, far),
        move(v_factors, near),
        move(v_factors, middle),
    )
    packed = call(
        functools.partial(pack_body, seg),
        [
            jax.ShapeDtypeStruct((columns, count * PLACES * seg), incident.dtype)
            for count in (clusters // 2, clusters - clusters // 2)
        ],
        [SMEM, VMEM],
        "pack",
        moved=3 * columns * width,
    )(position, incident)
    table = jnp.stack([block_slot, block_rank], axis=1)
    for stage in stages:
        table = double(table, stage)
    slots, ranks = table[:, 0], table[:, 1]
    wanted = owner * capacity + lax.broadcasted_iota(jnp.int32, (capacity, slots.shape[0]), 0)
    order = lax.broadcasted_iota(jnp.int32, (capacity, slots.shape[0]), 1)
    found = wanted == slots[None, :]
    feeding = jnp.max(jnp.where(found, order, -1), axis=1)
    used = jnp.sum(jnp.where(found, ranks[None, :], 0), axis=1)
    earlier = lax.broadcasted_iota(jnp.int32, (capacity, capacity), 1)
    earlier = earlier < lax.broadcasted_iota(jnp.int32, (capacity, capacity), 0)
    offset = jnp.sum(jnp.where(earlier, used[None, :], 0), axis=1)
    place = lax.broadcasted_iota(jnp.int32, (owners, slots.shape[0]), 0)
    held = (slots[None, :] >= place * capacity) & (slots[None, :] < (place + 1) * capacity)
    fullest = jnp.max(jnp.sum(jnp.where(held, ranks[None, :], 0), axis=1))
    tiles = sorted({-(-capacity * part // 10) for part in (5, 6, 7, 8, 10)})
    level = sum((fullest > count * rank_max).astype(jnp.int32) for count in tiles[:-1])
    squeezed = call(
        squeeze_body,
        jax.ShapeDtypeStruct(u_factors.shape, u_factors.dtype),
        [SMEM, SMEM, VMEM],
        "squeeze",
        moved=4 * u_factors.size,
        scratch=[pltpu.VMEM((capacity + 2, seg, rank_max), jnp.float32)],
    )(offset, used, u_factors)

    x_low, x_high = [across(part) for part in packed]
    v_ends = move(after(v_far, *packed), ends)
    arrived = lax.optimization_barrier(
        (x_low, x_high, v_near, v_far, v_middle, v_ends, squeezed, level)
    )

    def rest(count, x_low, x_high, v_near, v_far, v_middle, v_ends, squeezed):
        target_factors = squeezed[:count]
        u_far, u_near, u_middle = [move(target_factors, way) for way in (far, near, middle)]
        partial, sent = call(
            functools.partial(compress_body, seg),
            [
                jax.ShapeDtypeStruct((blocks, 2, padded, rank_max), jnp.float32),
                jax.ShapeDtypeStruct((blocks, 2, padded, rank_max), jnp.bfloat16),
            ],
            [SMEM, SMEM] + [VMEM] * 8,
            "compress",
            flops=4 * blocks * columns * seg * PLACES * rank_max,
            moved=3 * columns * width + 2 * PLACES * v_factors.size,
            scratch=[pltpu.VMEM((columns, width // 2), incident.dtype)],
        )(
            position, block_source, incident, x_low, x_high,
            v_factors, v_near, v_far, v_middle, v_ends,
        )
        received = across(sent)
        u_side = across(after(target_factors, received))
        rank_index = lax.broadcasted_iota(jnp.int32, (blocks, 1, 1, rank_max), 3)
        rows = jnp.where(
            rank_index < block_rank[:, None, None, None],
            partial + received.astype(jnp.float32),
            0.0,
        ).astype(jnp.bfloat16)

        rounds, gathered = 1 + jnp.minimum(me, 0), rows
        for stage in stages:
            other = lax.fori_loop(
                0, rounds, lambda _, array, stage=stage: swapped(array, stage), gathered
            )
            gathered = jnp.concatenate([gathered, other], axis=0)
        u_ends = move(after(u_far, gathered), ends)
        slot_rows = call(
            land_body,
            jax.ShapeDtypeStruct((count, clusters, 2 * padded, rank_max), jnp.bfloat16),
            [SMEM, SMEM, SMEM, VMEM],
            "land",
            moved=2 * gathered.size * (1 + clusters),
        )(feeding, slot_target, offset, gathered)

        chunk = jax.ShapeDtypeStruct((columns, clusters * seg), jnp.bfloat16)
        own_parts, other_parts = [None] * PLACES, [None] * PLACES
        work = 4 * clusters * count * columns * seg * rank_max
        first = call(
            functools.partial(expand_own_body, seg, columns),
            jax.ShapeDtypeStruct((columns, 2 * clusters * seg), jnp.bfloat16),
            [SMEM] + [VMEM] * 3,
            "expand_own",
            flops=work,
            moved=4 * target_factors.size + 2 * slot_rows.size + 4 * columns * clusters * seg,
            scratch=[pltpu.VMEM((clusters, padded, seg), jnp.float32)],
        )(position, slot_rows, target_factors, u_side)
        finished = []
        for step, shards in ((1, [u_near]), (2, [u_far]), (3, [u_middle, u_ends])):
            if finished:
                slot_rows = after(slot_rows, own_parts[finished[-1]])
            if len(finished) == 2:
                slot_rows = after(slot_rows, first, other_parts[finished[0]])
            own, other = call(
                functools.partial(expand_body, seg, columns),
                [chunk, chunk],
                [SMEM, VMEM] + [VMEM] * len(shards),
                "expand",
                flops=work,
                moved=2 * target_factors.size + 2 * slot_rows.size + 4 * columns * clusters * seg,
                scratch=[pltpu.VMEM((clusters, 2, padded, seg), jnp.float32)],
            )(position, slot_rows, *shards)
            own_parts[step], other_parts[step] = own, across(other)
            finished.append(step)
        return call(
            functools.partial(join_body, seg, clusters),
            jax.ShapeDtypeStruct((columns, width), jnp.bfloat16),
            [SMEM] + [VMEM] * (2 * PLACES - 1),
            "join",
            moved=4 * columns * width,
        )(position, first, *own_parts[1:], *other_parts[1:])

    return lax.switch(
        arrived[-1], [functools.partial(rest, count) for count in tiles], *arrived[:-1]
    )


def gathered_plan(
    incident, v_factors, u_factors, block_source, block_rank, block_slot, slot_target
):
    columns = incident.shape[0]
    blocks = v_factors.shape[0]
    rank_max = v_factors.shape[2]
    capacity = u_factors.shape[0]
    devices = lax.axis_size("clus")
    cluster_len = v_factors.shape[1] * lax.axis_size("rhs")
    local_clusters = incident.shape[1] // cluster_len
    per_peer = max(1, (2 * blocks + devices - 1) // devices)
    sources = jnp.take(incident.reshape(columns, local_clusters, cluster_len), block_source, axis=1)
    compressed = jnp.einsum(
        "cbr,brk->bck",
        sources,
        lax.all_gather(v_factors, "rhs", axis=1, tiled=True),
        preferred_element_type=jnp.float32,
    )
    rank_index = lax.broadcasted_iota(jnp.int32, (blocks, 1, rank_max), 2)
    compressed = jnp.where(rank_index < block_rank[:, None, None], compressed, 0.0).astype(
        jnp.bfloat16
    )
    target_dev = block_slot // capacity
    target_pos = block_slot % capacity
    later_index = lax.broadcasted_iota(jnp.int32, (blocks, blocks), 0)
    earlier_index = lax.broadcasted_iota(jnp.int32, (blocks, blocks), 1)
    same_target = target_dev[None, :] == target_dev[:, None]
    before = jnp.sum((same_target & (earlier_index < later_index)).astype(jnp.int32), axis=1)
    position = target_dev * per_peer + before
    places = lax.broadcasted_iota(jnp.int32, (blocks, devices * per_peer), 1)
    placed = position[:, None] == places
    outgoing = jnp.einsum(
        "bp,bck->pck", placed.astype(jnp.bfloat16), compressed, preferred_element_type=jnp.float32
    ).astype(jnp.bfloat16)
    labels = jnp.sum(jnp.where(placed, target_pos[:, None] + 1, 0), axis=0) - 1
    arrived, arrived_labels = (
        lax.all_to_all(outgoing, "clus", split_axis=0, concat_axis=0, tiled=True),
        lax.all_to_all(labels, "clus", split_axis=0, concat_axis=0, tiled=True),
    )
    slot_ids = lax.broadcasted_iota(jnp.int32, (devices * per_peer, capacity), 1)
    landing = (arrived_labels[:, None] == slot_ids).astype(jnp.bfloat16)
    slot_rows = jnp.einsum(
        "pj,pck->jck", landing, arrived, preferred_element_type=jnp.float32
    ).astype(jnp.bfloat16)
    cluster_ids = lax.broadcasted_iota(jnp.int32, (capacity, local_clusters), 1)
    owners = (slot_target[:, None] == cluster_ids).astype(jnp.float32)
    products = jnp.einsum(
        "jck,jrk->jcr",
        slot_rows,
        lax.all_gather(u_factors, "rhs", axis=1, tiled=True),
        preferred_element_type=jnp.float32,
    )
    summed = jnp.einsum("jt,jcr->ctr", owners, products, precision=lax.Precision.HIGHEST)
    return summed.reshape(columns, local_clusters * cluster_len).astype(jnp.bfloat16)


def local(incident, v_factors, *rest):
    owners = lax.axis_size("clus")
    fits = (
        lax.axis_size("rhs") == 2 * PLACES
        and v_factors.shape[1] % 128 == 0
        and owners > 1
        and incident.shape[1] > v_factors.shape[1] * 2 * PLACES
        and owners & (owners - 1) == 0
    )
    return (paired if fits else gathered_plan)(incident, v_factors, *rest)


def solution(mesh):
    placed = (
        P("rhs", "clus"),
        P("clus", "rhs", None),
        P("clus", "rhs", None),
        P("clus"),
        P("clus"),
        P("clus"),
        P("clus"),
    )
    return jax.shard_map(
        local, mesh=mesh, in_specs=placed, out_specs=P("rhs", "clus"), check_vma=False
    )
```

```python
import functools

import jax
import jax.numpy as jnp
from jax import lax
from jax.experimental import pallas as pl
from jax.experimental.pallas import tpu as pltpu
from jax.sharding import PartitionSpec as P

VMEM = pl.BlockSpec(memory_space=pltpu.VMEM)
SMEM = pl.BlockSpec(memory_space=pltpu.SMEM)
LIMIT = 10 * 1024 * 1024


def call(body, out_shape, in_specs, name, flops=0, moved=0, scratch=()):
    out_specs = [VMEM] * len(out_shape) if isinstance(out_shape, list) else VMEM
    return pl.pallas_call(
        body,
        out_shape=out_shape,
        in_specs=in_specs,
        out_specs=out_specs,
        scratch_shapes=list(scratch),
        compiler_params=pltpu.CompilerParams(vmem_limit_bytes=LIMIT),
        cost_estimate=pl.CostEstimate(flops=flops, bytes_accessed=moved, transcendentals=0),
        name=name,
    )


def pack_body(seg, pos_ref, x_ref, *out_refs):
    half, piece = 1 - pos_ref[0], 0
    for out_ref in out_refs:
        for place in range(0, out_ref.shape[1], seg):
            start = pl.multiple_of((2 * piece + half) * seg, seg)
            out_ref[:, place : place + seg] = x_ref[:, pl.ds(start, seg)]
            piece += 1


def blocks_of(*refs):
    return [ref[block] for ref in refs for block in range(ref.shape[0])]


def compress_own_body(
    seg, pos_ref, source_ref, x_ref, v0, v1, v2a, v2b, sum_ref, last_ref
):
    half, mine = pos_ref[0], pos_ref[1]
    columns = x_ref.shape[0]
    sum_ref[...] = jnp.zeros_like(sum_ref)
    shards = (blocks_of(v0), blocks_of(v1), blocks_of(v2a, v2b))
    for block in range(sum_ref.shape[0]):
        total = 0.0
        for step, shard in enumerate(shards):
            piece = source_ref[block] * PLACES + jnp.bitwise_xor(mine, step)
            start = pl.multiple_of((piece * 2 + half) * seg, seg)
            total += jnp.dot(
                x_ref[:, pl.ds(start, seg)], shard[block], preferred_element_type=jnp.float32
            )
        sum_ref[block, :columns] = total
    for cluster in range(last_ref.shape[0]):
        piece = cluster * PLACES + jnp.bitwise_xor(mine, PLACES - 1)
        start = pl.multiple_of((piece * 2 + half) * seg, seg)
        last_ref[cluster] = x_ref[:, pl.ds(start, seg)]


def compress_body(seg, pos_ref, source_ref, sum_ref, last_ref, xl_ref, xh_ref, *refs):
    v0, v1, v2a, v2b, middle, ends_a, ends_b, out_ref, send_ref, xn_ref = refs
    half, mine = pos_ref[0], pos_ref[1]
    columns = xl_ref.shape[0]
    xn_ref[:, : xl_ref.shape[1]] = xl_ref[...]
    xn_ref[:, xl_ref.shape[1] :] = xh_ref[...]
    out_ref[...] = jnp.zeros_like(out_ref)

    def run(last):
        shards = (blocks_of(v0), blocks_of(v1), blocks_of(v2a, v2b), last)
        for block in range(out_ref.shape[0]):
            source = source_ref[block]
            other = 0.0
            for step, shard in enumerate(shards):
                piece = source * PLACES + jnp.bitwise_xor(mine, step)
                start = pl.multiple_of(piece * seg, seg)
                other += jnp.dot(
                    xn_ref[:, pl.ds(start, seg)], shard[block], preferred_element_type=jnp.float32
                )
            own = jnp.dot(last_ref[source], last[block], preferred_element_type=jnp.float32)
            out_ref[block, half, :columns] = own + sum_ref[block, :columns]
            out_ref[block, 1 - half, :columns] = other

    inner = (mine == 1) | (mine == 2)

    @pl.when(inner)
    def _():
        run(blocks_of(middle))

    @pl.when(jnp.logical_not(inner))
    def _():
        run(blocks_of(ends_a, ends_b))

    send_ref[...] = out_ref[...].astype(send_ref.dtype)


def place_columns(value, offset, store):
    width = value.shape[-1]
    shift = lax.rem(offset, width)
    turned = pltpu.roll(value, shift, value.ndim - 1)
    lane = lax.broadcasted_iota(jnp.int32, value.shape, value.ndim - 1)
    store(offset // width, jnp.where(lane >= shift, turned, 0.0))
    store(offset // width + 1, jnp.where(lane < shift, turned, 0.0))


def squeeze_body(offset_ref, used_ref, u_ref, out_ref, acc):
    acc[...] = jnp.zeros_like(acc)
    for slot in range(u_ref.shape[0]):
        value = u_ref[slot].astype(jnp.float32)
        lane = lax.broadcasted_iota(jnp.int32, value.shape, 1)

        def store(tile, part):
            acc[tile] += part

        place_columns(jnp.where(lane < used_ref[slot], value, 0.0), offset_ref[slot], store)
    out_ref[...] = acc[: out_ref.shape[0]].astype(out_ref.dtype)


def land_body(index_ref, target_ref, offset_ref, *refs):
    rows_ref, comp_ref = refs[-2:]
    for place, piece in enumerate(refs[:-2]):
        count = piece.shape[0]
        comp_ref[place * count : (place + 1) * count] = piece[...]
    rows_ref[...] = jnp.zeros_like(rows_ref)
    last = rows_ref.shape[0] - 1
    for slot in range(index_ref.shape[0]):
        block, target = index_ref[slot], target_ref[slot]
        value = comp_ref[jnp.maximum(block, 0)].astype(jnp.float32)
        value = jnp.where(block >= 0, value, 0.0).reshape(rows_ref.shape[2:])

        def store(tile, part):
            rows_ref[jnp.minimum(tile, last), target] += part.astype(rows_ref.dtype)

        place_columns(value, offset_ref[slot], store)


def lined_up(ref, rows):
    return jnp.concatenate([ref[tile].reshape(rows, ref.shape[-1]) for tile in range(ref.shape[0])], axis=1)


def expand_body(seg, columns, pos_ref, rows_ref, *refs):
    own_ref, other_ref, acc = refs[-3:]
    half, mine = pos_ref[0], pos_ref[1]
    clusters, sides, padded = acc.shape[:3]

    def run(shard):
        product = lax.dot_general(
            lined_up(rows_ref, clusters * sides * padded),
            lined_up(shard, seg),
            (((1,), (1,)), ((), ())),
            preferred_element_type=jnp.float32,
        )
        acc[...] = product.reshape(acc.shape)

    if len(refs) == 4:
        run(refs[0])
    else:
        inner = (mine == 1) | (mine == 2)

        @pl.when(inner)
        def _():
            run(refs[0])

        @pl.when(jnp.logical_not(inner))
        def _():
            run(refs[1])

    for target in range(clusters):
        span = slice(target * seg, (target + 1) * seg)
        own_ref[:, span] = acc[target, half, :columns].astype(own_ref.dtype)
        other_ref[:, span] = acc[target, 1 - half, :columns].astype(other_ref.dtype)


def expand_own_body(seg, columns, pos_ref, rows_ref, u_ref, side_ref, out_ref, acc):
    half = pos_ref[0]
    clusters, padded = acc.shape[:2]
    start = pl.multiple_of(half * padded, padded)
    tiles = [
        rows_ref[tile, :, pl.ds(start, padded)].reshape(clusters * padded, rows_ref.shape[3])
        for tile in range(rows_ref.shape[0])
    ]
    rows = jnp.concatenate(tiles, axis=1)
    for shard, place in ((u_ref, half), (side_ref, 1 - half)):
        product = lax.dot_general(
            rows,
            lined_up(shard, seg),
            (((1,), (1,)), ((), ())),
            preferred_element_type=jnp.float32,
        )
        acc[...] = product.reshape(acc.shape)
        for target in range(clusters):
            start = pl.multiple_of((2 * target + place) * seg, seg)
            out_ref[:, pl.ds(start, seg)] = acc[target, :columns].astype(out_ref.dtype)


def join_body(seg, clusters, pos_ref, first_ref, *refs):
    out_ref = refs[-1]
    half, mine = pos_ref[0], pos_ref[1]
    for target in range(clusters):
        start = pl.multiple_of((target * PLACES + mine) * 2 * seg, 2 * seg)
        span = slice(2 * target * seg, 2 * (target + 1) * seg)
        out_ref[:, pl.ds(start, 2 * seg)] = first_ref[:, span]
    for step in range(1, PLACES):
        place = jnp.bitwise_xor(mine, step)
        for target in range(clusters):
            span = slice(target * seg, (target + 1) * seg)
            base = (target * PLACES + place) * 2
            here = pl.multiple_of((base + half) * seg, seg)
            there = pl.multiple_of((base + 1 - half) * seg, seg)
            out_ref[:, pl.ds(here, seg)] = refs[step - 1][:, span]
            out_ref[:, pl.ds(there, seg)] = refs[PLACES + step - 2][:, span]


def after(value, *first):
    return lax.optimization_barrier((value, *first))[0]


PLACES = 4


def paired(incident, v_factors, u_factors, block_source, block_rank, block_slot, slot_target):
    columns, width = incident.shape
    padded = -(-columns // 16) * 16
    blocks, seg, rank_max = v_factors.shape
    capacity = u_factors.shape[0]
    owners = lax.axis_size("clus")
    clusters = width // (seg * 2 * PLACES)
    me, owner = lax.axis_index("rhs"), lax.axis_index("clus")
    position = jnp.stack([me % 2, me // 2]).astype(jnp.int32)

    def move(array, pairs):
        return lax.ppermute(array, "rhs", [(2 * a + i, 2 * b + i) for a, b in pairs for i in (0, 1)])

    def across(array):
        return lax.ppermute(array, "rhs", [(p, p ^ 1) for p in range(2 * PLACES)])

    far = [(p, p ^ 2) for p in range(PLACES)]
    near = [(p, p ^ 1) for p in range(PLACES)]
    middle = [(1, 2), (2, 1)]
    ends = [(1, 0), (2, 3)]

    def swap_all(arrays, bits):
        return [
            lax.ppermute(array, "clus", [(p, p ^ bit) for p in range(owners)])
            for array, bit in zip(arrays, bits)
        ]

    def spread(array, exchange):
        pieces = {0: array}
        for turn in range(1, owners.bit_length()):
            masks = [mask for mask in range(owners) if mask.bit_count() == turn]
            bits = [mask & -mask for mask in masks]
            moved = exchange([pieces[mask ^ bit] for mask, bit in zip(masks, bits)], bits)
            pieces.update(zip(masks, moved))
        return [pieces[mask] for mask in range(owners)]

    early = (blocks + 1) // 2
    v_far = [move(v_factors[:early], far), move(v_factors[early:], far)]
    v_near, v_middle = move(v_factors, near), move(v_factors, middle)
    packed = call(
        functools.partial(pack_body, seg),
        [
            jax.ShapeDtypeStruct((columns, count * PLACES * seg), incident.dtype)
            for count in (clusters // 2, clusters - clusters // 2)
        ],
        [SMEM, VMEM],
        "pack",
        moved=3 * columns * width,
    )(position, incident)
    table = jnp.stack([block_slot, block_rank], axis=1)
    table = jnp.concatenate(spread(table, swap_all), axis=0)
    slots, ranks = table[:, 0], table[:, 1]
    wanted = owner * capacity + lax.broadcasted_iota(jnp.int32, (capacity, slots.shape[0]), 0)
    order = lax.broadcasted_iota(jnp.int32, (capacity, slots.shape[0]), 1)
    found = wanted == slots[None, :]
    feeding = jnp.max(jnp.where(found, order, -1), axis=1)
    used = jnp.sum(jnp.where(found, ranks[None, :], 0), axis=1)
    earlier = lax.broadcasted_iota(jnp.int32, (capacity, capacity), 1)
    earlier = earlier < lax.broadcasted_iota(jnp.int32, (capacity, capacity), 0)
    offset = jnp.sum(jnp.where(earlier, used[None, :], 0), axis=1)
    place = lax.broadcasted_iota(jnp.int32, (owners, slots.shape[0]), 0)
    held = (slots[None, :] >= place * capacity) & (slots[None, :] < (place + 1) * capacity)
    fullest = jnp.max(jnp.sum(jnp.where(held, ranks[None, :], 0), axis=1))
    tiles = sorted({-(-capacity * part // 10) for part in (5, 6, 7, 8, 10)})
    level = sum((fullest > count * rank_max).astype(jnp.int32) for count in tiles[:-1])
    squeezed = call(
        squeeze_body,
        jax.ShapeDtypeStruct(u_factors.shape, u_factors.dtype),
        [SMEM, SMEM, VMEM],
        "squeeze",
        moved=4 * u_factors.size,
        scratch=[pltpu.VMEM((capacity + 2, seg, rank_max), jnp.float32)],
    )(after(offset, v_far[0]), used, u_factors)

    x_low, x_high = [across(part) for part in packed]
    v_ends = [move(after(v_far[0], *packed), ends), move(after(v_far[1], squeezed), ends)]
    begun, last = call(
        functools.partial(compress_own_body, seg),
        [
            jax.ShapeDtypeStruct((blocks, padded, rank_max), jnp.float32),
            jax.ShapeDtypeStruct((clusters, columns, seg), incident.dtype),
        ],
        [SMEM, SMEM] + [VMEM] * 5,
        "compress_own",
        flops=2 * blocks * columns * seg * PLACES * rank_max,
        moved=2 * columns * width + 2 * PLACES * v_factors.size,
    )(after(position, v_ends[0]), block_source, incident, v_factors, v_near, *v_far)
    arrived = lax.optimization_barrier(
        (begun, last, x_low, x_high, v_near, *v_far, v_middle, *v_ends, squeezed, level)
    )

    def rest(count, begun, last, x_low, x_high, *operands):
        partial, sent = call(
            functools.partial(compress_body, seg),
            [
                jax.ShapeDtypeStruct((blocks, 2, padded, rank_max), jnp.float32),
                jax.ShapeDtypeStruct((blocks, 2, padded, rank_max), jnp.bfloat16),
            ],
            [SMEM, SMEM] + [VMEM] * 11,
            "compress",
            flops=2 * blocks * columns * seg * PLACES * rank_max,
            moved=columns * width + 2 * PLACES * v_factors.size,
            scratch=[pltpu.VMEM((columns, width // 2), incident.dtype)],
        )(position, block_source, begun, last, x_low, x_high, v_factors, *operands[:-1])
        received = across(sent)
        target_factors = after(operands[-1], sent)[:count]
        u_far, u_near, u_middle = [move(target_factors, way) for way in (far, near, middle)]
        u_side = across(after(target_factors, received))
        rank_index = lax.broadcasted_iota(jnp.int32, (blocks, 1, 1, rank_max), 3)
        rows = jnp.where(
            rank_index < block_rank[:, None, None, None],
            partial + received.astype(jnp.float32),
            0.0,
        ).astype(jnp.bfloat16)

        pieces = spread(
            rows,
            lambda arrays, bits: lax.fori_loop(
                0, 1 + jnp.minimum(me, 0), lambda _, held: swap_all(held, bits), arrays
            ),
        )
        slot_rows = call(
            land_body,
            jax.ShapeDtypeStruct((count, clusters, 2 * padded, rank_max), jnp.bfloat16),
            [SMEM] * 3 + [VMEM] * owners,
            "land",
            moved=2 * owners * rows.size * (1 + clusters),
            scratch=[pltpu.VMEM((owners * blocks, 2, padded, rank_max), jnp.bfloat16)],
        )(feeding, slot_target, offset, *pieces)

        slot_rows = after(slot_rows, u_side)
        chunk = jax.ShapeDtypeStruct((columns, clusters * seg), jnp.bfloat16)
        own_parts, other_parts = [None] * PLACES, [None] * PLACES
        work = 4 * clusters * count * columns * seg * rank_max
        first = call(
            functools.partial(expand_own_body, seg, columns),
            jax.ShapeDtypeStruct((columns, 2 * clusters * seg), jnp.bfloat16),
            [SMEM] + [VMEM] * 3,
            "expand_own",
            flops=work,
            moved=4 * target_factors.size + 2 * slot_rows.size + 4 * columns * clusters * seg,
            scratch=[pltpu.VMEM((clusters, padded, seg), jnp.float32)],
        )(position, slot_rows, target_factors, u_side)
        finished = []
        for step in range(1, PLACES):
            shards = [u_near] if step == 1 else [u_far] if step == 2 else [u_middle, u_ends]
            if finished:
                slot_rows = after(slot_rows, own_parts[finished[-1]])
            if len(finished) == 2:
                slot_rows = after(slot_rows, first, other_parts[finished[0]])
            own, other = call(
                functools.partial(expand_body, seg, columns),
                [chunk, chunk],
                [SMEM, VMEM] + [VMEM] * len(shards),
                "expand",
                flops=work,
                moved=2 * target_factors.size + 2 * slot_rows.size + 4 * columns * clusters * seg,
                scratch=[pltpu.VMEM((clusters, 2, padded, seg), jnp.float32)],
            )(position, slot_rows, *shards)
            own_parts[step], other_parts[step] = own, across(other)
            finished.append(step)
            if step == 1:
                u_far = after(u_far, own)
                u_ends = move(u_far, ends)
        return call(
            functools.partial(join_body, seg, clusters),
            jax.ShapeDtypeStruct((columns, width), jnp.bfloat16),
            [SMEM] + [VMEM] * (2 * PLACES - 1),
            "join",
            moved=4 * columns * width,
        )(position, first, *own_parts[1:], *other_parts[1:])

    return lax.switch(
        arrived[-1], [functools.partial(rest, count) for count in tiles], *arrived[:-1]
    )


def gathered_plan(
    incident, v_factors, u_factors, block_source, block_rank, block_slot, slot_target
):
    columns = incident.shape[0]
    blocks = v_factors.shape[0]
    rank_max = v_factors.shape[2]
    capacity = u_factors.shape[0]
    devices = lax.axis_size("clus")
    cluster_len = v_factors.shape[1] * lax.axis_size("rhs")
    local_clusters = incident.shape[1] // cluster_len
    per_peer = max(1, (2 * blocks + devices - 1) // devices)
    sources = jnp.take(incident.reshape(columns, local_clusters, cluster_len), block_source, axis=1)
    compressed = jnp.einsum(
        "cbr,brk->bck",
        sources,
        lax.all_gather(v_factors, "rhs", axis=1, tiled=True),
        preferred_element_type=jnp.float32,
    )
    rank_index = lax.broadcasted_iota(jnp.int32, (blocks, 1, rank_max), 2)
    compressed = jnp.where(rank_index < block_rank[:, None, None], compressed, 0.0).astype(
        jnp.bfloat16
    )
    target_dev = block_slot // capacity
    target_pos = block_slot % capacity
    later_index = lax.broadcasted_iota(jnp.int32, (blocks, blocks), 0)
    earlier_index = lax.broadcasted_iota(jnp.int32, (blocks, blocks), 1)
    same_target = target_dev[None, :] == target_dev[:, None]
    before = jnp.sum((same_target & (earlier_index < later_index)).astype(jnp.int32), axis=1)
    position = target_dev * per_peer + before
    places = lax.broadcasted_iota(jnp.int32, (blocks, devices * per_peer), 1)
    placed = position[:, None] == places
    outgoing = jnp.einsum(
        "bp,bck->pck", placed.astype(jnp.bfloat16), compressed, preferred_element_type=jnp.float32
    ).astype(jnp.bfloat16)
    labels = jnp.sum(jnp.where(placed, target_pos[:, None] + 1, 0), axis=0) - 1
    arrived, arrived_labels = (
        lax.all_to_all(outgoing, "clus", split_axis=0, concat_axis=0, tiled=True),
        lax.all_to_all(labels, "clus", split_axis=0, concat_axis=0, tiled=True),
    )
    slot_ids = lax.broadcasted_iota(jnp.int32, (devices * per_peer, capacity), 1)
    landing = (arrived_labels[:, None] == slot_ids).astype(jnp.bfloat16)
    slot_rows = jnp.einsum(
        "pj,pck->jck", landing, arrived, preferred_element_type=jnp.float32
    ).astype(jnp.bfloat16)
    cluster_ids = lax.broadcasted_iota(jnp.int32, (capacity, local_clusters), 1)
    owners = (slot_target[:, None] == cluster_ids).astype(jnp.float32)
    products = jnp.einsum(
        "jck,jrk->jcr",
        slot_rows,
        lax.all_gather(u_factors, "rhs", axis=1, tiled=True),
        preferred_element_type=jnp.float32,
    )
    summed = jnp.einsum("jt,jcr->ctr", owners, products, precision=lax.Precision.HIGHEST)
    return summed.reshape(columns, local_clusters * cluster_len).astype(jnp.bfloat16)


def local(incident, v_factors, *rest):
    owners = lax.axis_size("clus")
    fits = (
        lax.axis_size("rhs") == 2 * PLACES
        and v_factors.shape[1] % 128 == 0
        and owners > 1
        and incident.shape[1] > v_factors.shape[1] * 2 * PLACES
        and owners & (owners - 1) == 0
    )
    return (paired if fits else gathered_plan)(incident, v_factors, *rest)


def solution(mesh):
    placed = (
        P("rhs", "clus"),
        P("clus", "rhs", None),
        P("clus", "rhs", None),
        P("clus"),
        P("clus"),
        P("clus"),
        P("clus"),
    )
    return jax.shard_map(
        local, mesh=mesh, in_specs=placed, out_specs=P("rhs", "clus"), check_vma=False
    )
```

```python
import functools

import jax
import jax.numpy as jnp
from jax import lax
from jax.experimental import pallas as pl
from jax.experimental.pallas import tpu as pltpu
from jax.sharding import PartitionSpec as P

VMEM = pl.BlockSpec(memory_space=pltpu.VMEM)
SMEM = pl.BlockSpec(memory_space=pltpu.SMEM)
LIMIT = 10 * 1024 * 1024


def call(
    body, out_shape, in_specs, name, flops=0, moved=0, scratch=(), grid=(), out_specs=None
):
    if out_specs is None:
        out_specs = [VMEM] * len(out_shape) if isinstance(out_shape, list) else VMEM
    return pl.pallas_call(
        body,
        grid=grid,
        out_shape=out_shape,
        in_specs=in_specs,
        out_specs=out_specs,
        scratch_shapes=list(scratch),
        compiler_params=pltpu.CompilerParams(vmem_limit_bytes=LIMIT),
        cost_estimate=pl.CostEstimate(flops=flops, bytes_accessed=moved, transcendentals=0),
        name=name,
    )


def pack_body(seg, pos_ref, x_ref, *out_refs):
    half, piece = 1 - pos_ref[0], 0
    for out_ref in out_refs:
        for place in range(0, out_ref.shape[1], seg):
            start = pl.multiple_of((2 * piece + half) * seg, seg)
            out_ref[:, place : place + seg] = x_ref[:, pl.ds(start, seg)]
            piece += 1


def compress_body(seg, pos_ref, source_ref, x_ref, xl_ref, xh_ref, *refs):
    v0, v1, v2, v3, v4, out_ref, send_ref, xn_ref = refs
    half, mine = pos_ref[0], pos_ref[1]
    columns = x_ref.shape[0]
    xn_ref[:, : xl_ref.shape[1]] = xl_ref[...]
    xn_ref[:, xl_ref.shape[1] :] = xh_ref[...]
    out_ref[...] = jnp.zeros_like(out_ref)

    def run(shards):
        for block in range(out_ref.shape[0]):
            source = source_ref[block]
            own = other = 0.0
            for step, shard in enumerate(shards):
                piece = source * PLACES + jnp.bitwise_xor(mine, step)
                here = pl.multiple_of((piece * 2 + half) * seg, seg)
                there = pl.multiple_of(piece * seg, seg)
                rows = shard[block]
                own += jnp.dot(x_ref[:, pl.ds(here, seg)], rows, preferred_element_type=jnp.float32)
                other += jnp.dot(
                    xn_ref[:, pl.ds(there, seg)], rows, preferred_element_type=jnp.float32
                )
            out_ref[block, half, :columns] = own
            out_ref[block, 1 - half, :columns] = other

    inner = (mine == 1) | (mine == 2)

    @pl.when(inner)
    def _():
        run((v0, v1, v2, v3))

    @pl.when(jnp.logical_not(inner))
    def _():
        run((v0, v1, v2, v4))

    send_ref[...] = out_ref[...].astype(send_ref.dtype)


def place_columns(value, offset, store):
    width = value.shape[-1]
    shift = lax.rem(offset, width)
    turned = pltpu.roll(value, shift, value.ndim - 1)
    lane = lax.broadcasted_iota(jnp.int32, value.shape, value.ndim - 1)
    store(offset // width, jnp.where(lane >= shift, turned, 0.0))
    store(offset // width + 1, jnp.where(lane < shift, turned, 0.0))


def squeeze_body(offset_ref, used_ref, u_ref, out_ref, acc):
    acc[...] = jnp.zeros_like(acc)
    for slot in range(u_ref.shape[0]):
        value = u_ref[slot].astype(jnp.float32)
        lane = lax.broadcasted_iota(jnp.int32, value.shape, 1)

        def store(tile, part):
            acc[tile] += part

        place_columns(jnp.where(lane < used_ref[slot], value, 0.0), offset_ref[slot], store)
    out_ref[...] = acc[: out_ref.shape[0]].astype(out_ref.dtype)


def land_body(index_ref, target_ref, offset_ref, *refs):
    rows_ref, comp_ref = refs[-2:]
    for place, piece in enumerate(refs[:-2]):
        count = piece.shape[0]
        comp_ref[place * count : (place + 1) * count] = piece[...]
    rows_ref[...] = jnp.zeros_like(rows_ref)
    last = rows_ref.shape[0] - 1
    for slot in range(index_ref.shape[0]):
        block, target = index_ref[slot], target_ref[slot]
        value = comp_ref[jnp.maximum(block, 0)].astype(jnp.float32)
        value = jnp.where(block >= 0, value, 0.0).reshape(rows_ref.shape[2:])

        def store(tile, part):
            rows_ref[jnp.minimum(tile, last), target] += part.astype(rows_ref.dtype)

        place_columns(value, offset_ref[slot], store)


def lined_up(ref, rows):
    return jnp.concatenate([ref[tile].reshape(rows, ref.shape[-1]) for tile in range(ref.shape[0])], axis=1)


def expand_body(seg, columns, pos_ref, rows_ref, *refs):
    own_ref, other_ref, acc = refs[-3:]
    half, mine = pos_ref[0], pos_ref[1]
    clusters, sides, padded = acc.shape[:3]

    def run(shard):
        product = lax.dot_general(
            lined_up(rows_ref, clusters * sides * padded),
            lined_up(shard, seg),
            (((1,), (1,)), ((), ())),
            preferred_element_type=jnp.float32,
        )
        acc[...] = product.reshape(acc.shape)

    if len(refs) == 4:
        run(refs[0])
    else:
        inner = (mine == 1) | (mine == 2)

        @pl.when(inner)
        def _():
            run(refs[0])

        @pl.when(jnp.logical_not(inner))
        def _():
            run(refs[1])

    for target in range(clusters):
        span = slice(target * seg, (target + 1) * seg)
        own_ref[:, span] = acc[target, half, :columns].astype(own_ref.dtype)
        other_ref[:, span] = acc[target, 1 - half, :columns].astype(other_ref.dtype)


def expand_own_body(seg, columns, pos_ref, rows_ref, u_ref, side_ref, out_ref, acc):
    half = pos_ref[0]
    clusters, padded = acc.shape[:2]
    start = pl.multiple_of(half * padded, padded)
    tiles = [
        rows_ref[tile, :, pl.ds(start, padded)].reshape(clusters * padded, rows_ref.shape[3])
        for tile in range(rows_ref.shape[0])
    ]
    rows = jnp.concatenate(tiles, axis=1)
    for shard, place in ((u_ref, half), (side_ref, 1 - half)):
        product = lax.dot_general(
            rows,
            lined_up(shard, seg),
            (((1,), (1,)), ((), ())),
            preferred_element_type=jnp.float32,
        )
        acc[...] = product.reshape(acc.shape)
        for target in range(clusters):
            start = pl.multiple_of((2 * target + place) * seg, seg)
            out_ref[:, pl.ds(start, seg)] = acc[target, :columns].astype(out_ref.dtype)


def join_body(seg, pos_ref, *refs):
    first_ref, second_ref, far_ref, far_other_ref, last_ref, last_other_ref, out_ref = refs
    half, mine, target = pos_ref[0], pos_ref[1], pl.program_id(0)
    pair = pl.ds(pl.multiple_of(2 * target * seg, 2 * seg), 2 * seg)
    span = pl.ds(pl.multiple_of(target * seg, seg), seg)
    for step, ref in enumerate((first_ref, second_ref)):
        start = pl.multiple_of(jnp.bitwise_xor(mine, step) * 2 * seg, 2 * seg)
        out_ref[:, pl.ds(start, 2 * seg)] = ref[:, pair]
    for step, own, other in ((2, far_ref, far_other_ref), (3, last_ref, last_other_ref)):
        base = jnp.bitwise_xor(mine, step) * 2
        here = pl.multiple_of((base + half) * seg, seg)
        there = pl.multiple_of((base + 1 - half) * seg, seg)
        out_ref[:, pl.ds(here, seg)] = own[:, span]
        out_ref[:, pl.ds(there, seg)] = other[:, span]


def after(value, *first):
    return lax.optimization_barrier((value, *first))[0]


PLACES = 4


def paired(incident, v_factors, u_factors, block_source, block_rank, block_slot, slot_target):
    columns, width = incident.shape
    padded = -(-columns // 16) * 16
    blocks, seg, rank_max = v_factors.shape
    capacity = u_factors.shape[0]
    owners = lax.axis_size("clus")
    clusters = width // (seg * 2 * PLACES)
    me, owner = lax.axis_index("rhs"), lax.axis_index("clus")
    position = jnp.stack([me % 2, me // 2]).astype(jnp.int32)

    def move(array, pairs):
        return lax.ppermute(array, "rhs", [(2 * a + i, 2 * b + i) for a, b in pairs for i in (0, 1)])

    def across(array):
        return lax.ppermute(array, "rhs", [(p, p ^ 1) for p in range(2 * PLACES)])

    far = [(p, p ^ 2) for p in range(PLACES)]
    near = [(p, p ^ 1) for p in range(PLACES)]
    middle = [(1, 2), (2, 1)]
    ends = [(1, 0), (2, 3)]

    stages = [1 << bit for bit in reversed(range((owners - 1).bit_length()))]

    def swapped(array, stage):
        return lax.ppermute(array, "clus", [(p, p ^ stage) for p in range(owners)])

    def double(array, stage):
        return jnp.concatenate([array, swapped(array, stage)], axis=0)

    v_far, v_near, v_middle = (
        move(v_factors, far),
        move(v_factors, near),
        move(v_factors, middle),
    )
    packed = call(
        functools.partial(pack_body, seg),
        [
            jax.ShapeDtypeStruct((columns, count * PLACES * seg), incident.dtype)
            for count in (clusters // 2, clusters - clusters // 2)
        ],
        [SMEM, VMEM],
        "pack",
        moved=3 * columns * width,
    )(position, incident)
    table = jnp.stack([block_slot, block_rank], axis=1)
    for stage in stages:
        table = double(table, stage)
    slots, ranks = table[:, 0], table[:, 1]
    wanted = owner * capacity + lax.broadcasted_iota(jnp.int32, (capacity, slots.shape[0]), 0)
    order = lax.broadcasted_iota(jnp.int32, (capacity, slots.shape[0]), 1)
    found = wanted == slots[None, :]
    feeding = jnp.max(jnp.where(found, order, -1), axis=1)
    used = jnp.sum(jnp.where(found, ranks[None, :], 0), axis=1)
    earlier = lax.broadcasted_iota(jnp.int32, (capacity, capacity), 1)
    earlier = earlier < lax.broadcasted_iota(jnp.int32, (capacity, capacity), 0)
    offset = jnp.sum(jnp.where(earlier, used[None, :], 0), axis=1)
    place = lax.broadcasted_iota(jnp.int32, (owners, slots.shape[0]), 0)
    held = (slots[None, :] >= place * capacity) & (slots[None, :] < (place + 1) * capacity)
    fullest = jnp.max(jnp.sum(jnp.where(held, ranks[None, :], 0), axis=1))
    tiles = sorted({-(-capacity * part // 10) for part in (5, 6, 7, 8, 10)})
    level = sum((fullest > count * rank_max).astype(jnp.int32) for count in tiles[:-1])
    squeezed = call(
        squeeze_body,
        jax.ShapeDtypeStruct(u_factors.shape, u_factors.dtype),
        [SMEM, SMEM, VMEM],
        "squeeze",
        moved=4 * u_factors.size,
        scratch=[pltpu.VMEM((capacity + 2, seg, rank_max), jnp.float32)],
    )(offset, used, u_factors)

    x_low, x_high = [across(part) for part in packed]
    v_ends = move(after(v_far, *packed), ends)
    arrived = lax.optimization_barrier(
        (x_low, x_high, v_near, v_far, v_middle, v_ends, squeezed, level)
    )

    def rest(count, x_low, x_high, v_near, v_far, v_middle, v_ends, squeezed):
        target_factors = squeezed[:count]
        u_far, u_near, u_middle = [move(target_factors, way) for way in (far, near, middle)]
        partial, sent = call(
            functools.partial(compress_body, seg),
            [
                jax.ShapeDtypeStruct((blocks, 2, padded, rank_max), jnp.float32),
                jax.ShapeDtypeStruct((blocks, 2, padded, rank_max), jnp.bfloat16),
            ],
            [SMEM, SMEM] + [VMEM] * 8,
            "compress",
            flops=4 * blocks * columns * seg * PLACES * rank_max,
            moved=3 * columns * width + 2 * PLACES * v_factors.size,
            scratch=[pltpu.VMEM((columns, width // 2), incident.dtype)],
        )(
            position, block_source, incident, x_low, x_high,
            v_factors, v_near, v_far, v_middle, v_ends,
        )
        received = across(sent)
        u_side = across(after(target_factors, received))
        rank_index = lax.broadcasted_iota(jnp.int32, (blocks, 1, 1, rank_max), 3)
        rows = jnp.where(
            rank_index < block_rank[:, None, None, None],
            partial + received.astype(jnp.float32),
            0.0,
        ).astype(jnp.bfloat16)

        pieces = [rows]
        for stage in stages:
            pieces += lax.fori_loop(
                0,
                1 + jnp.minimum(me, 0),
                lambda _, arrays, stage=stage: [swapped(array, stage) for array in arrays],
                pieces,
            )
            if stage == stages[0]:
                u_near_side = across(after(u_near, pieces[-1]))
        u_ends = move(after(u_far, pieces[-1]), ends)
        slot_rows = call(
            land_body,
            jax.ShapeDtypeStruct((count, clusters, 2 * padded, rank_max), jnp.bfloat16),
            [SMEM] * 3 + [VMEM] * owners,
            "land",
            moved=2 * owners * rows.size * (1 + clusters),
            scratch=[pltpu.VMEM((owners * blocks, 2, padded, rank_max), jnp.bfloat16)],
        )(feeding, slot_target, offset, *pieces)

        chunk = jax.ShapeDtypeStruct((columns, clusters * seg), jnp.bfloat16)
        work = 4 * clusters * count * columns * seg * rank_max

        def expand_own(shard, side):
            return call(
                functools.partial(expand_own_body, seg, columns),
                jax.ShapeDtypeStruct((columns, 2 * clusters * seg), jnp.bfloat16),
                [SMEM] + [VMEM] * 3,
                "expand_own",
                flops=work,
                moved=4 * shard.size + 2 * slot_rows.size + 4 * columns * clusters * seg,
                scratch=[pltpu.VMEM((clusters, padded, seg), jnp.float32)],
            )(position, slot_rows, shard, side)

        def expand(rows, *shards):
            own, other = call(
                functools.partial(expand_body, seg, columns),
                [chunk, chunk],
                [SMEM, VMEM] + [VMEM] * len(shards),
                "expand",
                flops=work,
                moved=2 * shards[0].size + 2 * slot_rows.size + 4 * columns * clusters * seg,
                scratch=[pltpu.VMEM((clusters, 2, padded, seg), jnp.float32)],
            )(position, rows, *shards)
            return own, across(other)

        far_chunk = expand(slot_rows, u_far)
        slot_rows = after(slot_rows, far_chunk[0])
        first, second = expand_own(target_factors, u_side), expand_own(u_near, u_near_side)
        last_chunk = expand(after(slot_rows, first, second), u_middle, u_ends)
        return first, second, *far_chunk, *last_chunk

    chunks = lax.switch(
        arrived[-1], [functools.partial(rest, count) for count in tiles], *arrived[:-1]
    )
    return call(
        functools.partial(join_body, seg),
        jax.ShapeDtypeStruct((columns, width), jnp.bfloat16),
        [SMEM] + [VMEM] * len(chunks),
        "join",
        moved=4 * columns * width,
        grid=(clusters,),
        out_specs=pl.BlockSpec((columns, width // clusters), lambda target: (0, target)),
    )(position, *chunks)


def gathered_plan(
    incident, v_factors, u_factors, block_source, block_rank, block_slot, slot_target
):
    columns = incident.shape[0]
    blocks = v_factors.shape[0]
    rank_max = v_factors.shape[2]
    capacity = u_factors.shape[0]
    devices = lax.axis_size("clus")
    cluster_len = v_factors.shape[1] * lax.axis_size("rhs")
    local_clusters = incident.shape[1] // cluster_len
    per_peer = max(1, (2 * blocks + devices - 1) // devices)
    sources = jnp.take(incident.reshape(columns, local_clusters, cluster_len), block_source, axis=1)
    compressed = jnp.einsum(
        "cbr,brk->bck",
        sources,
        lax.all_gather(v_factors, "rhs", axis=1, tiled=True),
        preferred_element_type=jnp.float32,
    )
    rank_index = lax.broadcasted_iota(jnp.int32, (blocks, 1, rank_max), 2)
    compressed = jnp.where(rank_index < block_rank[:, None, None], compressed, 0.0).astype(
        jnp.bfloat16
    )
    target_dev = block_slot // capacity
    target_pos = block_slot % capacity
    later_index = lax.broadcasted_iota(jnp.int32, (blocks, blocks), 0)
    earlier_index = lax.broadcasted_iota(jnp.int32, (blocks, blocks), 1)
    same_target = target_dev[None, :] == target_dev[:, None]
    before = jnp.sum((same_target & (earlier_index < later_index)).astype(jnp.int32), axis=1)
    position = target_dev * per_peer + before
    places = lax.broadcasted_iota(jnp.int32, (blocks, devices * per_peer), 1)
    placed = position[:, None] == places
    outgoing = jnp.einsum(
        "bp,bck->pck", placed.astype(jnp.bfloat16), compressed, preferred_element_type=jnp.float32
    ).astype(jnp.bfloat16)
    labels = jnp.sum(jnp.where(placed, target_pos[:, None] + 1, 0), axis=0) - 1
    arrived, arrived_labels = (
        lax.all_to_all(outgoing, "clus", split_axis=0, concat_axis=0, tiled=True),
        lax.all_to_all(labels, "clus", split_axis=0, concat_axis=0, tiled=True),
    )
    slot_ids = lax.broadcasted_iota(jnp.int32, (devices * per_peer, capacity), 1)
    landing = (arrived_labels[:, None] == slot_ids).astype(jnp.bfloat16)
    slot_rows = jnp.einsum(
        "pj,pck->jck", landing, arrived, preferred_element_type=jnp.float32
    ).astype(jnp.bfloat16)
    cluster_ids = lax.broadcasted_iota(jnp.int32, (capacity, local_clusters), 1)
    owners = (slot_target[:, None] == cluster_ids).astype(jnp.float32)
    products = jnp.einsum(
        "jck,jrk->jcr",
        slot_rows,
        lax.all_gather(u_factors, "rhs", axis=1, tiled=True),
        preferred_element_type=jnp.float32,
    )
    summed = jnp.einsum("jt,jcr->ctr", owners, products, precision=lax.Precision.HIGHEST)
    return summed.reshape(columns, local_clusters * cluster_len).astype(jnp.bfloat16)


def local(incident, v_factors, *rest):
    owners = lax.axis_size("clus")
    fits = (
        lax.axis_size("rhs") == 2 * PLACES
        and v_factors.shape[1] % 128 == 0
        and owners > 1
        and incident.shape[1] > v_factors.shape[1] * 2 * PLACES
        and owners & (owners - 1) == 0
    )
    return (paired if fits else gathered_plan)(incident, v_factors, *rest)


def solution(mesh):
    placed = (
        P("rhs", "clus"),
        P("clus", "rhs", None),
        P("clus", "rhs", None),
        P("clus"),
        P("clus"),
        P("clus"),
        P("clus"),
    )
    return jax.shard_map(
        local, mesh=mesh, in_specs=placed, out_specs=P("rhs", "clus"), check_vma=False
    )
```

```python
import functools

import jax
import jax.numpy as jnp
from jax import lax
from jax.experimental import pallas as pl
from jax.experimental.pallas import tpu as pltpu
from jax.sharding import PartitionSpec as P

VMEM = pl.BlockSpec(memory_space=pltpu.VMEM)
SMEM = pl.BlockSpec(memory_space=pltpu.SMEM)
LIMIT = 10 * 1024 * 1024


def call(body, out_shape, in_specs, name, flops=0, moved=0, scratch=()):
    out_specs = [VMEM] * len(out_shape) if isinstance(out_shape, list) else VMEM
    return pl.pallas_call(
        body,
        out_shape=out_shape,
        in_specs=in_specs,
        out_specs=out_specs,
        scratch_shapes=list(scratch),
        compiler_params=pltpu.CompilerParams(vmem_limit_bytes=LIMIT),
        cost_estimate=pl.CostEstimate(flops=flops, bytes_accessed=moved, transcendentals=0),
        name=name,
    )


def pack_body(seg, pos_ref, x_ref, *out_refs):
    half, piece = 1 - pos_ref[0], 0
    for out_ref in out_refs:
        for place in range(0, out_ref.shape[1], seg):
            start = pl.multiple_of((2 * piece + half) * seg, seg)
            out_ref[:, place : place + seg] = x_ref[:, pl.ds(start, seg)]
            piece += 1


def compress_body(seg, pos_ref, source_ref, x_ref, xl_ref, xh_ref, *refs):
    v0, v1, v2, v3, v4, out_ref, send_ref, xn_ref = refs
    half, mine = pos_ref[0], pos_ref[1]
    columns = x_ref.shape[0]
    xn_ref[:, : xl_ref.shape[1]] = xl_ref[...]
    xn_ref[:, xl_ref.shape[1] :] = xh_ref[...]
    out_ref[...] = jnp.zeros_like(out_ref)

    def run(shards):
        for block in range(out_ref.shape[0]):
            source = source_ref[block]
            own = other = 0.0
            for step, shard in enumerate(shards):
                piece = source * PLACES + jnp.bitwise_xor(mine, step)
                here = pl.multiple_of((piece * 2 + half) * seg, seg)
                there = pl.multiple_of(piece * seg, seg)
                rows = shard[block]
                own += jnp.dot(x_ref[:, pl.ds(here, seg)], rows, preferred_element_type=jnp.float32)
                other += jnp.dot(
                    xn_ref[:, pl.ds(there, seg)], rows, preferred_element_type=jnp.float32
                )
            out_ref[block, half, :columns] = own
            out_ref[block, 1 - half, :columns] = other

    inner = (mine == 1) | (mine == 2)

    @pl.when(inner)
    def _():
        run((v0, v1, v2, v3))

    @pl.when(jnp.logical_not(inner))
    def _():
        run((v0, v1, v2, v4))

    send_ref[...] = out_ref[...].astype(send_ref.dtype)


def place_columns(value, offset, store):
    width = value.shape[-1]
    shift = lax.rem(offset, width)
    turned = pltpu.roll(value, shift, value.ndim - 1)
    lane = lax.broadcasted_iota(jnp.int32, value.shape, value.ndim - 1)
    store(offset // width, jnp.where(lane >= shift, turned, 0.0))
    store(offset // width + 1, jnp.where(lane < shift, turned, 0.0))


def squeeze_body(offset_ref, used_ref, u_ref, out_ref, acc):
    acc[...] = jnp.zeros_like(acc)
    for slot in range(u_ref.shape[0]):
        value = u_ref[slot].astype(jnp.float32)
        lane = lax.broadcasted_iota(jnp.int32, value.shape, 1)

        def store(tile, part):
            acc[tile] += part

        place_columns(jnp.where(lane < used_ref[slot], value, 0.0), offset_ref[slot], store)
    out_ref[...] = acc[: out_ref.shape[0]].astype(out_ref.dtype)


def land_body(index_ref, target_ref, offset_ref, comp_ref, rows_ref):
    rows_ref[...] = jnp.zeros_like(rows_ref)
    last = rows_ref.shape[0] - 1
    for slot in range(index_ref.shape[0]):
        block, target = index_ref[slot], target_ref[slot]
        value = comp_ref[jnp.maximum(block, 0)].astype(jnp.float32)
        value = jnp.where(block >= 0, value, 0.0).reshape(rows_ref.shape[2:])

        def store(tile, part):
            rows_ref[jnp.minimum(tile, last), target] += part.astype(rows_ref.dtype)

        place_columns(value, offset_ref[slot], store)


def lined_up(ref, rows):
    return jnp.concatenate([ref[tile].reshape(rows, ref.shape[-1]) for tile in range(ref.shape[0])], axis=1)


def expand_body(seg, columns, pos_ref, rows_ref, *refs):
    own_ref, other_ref, acc = refs[-3:]
    half, mine = pos_ref[0], pos_ref[1]
    clusters, sides, padded = acc.shape[:3]

    def run(shard):
        product = lax.dot_general(
            lined_up(rows_ref, clusters * sides * padded),
            lined_up(shard, seg),
            (((1,), (1,)), ((), ())),
            preferred_element_type=jnp.float32,
        )
        acc[...] = product.reshape(acc.shape)

    if len(refs) == 4:
        run(refs[0])
    else:
        inner = (mine == 1) | (mine == 2)

        @pl.when(inner)
        def _():
            run(refs[0])

        @pl.when(jnp.logical_not(inner))
        def _():
            run(refs[1])

    for target in range(clusters):
        span = slice(target * seg, (target + 1) * seg)
        own_ref[:, span] = acc[target, half, :columns].astype(own_ref.dtype)
        other_ref[:, span] = acc[target, 1 - half, :columns].astype(other_ref.dtype)


def expand_own_body(seg, columns, pos_ref, rows_ref, u_ref, side_ref, out_ref, acc):
    half = pos_ref[0]
    clusters, padded = acc.shape[:2]
    start = pl.multiple_of(half * padded, padded)
    tiles = [
        rows_ref[tile, :, pl.ds(start, padded)].reshape(clusters * padded, rows_ref.shape[3])
        for tile in range(rows_ref.shape[0])
    ]
    rows = jnp.concatenate(tiles, axis=1)
    for shard, place in ((u_ref, half), (side_ref, 1 - half)):
        product = lax.dot_general(
            rows,
            lined_up(shard, seg),
            (((1,), (1,)), ((), ())),
            preferred_element_type=jnp.float32,
        )
        acc[...] = product.reshape(acc.shape)
        for target in range(clusters):
            start = pl.multiple_of((2 * target + place) * seg, seg)
            out_ref[:, pl.ds(start, seg)] = acc[target, :columns].astype(out_ref.dtype)


def join_body(seg, clusters, pos_ref, first_ref, *refs):
    out_ref = refs[-1]
    half, mine = pos_ref[0], pos_ref[1]
    for target in range(clusters):
        start = pl.multiple_of((target * PLACES + mine) * 2 * seg, 2 * seg)
        span = slice(2 * target * seg, 2 * (target + 1) * seg)
        out_ref[:, pl.ds(start, 2 * seg)] = first_ref[:, span]
    for step in range(1, PLACES):
        place = jnp.bitwise_xor(mine, step)
        for target in range(clusters):
            span = slice(target * seg, (target + 1) * seg)
            base = (target * PLACES + place) * 2
            here = pl.multiple_of((base + half) * seg, seg)
            there = pl.multiple_of((base + 1 - half) * seg, seg)
            out_ref[:, pl.ds(here, seg)] = refs[step - 1][:, span]
            out_ref[:, pl.ds(there, seg)] = refs[PLACES + step - 2][:, span]


def after(value, *first):
    return lax.optimization_barrier((value, *first))[0]


PLACES = 4


def paired(incident, v_factors, u_factors, block_source, block_rank, block_slot, slot_target):
    columns, width = incident.shape
    padded = -(-columns // 16) * 16
    blocks, seg, rank_max = v_factors.shape
    capacity = u_factors.shape[0]
    owners = lax.axis_size("clus")
    clusters = width // (seg * 2 * PLACES)
    me, owner = lax.axis_index("rhs"), lax.axis_index("clus")
    position = jnp.stack([me % 2, me // 2]).astype(jnp.int32)

    def move(array, pairs):
        return lax.ppermute(array, "rhs", [(2 * a + i, 2 * b + i) for a, b in pairs for i in (0, 1)])

    def across(array):
        return lax.ppermute(array, "rhs", [(p, p ^ 1) for p in range(2 * PLACES)])

    far = [(p, p ^ 2) for p in range(PLACES)]
    near = [(p, p ^ 1) for p in range(PLACES)]
    middle = [(1, 2), (2, 1)]
    ends = [(1, 0), (2, 3)]

    stages = [1 << bit for bit in reversed(range((owners - 1).bit_length()))]

    def swapped(array, stage):
        return lax.ppermute(array, "clus", [(p, p ^ stage) for p in range(owners)])

    def double(array, stage):
        return jnp.concatenate([array, swapped(array, stage)], axis=0)

    v_far, v_near = move(v_factors, far), move(v_factors, near)
    packed = call(
        functools.partial(pack_body, seg),
        [
            jax.ShapeDtypeStruct((columns, count * PLACES * seg), incident.dtype)
            for count in (clusters // 2, clusters - clusters // 2)
        ],
        [SMEM, VMEM],
        "pack",
        moved=3 * columns * width,
    )(position, incident)
    table = jnp.stack([block_slot, block_rank], axis=1)
    for stage in stages:
        table = double(table, stage)
    slots, ranks = table[:, 0], table[:, 1]
    wanted = owner * capacity + lax.broadcasted_iota(jnp.int32, (capacity, slots.shape[0]), 0)
    order = lax.broadcasted_iota(jnp.int32, (capacity, slots.shape[0]), 1)
    found = wanted == slots[None, :]
    feeding = jnp.max(jnp.where(found, order, -1), axis=1)
    used = jnp.sum(jnp.where(found, ranks[None, :], 0), axis=1)
    earlier = lax.broadcasted_iota(jnp.int32, (capacity, capacity), 1)
    earlier = earlier < lax.broadcasted_iota(jnp.int32, (capacity, capacity), 0)
    offset = jnp.sum(jnp.where(earlier, used[None, :], 0), axis=1)
    place = lax.broadcasted_iota(jnp.int32, (owners, slots.shape[0]), 0)
    held = (slots[None, :] >= place * capacity) & (slots[None, :] < (place + 1) * capacity)
    fullest = jnp.max(jnp.sum(jnp.where(held, ranks[None, :], 0), axis=1))
    tiles = sorted({-(-capacity * part // 10) for part in (5, 6, 7, 8, 10)})
    level = sum((fullest > count * rank_max).astype(jnp.int32) for count in tiles[:-1])
    squeezed = call(
        squeeze_body,
        jax.ShapeDtypeStruct(u_factors.shape, u_factors.dtype),
        [SMEM, SMEM, VMEM],
        "squeeze",
        moved=4 * u_factors.size,
        scratch=[pltpu.VMEM((capacity + 2, seg, rank_max), jnp.float32)],
    )(offset, used, u_factors)

    x_low, x_high = [across(part) for part in packed]
    v_ends = move(after(v_far, *packed), ends)
    v_middle = move(after(v_factors, v_far), middle)
    arrived = lax.optimization_barrier(
        (x_low, x_high, v_near, v_far, v_middle, v_ends, squeezed, level)
    )

    def rest(count, x_low, x_high, v_near, v_far, v_middle, v_ends, squeezed):
        target_factors = squeezed[:count]
        u_far, u_near = move(target_factors, far), move(target_factors, near)
        partial, sent = call(
            functools.partial(compress_body, seg),
            [
                jax.ShapeDtypeStruct((blocks, 2, padded, rank_max), jnp.float32),
                jax.ShapeDtypeStruct((blocks, 2, padded, rank_max), jnp.bfloat16),
            ],
            [SMEM, SMEM] + [VMEM] * 8,
            "compress",
            flops=4 * blocks * columns * seg * PLACES * rank_max,
            moved=3 * columns * width + 2 * PLACES * v_factors.size,
            scratch=[pltpu.VMEM((columns, width // 2), incident.dtype)],
        )(
            position, block_source, incident, x_low, x_high,
            v_factors, v_near, v_far, v_middle, v_ends,
        )
        received = across(sent)
        u_side = across(after(target_factors, received))
        rank_index = lax.broadcasted_iota(jnp.int32, (blocks, 1, 1, rank_max), 3)
        rows = jnp.where(
            rank_index < block_rank[:, None, None, None],
            partial + received.astype(jnp.float32),
            0.0,
        ).astype(jnp.bfloat16)

        rounds, gathered = 1 + jnp.minimum(me, 0), rows
        for stage in stages:
            other = lax.fori_loop(
                0, rounds, lambda _, array, stage=stage: swapped(array, stage), gathered
            )
            gathered = jnp.concatenate([gathered, other], axis=0)
        u_ends = move(after(u_far, gathered), ends)
        u_middle = move(after(target_factors, u_far, gathered), middle)
        slot_rows = call(
            land_body,
            jax.ShapeDtypeStruct((count, clusters, 2 * padded, rank_max), jnp.bfloat16),
            [SMEM, SMEM, SMEM, VMEM],
            "land",
            moved=2 * gathered.size * (1 + clusters),
        )(feeding, slot_target, offset, gathered)

        chunk = jax.ShapeDtypeStruct((columns, clusters * seg), jnp.bfloat16)
        own_parts, other_parts = [None] * PLACES, [None] * PLACES
        work = 4 * clusters * count * columns * seg * rank_max
        first = call(
            functools.partial(expand_own_body, seg, columns),
            jax.ShapeDtypeStruct((columns, 2 * clusters * seg), jnp.bfloat16),
            [SMEM] + [VMEM] * 3,
            "expand_own",
            flops=work,
            moved=4 * target_factors.size + 2 * slot_rows.size + 4 * columns * clusters * seg,
            scratch=[pltpu.VMEM((clusters, padded, seg), jnp.float32)],
        )(position, slot_rows, target_factors, u_side)
        finished = []
        for step, shards in ((1, [u_near]), (2, [u_far]), (3, [u_middle, u_ends])):
            if finished:
                slot_rows = after(slot_rows, own_parts[finished[-1]])
            if len(finished) == 2:
                slot_rows = after(slot_rows, first, other_parts[finished[0]])
            own, other = call(
                functools.partial(expand_body, seg, columns),
                [chunk, chunk],
                [SMEM, VMEM] + [VMEM] * len(shards),
                "expand",
                flops=work,
                moved=2 * target_factors.size + 2 * slot_rows.size + 4 * columns * clusters * seg,
                scratch=[pltpu.VMEM((clusters, 2, padded, seg), jnp.float32)],
            )(position, slot_rows, *shards)
            own_parts[step], other_parts[step] = own, across(other)
            finished.append(step)
        return call(
            functools.partial(join_body, seg, clusters),
            jax.ShapeDtypeStruct((columns, width), jnp.bfloat16),
            [SMEM] + [VMEM] * (2 * PLACES - 1),
            "join",
            moved=4 * columns * width,
        )(position, first, *own_parts[1:], *other_parts[1:])

    return lax.switch(
        arrived[-1], [functools.partial(rest, count) for count in tiles], *arrived[:-1]
    )


def gathered_plan(
    incident, v_factors, u_factors, block_source, block_rank, block_slot, slot_target
):
    columns = incident.shape[0]
    blocks = v_factors.shape[0]
    rank_max = v_factors.shape[2]
    capacity = u_factors.shape[0]
    devices = lax.axis_size("clus")
    cluster_len = v_factors.shape[1] * lax.axis_size("rhs")
    local_clusters = incident.shape[1] // cluster_len
    per_peer = max(1, (2 * blocks + devices - 1) // devices)
    sources = jnp.take(incident.reshape(columns, local_clusters, cluster_len), block_source, axis=1)
    compressed = jnp.einsum(
        "cbr,brk->bck",
        sources,
        lax.all_gather(v_factors, "rhs", axis=1, tiled=True),
        preferred_element_type=jnp.float32,
    )
    rank_index = lax.broadcasted_iota(jnp.int32, (blocks, 1, rank_max), 2)
    compressed = jnp.where(rank_index < block_rank[:, None, None], compressed, 0.0).astype(
        jnp.bfloat16
    )
    target_dev = block_slot // capacity
    target_pos = block_slot % capacity
    later_index = lax.broadcasted_iota(jnp.int32, (blocks, blocks), 0)
    earlier_index = lax.broadcasted_iota(jnp.int32, (blocks, blocks), 1)
    same_target = target_dev[None, :] == target_dev[:, None]
    before = jnp.sum((same_target & (earlier_index < later_index)).astype(jnp.int32), axis=1)
    position = target_dev * per_peer + before
    places = lax.broadcasted_iota(jnp.int32, (blocks, devices * per_peer), 1)
    placed = position[:, None] == places
    outgoing = jnp.einsum(
        "bp,bck->pck", placed.astype(jnp.bfloat16), compressed, preferred_element_type=jnp.float32
    ).astype(jnp.bfloat16)
    labels = jnp.sum(jnp.where(placed, target_pos[:, None] + 1, 0), axis=0) - 1
    arrived, arrived_labels = (
        lax.all_to_all(outgoing, "clus", split_axis=0, concat_axis=0, tiled=True),
        lax.all_to_all(labels, "clus", split_axis=0, concat_axis=0, tiled=True),
    )
    slot_ids = lax.broadcasted_iota(jnp.int32, (devices * per_peer, capacity), 1)
    landing = (arrived_labels[:, None] == slot_ids).astype(jnp.bfloat16)
    slot_rows = jnp.einsum(
        "pj,pck->jck", landing, arrived, preferred_element_type=jnp.float32
    ).astype(jnp.bfloat16)
    cluster_ids = lax.broadcasted_iota(jnp.int32, (capacity, local_clusters), 1)
    owners = (slot_target[:, None] == cluster_ids).astype(jnp.float32)
    products = jnp.einsum(
        "jck,jrk->jcr",
        slot_rows,
        lax.all_gather(u_factors, "rhs", axis=1, tiled=True),
        preferred_element_type=jnp.float32,
    )
    summed = jnp.einsum("jt,jcr->ctr", owners, products, precision=lax.Precision.HIGHEST)
    return summed.reshape(columns, local_clusters * cluster_len).astype(jnp.bfloat16)


def local(incident, v_factors, *rest):
    owners = lax.axis_size("clus")
    fits = (
        lax.axis_size("rhs") == 2 * PLACES
        and v_factors.shape[1] % 128 == 0
        and owners > 1
        and incident.shape[1] > v_factors.shape[1] * 2 * PLACES
        and owners & (owners - 1) == 0
    )
    return (paired if fits else gathered_plan)(incident, v_factors, *rest)


def solution(mesh):
    placed = (
        P("rhs", "clus"),
        P("clus", "rhs", None),
        P("clus", "rhs", None),
        P("clus"),
        P("clus"),
        P("clus"),
        P("clus"),
    )
    return jax.shard_map(
        local, mesh=mesh, in_specs=placed, out_specs=P("rhs", "clus"), check_vma=False
    )
```

```python
import functools

import jax
import jax.numpy as jnp
from jax import lax
from jax.experimental import pallas as pl
from jax.experimental.pallas import tpu as pltpu
from jax.sharding import PartitionSpec as P

VMEM = pl.BlockSpec(memory_space=pltpu.VMEM)
SMEM = pl.BlockSpec(memory_space=pltpu.SMEM)
LIMIT = 10 * 1024 * 1024


def call(body, out_shape, in_specs, name, flops=0, moved=0, scratch=()):
    out_specs = [VMEM] * len(out_shape) if isinstance(out_shape, list) else VMEM
    return pl.pallas_call(
        body,
        out_shape=out_shape,
        in_specs=in_specs,
        out_specs=out_specs,
        scratch_shapes=list(scratch),
        compiler_params=pltpu.CompilerParams(vmem_limit_bytes=LIMIT),
        cost_estimate=pl.CostEstimate(flops=flops, bytes_accessed=moved, transcendentals=0),
        name=name,
    )


def pack_body(seg, pos_ref, x_ref, *out_refs):
    half, piece = 1 - pos_ref[0], 0
    for out_ref in out_refs:
        for place in range(0, out_ref.shape[1], seg):
            start = pl.multiple_of((2 * piece + half) * seg, seg)
            out_ref[:, place : place + seg] = x_ref[:, pl.ds(start, seg)]
            piece += 1


def compress_body(seg, pos_ref, source_ref, x_ref, xl_ref, xh_ref, *refs):
    v0, v1, v2, v3, v4, out_ref, low_ref, high_ref, xn_ref = refs
    half, mine = pos_ref[0], pos_ref[1]
    columns = x_ref.shape[0]
    xn_ref[:, : xl_ref.shape[1]] = xl_ref[...]
    xn_ref[:, xl_ref.shape[1] :] = xh_ref[...]
    out_ref[...] = jnp.zeros_like(out_ref)

    def run(shards):
        for block in range(out_ref.shape[0]):
            source = source_ref[block]
            own = other = 0.0
            for step, shard in enumerate(shards):
                piece = source * PLACES + jnp.bitwise_xor(mine, step)
                here = pl.multiple_of((piece * 2 + half) * seg, seg)
                there = pl.multiple_of(piece * seg, seg)
                rows = shard[block]
                own += jnp.dot(x_ref[:, pl.ds(here, seg)], rows, preferred_element_type=jnp.float32)
                other += jnp.dot(
                    xn_ref[:, pl.ds(there, seg)], rows, preferred_element_type=jnp.float32
                )
            out_ref[block, half, :columns] = own
            out_ref[block, 1 - half, :columns] = other

    inner = (mine == 1) | (mine == 2)

    @pl.when(inner)
    def _():
        run((v0, v1, v2, v3))

    @pl.when(jnp.logical_not(inner))
    def _():
        run((v0, v1, v2, v4))

    low_ref[...] = out_ref[:, 0].astype(low_ref.dtype)
    high_ref[...] = out_ref[:, 1].astype(high_ref.dtype)


def place_columns(value, offset, store):
    width = value.shape[-1]
    shift = lax.rem(offset, width)
    turned = pltpu.roll(value, shift, value.ndim - 1)
    lane = lax.broadcasted_iota(jnp.int32, value.shape, value.ndim - 1)
    store(offset // width, jnp.where(lane >= shift, turned, 0.0))
    store(offset // width + 1, jnp.where(lane < shift, turned, 0.0))


def squeeze_body(offset_ref, used_ref, u_ref, out_ref, acc):
    acc[...] = jnp.zeros_like(acc)
    for slot in range(u_ref.shape[0]):
        value = u_ref[slot].astype(jnp.float32)
        lane = lax.broadcasted_iota(jnp.int32, value.shape, 1)

        def store(tile, part):
            acc[tile] += part

        place_columns(jnp.where(lane < used_ref[slot], value, 0.0), offset_ref[slot], store)
    out_ref[...] = acc[: out_ref.shape[0]].astype(out_ref.dtype)


def land_body(index_ref, target_ref, offset_ref, comp_ref, rows_ref):
    rows_ref[...] = jnp.zeros_like(rows_ref)
    last = rows_ref.shape[0] - 1
    for slot in range(index_ref.shape[0]):
        block, target = index_ref[slot], target_ref[slot]
        value = comp_ref[jnp.maximum(block, 0)].astype(jnp.float32)
        value = jnp.where(block >= 0, value, 0.0).reshape(rows_ref.shape[2:])

        def store(tile, part):
            rows_ref[jnp.minimum(tile, last), target] += part.astype(rows_ref.dtype)

        place_columns(value, offset_ref[slot], store)


def lined_up(rows, *refs):
    tiles = [ref[tile].reshape(rows, ref.shape[-1]) for ref in refs for tile in range(ref.shape[0])]
    return jnp.concatenate(tiles, axis=1)


def expand_body(seg, columns, choices, pos_ref, rows_ref, *refs):
    own_ref, other_ref, acc = refs[-3:]
    half, mine = pos_ref[0], pos_ref[1]
    clusters, sides, padded = acc.shape[:3]

    def run(choice):
        product = lax.dot_general(
            lined_up(clusters * sides * padded, rows_ref),
            lined_up(seg, *refs[choice]),
            (((1,), (1,)), ((), ())),
            preferred_element_type=jnp.float32,
        )
        acc[...] = product.reshape(acc.shape)

    if len(choices) == 1:
        run(choices[0])
    else:
        inner = (mine == 1) | (mine == 2)

        @pl.when(inner)
        def _():
            run(choices[0])

        @pl.when(jnp.logical_not(inner))
        def _():
            run(choices[1])

    for target in range(clusters):
        span = slice(target * seg, (target + 1) * seg)
        own_ref[:, span] = acc[target, half, :columns].astype(own_ref.dtype)
        other_ref[:, span] = acc[target, 1 - half, :columns].astype(other_ref.dtype)


def expand_own_body(seg, columns, pos_ref, rows_ref, u_ref, side_ref, out_ref, acc):
    half = pos_ref[0]
    clusters, padded = acc.shape[:2]
    start = pl.multiple_of(half * padded, padded)
    tiles = [
        rows_ref[tile, :, pl.ds(start, padded)].reshape(clusters * padded, rows_ref.shape[3])
        for tile in range(rows_ref.shape[0])
    ]
    rows = jnp.concatenate(tiles, axis=1)
    for shard, place in ((u_ref, half), (side_ref, 1 - half)):
        product = lax.dot_general(
            rows,
            lined_up(seg, shard),
            (((1,), (1,)), ((), ())),
            preferred_element_type=jnp.float32,
        )
        acc[...] = product.reshape(acc.shape)
        for target in range(clusters):
            start = pl.multiple_of((2 * target + place) * seg, seg)
            out_ref[:, pl.ds(start, seg)] = acc[target, :columns].astype(out_ref.dtype)


def join_body(seg, clusters, pos_ref, first_ref, *refs):
    out_ref = refs[-1]
    half, mine = pos_ref[0], pos_ref[1]
    for target in range(clusters):
        start = pl.multiple_of((target * PLACES + mine) * 2 * seg, 2 * seg)
        span = slice(2 * target * seg, 2 * (target + 1) * seg)
        out_ref[:, pl.ds(start, 2 * seg)] = first_ref[:, span]
    for step in range(1, PLACES):
        place = jnp.bitwise_xor(mine, step)
        for target in range(clusters):
            span = slice(target * seg, (target + 1) * seg)
            base = (target * PLACES + place) * 2
            here = pl.multiple_of((base + half) * seg, seg)
            there = pl.multiple_of((base + 1 - half) * seg, seg)
            out_ref[:, pl.ds(here, seg)] = refs[step - 1][:, span]
            out_ref[:, pl.ds(there, seg)] = refs[PLACES + step - 2][:, span]


def after(value, *first):
    return lax.optimization_barrier((value, *first))[0]


PLACES = 4


def paired(incident, v_factors, u_factors, block_source, block_rank, block_slot, slot_target):
    columns, width = incident.shape
    padded = -(-columns // 16) * 16
    blocks, seg, rank_max = v_factors.shape
    capacity = u_factors.shape[0]
    owners = lax.axis_size("clus")
    clusters = width // (seg * 2 * PLACES)
    me, owner = lax.axis_index("rhs"), lax.axis_index("clus")
    position = jnp.stack([me % 2, me // 2]).astype(jnp.int32)

    def move(array, pairs):
        return lax.ppermute(array, "rhs", [(2 * a + i, 2 * b + i) for a, b in pairs for i in (0, 1)])

    def across(array):
        return lax.ppermute(array, "rhs", [(p, p ^ 1) for p in range(2 * PLACES)])

    far = [(p, p ^ 2) for p in range(PLACES)]
    near = [(p, p ^ 1) for p in range(PLACES)]
    middle = [(1, 2), (2, 1)]
    ends = [(1, 0), (2, 3)]

    stages = [1 << bit for bit in reversed(range((owners - 1).bit_length()))]

    def swapped(array, stage):
        return lax.ppermute(array, "clus", [(p, p ^ stage) for p in range(owners)])

    def double(array, stage):
        return jnp.concatenate([array, swapped(array, stage)], axis=0)

    v_far, v_near = move(v_factors, far), move(v_factors, near)
    packed = call(
        functools.partial(pack_body, seg),
        [
            jax.ShapeDtypeStruct((columns, count * PLACES * seg), incident.dtype)
            for count in (clusters // 2, clusters - clusters // 2)
        ],
        [SMEM, VMEM],
        "pack",
        moved=3 * columns * width,
    )(position, incident)
    table = jnp.stack([block_slot, block_rank], axis=1)
    for stage in stages:
        table = double(table, stage)
    slots, ranks = table[:, 0], table[:, 1]
    wanted = owner * capacity + lax.broadcasted_iota(jnp.int32, (capacity, slots.shape[0]), 0)
    order = lax.broadcasted_iota(jnp.int32, (capacity, slots.shape[0]), 1)
    found = wanted == slots[None, :]
    feeding = jnp.max(jnp.where(found, order, -1), axis=1)
    used = jnp.sum(jnp.where(found, ranks[None, :], 0), axis=1)
    earlier = lax.broadcasted_iota(jnp.int32, (capacity, capacity), 1)
    earlier = earlier < lax.broadcasted_iota(jnp.int32, (capacity, capacity), 0)
    offset = jnp.sum(jnp.where(earlier, used[None, :], 0), axis=1)
    place = lax.broadcasted_iota(jnp.int32, (owners, slots.shape[0]), 0)
    held = (slots[None, :] >= place * capacity) & (slots[None, :] < (place + 1) * capacity)
    fullest = jnp.max(jnp.sum(jnp.where(held, ranks[None, :], 0), axis=1))
    tiles = sorted({-(-capacity * part // 10) for part in (5, 6, 7, 8, 10)})
    level = sum((fullest > count * rank_max).astype(jnp.int32) for count in tiles[:-1])
    squeezed = call(
        squeeze_body,
        jax.ShapeDtypeStruct(u_factors.shape, u_factors.dtype),
        [SMEM, SMEM, VMEM],
        "squeeze",
        moved=4 * u_factors.size,
        scratch=[pltpu.VMEM((capacity + 2, seg, rank_max), jnp.float32)],
    )(offset, used, u_factors)

    arrived = lax.optimization_barrier(
        (across(packed[0]), packed[1], v_near, v_far, squeezed, level)
    )

    def rest(count, x_low, high, v_near, v_far, squeezed):
        v_ends, v_middle = move(v_far, ends), move(v_factors, middle)
        x_high = across(high)
        target_factors = squeezed[:count]
        u_first, u_second = [
            move(part, far) for part in (target_factors[: count // 2], target_factors[count // 2 :])
        ]
        u_near = move(target_factors, near)
        partial, *sent = call(
            functools.partial(compress_body, seg),
            [
                jax.ShapeDtypeStruct((blocks, 2, padded, rank_max), jnp.float32),
                jax.ShapeDtypeStruct((blocks, padded, rank_max), jnp.bfloat16),
                jax.ShapeDtypeStruct((blocks, padded, rank_max), jnp.bfloat16),
            ],
            [SMEM, SMEM] + [VMEM] * 8,
            "compress",
            flops=4 * blocks * columns * seg * PLACES * rank_max,
            moved=3 * columns * width + 2 * PLACES * v_factors.size,
            scratch=[pltpu.VMEM((columns, width // 2), incident.dtype)],
        )(
            position, block_source, incident, x_low, x_high,
            v_factors, v_near, v_far, v_middle, v_ends,
        )
        received = jnp.stack([across(part) for part in sent], axis=1)
        u_side = across(after(target_factors, received))
        rank_index = lax.broadcasted_iota(jnp.int32, (blocks, 1, 1, rank_max), 3)
        rows = jnp.where(
            rank_index < block_rank[:, None, None, None],
            partial + received.astype(jnp.float32),
            0.0,
        ).astype(jnp.bfloat16)

        rounds, gathered = 1 + jnp.minimum(me, 0), after(rows, u_first)
        for stage in stages:
            other = lax.fori_loop(
                0, rounds, lambda _, array, stage=stage: swapped(array, stage), gathered
            )
            gathered = jnp.concatenate([gathered, other], axis=0)
        u_ends = [move(after(part, gathered), ends) for part in (u_first, u_second)]
        u_middle = move(after(target_factors, u_second, gathered), middle)
        slot_rows = call(
            land_body,
            jax.ShapeDtypeStruct((count, clusters, 2 * padded, rank_max), jnp.bfloat16),
            [SMEM, SMEM, SMEM, VMEM],
            "land",
            moved=2 * gathered.size * (1 + clusters),
        )(feeding, slot_target, offset, gathered)

        chunk = jax.ShapeDtypeStruct((columns, clusters * seg), jnp.bfloat16)
        own_parts, other_parts = [None] * PLACES, [None] * PLACES
        work = 4 * clusters * count * columns * seg * rank_max
        first = call(
            functools.partial(expand_own_body, seg, columns),
            jax.ShapeDtypeStruct((columns, 2 * clusters * seg), jnp.bfloat16),
            [SMEM] + [VMEM] * 3,
            "expand_own",
            flops=work,
            moved=4 * target_factors.size + 2 * slot_rows.size + 4 * columns * clusters * seg,
            scratch=[pltpu.VMEM((clusters, padded, seg), jnp.float32)],
        )(position, slot_rows, target_factors, u_side)
        finished = []
        for step, shards, choices in (
            (1, [u_near], [slice(0, 1)]),
            (2, [u_first, u_second], [slice(0, 2)]),
            (3, [u_middle, *u_ends], [slice(0, 1), slice(1, 3)]),
        ):
            if finished:
                slot_rows = after(slot_rows, own_parts[finished[-1]])
            if len(finished) == 2:
                slot_rows = after(slot_rows, first, other_parts[finished[0]])
            own, other = call(
                functools.partial(expand_body, seg, columns, choices),
                [chunk, chunk],
                [SMEM, VMEM] + [VMEM] * len(shards),
                "expand",
                flops=work,
                moved=2 * target_factors.size + 2 * slot_rows.size + 4 * columns * clusters * seg,
                scratch=[pltpu.VMEM((clusters, 2, padded, seg), jnp.float32)],
            )(position, slot_rows, *shards)
            own_parts[step], other_parts[step] = own, across(other)
            finished.append(step)
        return call(
            functools.partial(join_body, seg, clusters),
            jax.ShapeDtypeStruct((columns, width), jnp.bfloat16),
            [SMEM] + [VMEM] * (2 * PLACES - 1),
            "join",
            moved=4 * columns * width,
        )(position, first, *own_parts[1:], *other_parts[1:])

    return lax.switch(
        arrived[-1], [functools.partial(rest, count) for count in tiles], *arrived[:-1]
    )


def gathered_plan(
    incident, v_factors, u_factors, block_source, block_rank, block_slot, slot_target
):
    columns = incident.shape[0]
    blocks = v_factors.shape[0]
    rank_max = v_factors.shape[2]
    capacity = u_factors.shape[0]
    devices = lax.axis_size("clus")
    cluster_len = v_factors.shape[1] * lax.axis_size("rhs")
    local_clusters = incident.shape[1] // cluster_len
    per_peer = max(1, (2 * blocks + devices - 1) // devices)
    sources = jnp.take(incident.reshape(columns, local_clusters, cluster_len), block_source, axis=1)
    compressed = jnp.einsum(
        "cbr,brk->bck",
        sources,
        lax.all_gather(v_factors, "rhs", axis=1, tiled=True),
        preferred_element_type=jnp.float32,
    )
    rank_index = lax.broadcasted_iota(jnp.int32, (blocks, 1, rank_max), 2)
    compressed = jnp.where(rank_index < block_rank[:, None, None], compressed, 0.0).astype(
        jnp.bfloat16
    )
    target_dev = block_slot // capacity
    target_pos = block_slot % capacity
    later_index = lax.broadcasted_iota(jnp.int32, (blocks, blocks), 0)
    earlier_index = lax.broadcasted_iota(jnp.int32, (blocks, blocks), 1)
    same_target = target_dev[None, :] == target_dev[:, None]
    before = jnp.sum((same_target & (earlier_index < later_index)).astype(jnp.int32), axis=1)
    position = target_dev * per_peer + before
    places = lax.broadcasted_iota(jnp.int32, (blocks, devices * per_peer), 1)
    placed = position[:, None] == places
    outgoing = jnp.einsum(
        "bp,bck->pck", placed.astype(jnp.bfloat16), compressed, preferred_element_type=jnp.float32
    ).astype(jnp.bfloat16)
    labels = jnp.sum(jnp.where(placed, target_pos[:, None] + 1, 0), axis=0) - 1
    arrived, arrived_labels = (
        lax.all_to_all(outgoing, "clus", split_axis=0, concat_axis=0, tiled=True),
        lax.all_to_all(labels, "clus", split_axis=0, concat_axis=0, tiled=True),
    )
    slot_ids = lax.broadcasted_iota(jnp.int32, (devices * per_peer, capacity), 1)
    landing = (arrived_labels[:, None] == slot_ids).astype(jnp.bfloat16)
    slot_rows = jnp.einsum(
        "pj,pck->jck", landing, arrived, preferred_element_type=jnp.float32
    ).astype(jnp.bfloat16)
    cluster_ids = lax.broadcasted_iota(jnp.int32, (capacity, local_clusters), 1)
    owners = (slot_target[:, None] == cluster_ids).astype(jnp.float32)
    products = jnp.einsum(
        "jck,jrk->jcr",
        slot_rows,
        lax.all_gather(u_factors, "rhs", axis=1, tiled=True),
        preferred_element_type=jnp.float32,
    )
    summed = jnp.einsum("jt,jcr->ctr", owners, products, precision=lax.Precision.HIGHEST)
    return summed.reshape(columns, local_clusters * cluster_len).astype(jnp.bfloat16)


def local(incident, v_factors, *rest):
    owners = lax.axis_size("clus")
    fits = (
        lax.axis_size("rhs") == 2 * PLACES
        and v_factors.shape[1] % 128 == 0
        and owners > 1
        and incident.shape[1] > v_factors.shape[1] * 2 * PLACES
        and owners & (owners - 1) == 0
    )
    return (paired if fits else gathered_plan)(incident, v_factors, *rest)


def solution(mesh):
    placed = (
        P("rhs", "clus"),
        P("clus", "rhs", None),
        P("clus", "rhs", None),
        P("clus"),
        P("clus"),
        P("clus"),
        P("clus"),
    )
    return jax.shard_map(
        local, mesh=mesh, in_specs=placed, out_specs=P("rhs", "clus"), check_vma=False
    )
```

```python
import functools

import jax
import jax.numpy as jnp
from jax import lax
from jax.experimental import pallas as pl
from jax.experimental.pallas import tpu as pltpu
from jax.sharding import PartitionSpec as P

VMEM = pl.BlockSpec(memory_space=pltpu.VMEM)
SMEM = pl.BlockSpec(memory_space=pltpu.SMEM)
LIMIT = 10 * 1024 * 1024


def call(body, out_shape, in_specs, name, flops=0, moved=0, scratch=()):
    out_specs = [VMEM] * len(out_shape) if isinstance(out_shape, list) else VMEM
    return pl.pallas_call(
        body,
        out_shape=out_shape,
        in_specs=in_specs,
        out_specs=out_specs,
        scratch_shapes=list(scratch),
        compiler_params=pltpu.CompilerParams(vmem_limit_bytes=LIMIT),
        cost_estimate=pl.CostEstimate(flops=flops, bytes_accessed=moved, transcendentals=0),
        name=name,
    )


def pack_body(seg, pos_ref, x_ref, *out_refs):
    half, piece = 1 - pos_ref[0], 0
    for out_ref in out_refs:
        for place in range(0, out_ref.shape[1], seg):
            start = pl.multiple_of((2 * piece + half) * seg, seg)
            out_ref[:, place : place + seg] = x_ref[:, pl.ds(start, seg)]
            piece += 1


def compress_body(seg, pos_ref, source_ref, x_ref, xl_ref, xh_ref, *refs):
    v0, v1, v2, v3, v4, out_ref, send_ref, xn_ref = refs
    half, mine = pos_ref[0], pos_ref[1]
    columns = x_ref.shape[0]
    xn_ref[:, : xl_ref.shape[1]] = xl_ref[...]
    xn_ref[:, xl_ref.shape[1] :] = xh_ref[...]
    out_ref[...] = jnp.zeros_like(out_ref)

    def run(shards):
        for block in range(out_ref.shape[0]):
            source = source_ref[block]
            own = other = 0.0
            for step, shard in enumerate(shards):
                piece = source * PLACES + jnp.bitwise_xor(mine, step)
                here = pl.multiple_of((piece * 2 + half) * seg, seg)
                there = pl.multiple_of(piece * seg, seg)
                rows = shard[block]
                own += jnp.dot(x_ref[:, pl.ds(here, seg)], rows, preferred_element_type=jnp.float32)
                other += jnp.dot(
                    xn_ref[:, pl.ds(there, seg)], rows, preferred_element_type=jnp.float32
                )
            out_ref[block, half, :columns] = own
            out_ref[block, 1 - half, :columns] = other

    inner = (mine == 1) | (mine == 2)

    @pl.when(inner)
    def _():
        run((v0, v1, v2, v3))

    @pl.when(jnp.logical_not(inner))
    def _():
        run((v0, v1, v2, v4))

    send_ref[...] = out_ref[...].astype(send_ref.dtype)


def place_columns(value, offset, store):
    width = value.shape[-1]
    shift = lax.rem(offset, width)
    turned = pltpu.roll(value, shift, value.ndim - 1)
    lane = lax.broadcasted_iota(jnp.int32, value.shape, value.ndim - 1)
    store(offset // width, jnp.where(lane >= shift, turned, 0.0))
    store(offset // width + 1, jnp.where(lane < shift, turned, 0.0))


def squeeze_body(offset_ref, used_ref, u_ref, out_ref, acc):
    acc[...] = jnp.zeros_like(acc)
    for slot in range(u_ref.shape[0]):
        value = u_ref[slot].astype(jnp.float32)
        lane = lax.broadcasted_iota(jnp.int32, value.shape, 1)

        def store(tile, part):
            acc[tile] += part

        place_columns(jnp.where(lane < used_ref[slot], value, 0.0), offset_ref[slot], store)
    out_ref[...] = acc[: out_ref.shape[0]].astype(out_ref.dtype)


def land_body(index_ref, target_ref, offset_ref, comp_ref, rows_ref):
    rows_ref[...] = jnp.zeros_like(rows_ref)
    last = rows_ref.shape[0] - 1
    for slot in range(index_ref.shape[0]):
        block, target = index_ref[slot], target_ref[slot]
        value = comp_ref[jnp.maximum(block, 0)].astype(jnp.float32)
        value = jnp.where(block >= 0, value, 0.0).reshape(rows_ref.shape[2:])

        def store(tile, part):
            rows_ref[jnp.minimum(tile, last), target] += part.astype(rows_ref.dtype)

        place_columns(value, offset_ref[slot], store)


def lined_up(ref, rows):
    return jnp.concatenate([ref[tile].reshape(rows, ref.shape[-1]) for tile in range(ref.shape[0])], axis=1)


def expand_body(seg, columns, pos_ref, rows_ref, *refs):
    own_ref, other_ref, acc = refs[-3:]
    half, mine = pos_ref[0], pos_ref[1]
    clusters, sides, padded = acc.shape[:3]

    def run(shard):
        product = lax.dot_general(
            lined_up(rows_ref, clusters * sides * padded),
            lined_up(shard, seg),
            (((1,), (1,)), ((), ())),
            preferred_element_type=jnp.float32,
        )
        acc[...] = product.reshape(acc.shape)

    if len(refs) == 4:
        run(refs[0])
    else:
        inner = (mine == 1) | (mine == 2)

        @pl.when(inner)
        def _():
            run(refs[0])

        @pl.when(jnp.logical_not(inner))
        def _():
            run(refs[1])

    for target in range(clusters):
        span = slice(target * seg, (target + 1) * seg)
        own_ref[:, span] = acc[target, half, :columns].astype(own_ref.dtype)
        other_ref[:, span] = acc[target, 1 - half, :columns].astype(other_ref.dtype)


def expand_own_body(seg, columns, pos_ref, rows_ref, u_ref, side_ref, out_ref, acc):
    half = pos_ref[0]
    clusters, padded = acc.shape[:2]
    start = pl.multiple_of(half * padded, padded)
    tiles = [
        rows_ref[tile, :, pl.ds(start, padded)].reshape(clusters * padded, rows_ref.shape[3])
        for tile in range(rows_ref.shape[0])
    ]
    rows = jnp.concatenate(tiles, axis=1)
    for shard, place in ((u_ref, half), (side_ref, 1 - half)):
        product = lax.dot_general(
            rows,
            lined_up(shard, seg),
            (((1,), (1,)), ((), ())),
            preferred_element_type=jnp.float32,
        )
        acc[...] = product.reshape(acc.shape)
        for target in range(clusters):
            start = pl.multiple_of((2 * target + place) * seg, seg)
            out_ref[:, pl.ds(start, seg)] = acc[target, :columns].astype(out_ref.dtype)


def join_body(seg, clusters, pos_ref, first_ref, *refs):
    out_ref = refs[-1]
    half, mine = pos_ref[0], pos_ref[1]
    for target in range(clusters):
        start = pl.multiple_of((target * PLACES + mine) * 2 * seg, 2 * seg)
        span = slice(2 * target * seg, 2 * (target + 1) * seg)
        out_ref[:, pl.ds(start, 2 * seg)] = first_ref[:, span]
    for step in range(1, PLACES):
        place = jnp.bitwise_xor(mine, step)
        for target in range(clusters):
            span = slice(target * seg, (target + 1) * seg)
            base = (target * PLACES + place) * 2
            here = pl.multiple_of((base + half) * seg, seg)
            there = pl.multiple_of((base + 1 - half) * seg, seg)
            out_ref[:, pl.ds(here, seg)] = refs[step - 1][:, span]
            out_ref[:, pl.ds(there, seg)] = refs[PLACES + step - 2][:, span]


def after(value, *first):
    return lax.optimization_barrier((value, *first))[0]


PLACES = 4


def paired(incident, v_factors, u_factors, block_source, block_rank, block_slot, slot_target):
    columns, width = incident.shape
    padded = -(-columns // 16) * 16
    blocks, seg, rank_max = v_factors.shape
    capacity = u_factors.shape[0]
    owners = lax.axis_size("clus")
    clusters = width // (seg * 2 * PLACES)
    me, owner = lax.axis_index("rhs"), lax.axis_index("clus")
    position = jnp.stack([me % 2, me // 2]).astype(jnp.int32)

    def move(array, pairs):
        return lax.ppermute(array, "rhs", [(2 * a + i, 2 * b + i) for a, b in pairs for i in (0, 1)])

    def across(array):
        return lax.ppermute(array, "rhs", [(p, p ^ 1) for p in range(2 * PLACES)])

    far = [(p, p ^ 2) for p in range(PLACES)]
    near = [(p, p ^ 1) for p in range(PLACES)]
    middle = [(1, 2), (2, 1)]
    ends = [(1, 0), (2, 3)]

    stages = [1 << bit for bit in reversed(range((owners - 1).bit_length()))]

    def swapped(array, stage):
        return lax.ppermute(array, "clus", [(p, p ^ stage) for p in range(owners)])

    def double(array, stage):
        return jnp.concatenate([array, swapped(array, stage)], axis=0)

    v_far, v_near = move(v_factors, far), move(v_factors, near)
    packed = call(
        functools.partial(pack_body, seg),
        [
            jax.ShapeDtypeStruct((columns, count * PLACES * seg), incident.dtype)
            for count in (clusters // 2, clusters - clusters // 2)
        ],
        [SMEM, VMEM],
        "pack",
        moved=3 * columns * width,
    )(position, incident)
    table = jnp.stack([block_slot, block_rank], axis=1)
    for stage in stages:
        table = double(table, stage)
    slots, ranks = table[:, 0], table[:, 1]
    wanted = owner * capacity + lax.broadcasted_iota(jnp.int32, (capacity, slots.shape[0]), 0)
    order = lax.broadcasted_iota(jnp.int32, (capacity, slots.shape[0]), 1)
    found = wanted == slots[None, :]
    feeding = jnp.max(jnp.where(found, order, -1), axis=1)
    used = jnp.sum(jnp.where(found, ranks[None, :], 0), axis=1)
    earlier = lax.broadcasted_iota(jnp.int32, (capacity, capacity), 1)
    earlier = earlier < lax.broadcasted_iota(jnp.int32, (capacity, capacity), 0)
    offset = jnp.sum(jnp.where(earlier, used[None, :], 0), axis=1)
    place = lax.broadcasted_iota(jnp.int32, (owners, slots.shape[0]), 0)
    held = (slots[None, :] >= place * capacity) & (slots[None, :] < (place + 1) * capacity)
    fullest = jnp.max(jnp.sum(jnp.where(held, ranks[None, :], 0), axis=1))
    tiles = sorted({-(-capacity * part // 10) for part in (5, 6, 7, 8, 10)})
    level = sum((fullest > count * rank_max).astype(jnp.int32) for count in tiles[:-1])
    squeezed = call(
        squeeze_body,
        jax.ShapeDtypeStruct(u_factors.shape, u_factors.dtype),
        [SMEM, SMEM, VMEM],
        "squeeze",
        moved=4 * u_factors.size,
        scratch=[pltpu.VMEM((capacity + 2, seg, rank_max), jnp.float32)],
    )(offset, used, u_factors)

    x_low, x_high = [across(part) for part in packed]
    v_ends = move(after(v_far, *packed), ends)
    v_middle = move(v_factors, middle)
    arrived = lax.optimization_barrier(
        (x_low, x_high, v_near, v_far, v_middle, v_ends, squeezed, level)
    )

    def rest(count, x_low, x_high, v_near, v_far, v_middle, v_ends, squeezed):
        target_factors = squeezed[:count]
        u_far, u_near = move(target_factors, far), move(target_factors, near)
        partial, sent = call(
            functools.partial(compress_body, seg),
            [
                jax.ShapeDtypeStruct((blocks, 2, padded, rank_max), jnp.float32),
                jax.ShapeDtypeStruct((blocks, 2, padded, rank_max), jnp.bfloat16),
            ],
            [SMEM, SMEM] + [VMEM] * 8,
            "compress",
            flops=4 * blocks * columns * seg * PLACES * rank_max,
            moved=3 * columns * width + 2 * PLACES * v_factors.size,
            scratch=[pltpu.VMEM((columns, width // 2), incident.dtype)],
        )(
            position, block_source, incident, x_low, x_high,
            v_factors, v_near, v_far, v_middle, v_ends,
        )
        received = across(sent)
        u_side = across(after(target_factors, received))
        rank_index = lax.broadcasted_iota(jnp.int32, (blocks, 1, 1, rank_max), 3)
        rows = jnp.where(
            rank_index < block_rank[:, None, None, None],
            partial + received.astype(jnp.float32),
            0.0,
        ).astype(jnp.bfloat16)

        rounds, gathered = 1 + jnp.minimum(me, 0), rows
        for stage in stages:
            other = lax.fori_loop(
                0, rounds, lambda _, array, stage=stage: swapped(array, stage), gathered
            )
            gathered = jnp.concatenate([gathered, other], axis=0)
        u_ends = move(after(u_far, gathered), ends)
        u_middle = move(after(target_factors, u_far, gathered), middle)
        slot_rows = call(
            land_body,
            jax.ShapeDtypeStruct((count, clusters, 2 * padded, rank_max), jnp.bfloat16),
            [SMEM, SMEM, SMEM, VMEM],
            "land",
            moved=2 * gathered.size * (1 + clusters),
        )(feeding, slot_target, offset, gathered)

        chunk = jax.ShapeDtypeStruct((columns, clusters * seg), jnp.bfloat16)
        own_parts, other_parts = [None] * PLACES, [None] * PLACES
        work = 4 * clusters * count * columns * seg * rank_max
        first = call(
            functools.partial(expand_own_body, seg, columns),
            jax.ShapeDtypeStruct((columns, 2 * clusters * seg), jnp.bfloat16),
            [SMEM] + [VMEM] * 3,
            "expand_own",
            flops=work,
            moved=4 * target_factors.size + 2 * slot_rows.size + 4 * columns * clusters * seg,
            scratch=[pltpu.VMEM((clusters, padded, seg), jnp.float32)],
        )(position, slot_rows, target_factors, u_side)
        finished = []
        for step, shards in ((1, [u_near]), (2, [u_far]), (3, [u_middle, u_ends])):
            if finished:
                slot_rows = after(slot_rows, own_parts[finished[-1]])
            if len(finished) == 2:
                slot_rows = after(slot_rows, first, other_parts[finished[0]])
            own, other = call(
                functools.partial(expand_body, seg, columns),
                [chunk, chunk],
                [SMEM, VMEM] + [VMEM] * len(shards),
                "expand",
                flops=work,
                moved=2 * target_factors.size + 2 * slot_rows.size + 4 * columns * clusters * seg,
                scratch=[pltpu.VMEM((clusters, 2, padded, seg), jnp.float32)],
            )(position, slot_rows, *shards)
            own_parts[step], other_parts[step] = own, across(other)
            finished.append(step)
        return call(
            functools.partial(join_body, seg, clusters),
            jax.ShapeDtypeStruct((columns, width), jnp.bfloat16),
            [SMEM] + [VMEM] * (2 * PLACES - 1),
            "join",
            moved=4 * columns * width,
        )(position, first, *own_parts[1:], *other_parts[1:])

    return lax.switch(
        arrived[-1], [functools.partial(rest, count) for count in tiles], *arrived[:-1]
    )


def gathered_plan(
    incident, v_factors, u_factors, block_source, block_rank, block_slot, slot_target
):
    columns = incident.shape[0]
    blocks = v_factors.shape[0]
    rank_max = v_factors.shape[2]
    capacity = u_factors.shape[0]
    devices = lax.axis_size("clus")
    cluster_len = v_factors.shape[1] * lax.axis_size("rhs")
    local_clusters = incident.shape[1] // cluster_len
    per_peer = max(1, (2 * blocks + devices - 1) // devices)
    sources = jnp.take(incident.reshape(columns, local_clusters, cluster_len), block_source, axis=1)
    compressed = jnp.einsum(
        "cbr,brk->bck",
        sources,
        lax.all_gather(v_factors, "rhs", axis=1, tiled=True),
        preferred_element_type=jnp.float32,
    )
    rank_index = lax.broadcasted_iota(jnp.int32, (blocks, 1, rank_max), 2)
    compressed = jnp.where(rank_index < block_rank[:, None, None], compressed, 0.0).astype(
        jnp.bfloat16
    )
    target_dev = block_slot // capacity
    target_pos = block_slot % capacity
    later_index = lax.broadcasted_iota(jnp.int32, (blocks, blocks), 0)
    earlier_index = lax.broadcasted_iota(jnp.int32, (blocks, blocks), 1)
    same_target = target_dev[None, :] == target_dev[:, None]
    before = jnp.sum((same_target & (earlier_index < later_index)).astype(jnp.int32), axis=1)
    position = target_dev * per_peer + before
    places = lax.broadcasted_iota(jnp.int32, (blocks, devices * per_peer), 1)
    placed = position[:, None] == places
    outgoing = jnp.einsum(
        "bp,bck->pck", placed.astype(jnp.bfloat16), compressed, preferred_element_type=jnp.float32
    ).astype(jnp.bfloat16)
    labels = jnp.sum(jnp.where(placed, target_pos[:, None] + 1, 0), axis=0) - 1
    arrived, arrived_labels = (
        lax.all_to_all(outgoing, "clus", split_axis=0, concat_axis=0, tiled=True),
        lax.all_to_all(labels, "clus", split_axis=0, concat_axis=0, tiled=True),
    )
    slot_ids = lax.broadcasted_iota(jnp.int32, (devices * per_peer, capacity), 1)
    landing = (arrived_labels[:, None] == slot_ids).astype(jnp.bfloat16)
    slot_rows = jnp.einsum(
        "pj,pck->jck", landing, arrived, preferred_element_type=jnp.float32
    ).astype(jnp.bfloat16)
    cluster_ids = lax.broadcasted_iota(jnp.int32, (capacity, local_clusters), 1)
    owners = (slot_target[:, None] == cluster_ids).astype(jnp.float32)
    products = jnp.einsum(
        "jck,jrk->jcr",
        slot_rows,
        lax.all_gather(u_factors, "rhs", axis=1, tiled=True),
        preferred_element_type=jnp.float32,
    )
    summed = jnp.einsum("jt,jcr->ctr", owners, products, precision=lax.Precision.HIGHEST)
    return summed.reshape(columns, local_clusters * cluster_len).astype(jnp.bfloat16)


def local(incident, v_factors, *rest):
    owners = lax.axis_size("clus")
    fits = (
        lax.axis_size("rhs") == 2 * PLACES
        and v_factors.shape[1] % 128 == 0
        and owners > 1
        and incident.shape[1] > v_factors.shape[1] * 2 * PLACES
        and owners & (owners - 1) == 0
    )
    return (paired if fits else gathered_plan)(incident, v_factors, *rest)


def solution(mesh):
    placed = (
        P("rhs", "clus"),
        P("clus", "rhs", None),
        P("clus", "rhs", None),
        P("clus"),
        P("clus"),
        P("clus"),
        P("clus"),
    )
    return jax.shard_map(
        local, mesh=mesh, in_specs=placed, out_specs=P("rhs", "clus"), check_vma=False
    )
```

```python
import functools

import jax
import jax.numpy as jnp
from jax import lax
from jax.experimental import pallas as pl
from jax.experimental.pallas import tpu as pltpu
from jax.sharding import PartitionSpec as P

VMEM = pl.BlockSpec(memory_space=pltpu.VMEM)
SMEM = pl.BlockSpec(memory_space=pltpu.SMEM)
LIMIT = 10 * 1024 * 1024


def call(body, out_shape, in_specs, name, flops=0, moved=0, scratch=()):
    out_specs = [VMEM] * len(out_shape) if isinstance(out_shape, list) else VMEM
    return pl.pallas_call(
        body,
        out_shape=out_shape,
        in_specs=in_specs,
        out_specs=out_specs,
        scratch_shapes=list(scratch),
        compiler_params=pltpu.CompilerParams(vmem_limit_bytes=LIMIT),
        cost_estimate=pl.CostEstimate(flops=flops, bytes_accessed=moved, transcendentals=0),
        name=name,
    )


def pack_body(seg, pos_ref, x_ref, *out_refs):
    half, piece = 1 - pos_ref[0], 0
    for out_ref in out_refs:
        for place in range(0, out_ref.shape[1], seg):
            start = pl.multiple_of((2 * piece + half) * seg, seg)
            out_ref[:, place : place + seg] = x_ref[:, pl.ds(start, seg)]
            piece += 1


def compress_body(seg, pos_ref, source_ref, x_ref, xl_ref, xh_ref, *refs):
    v0, v1, v2, v3, v4, out_ref, send_ref, xn_ref = refs
    half, mine = pos_ref[0], pos_ref[1]
    columns = x_ref.shape[0]
    xn_ref[:, : xl_ref.shape[1]] = xl_ref[...]
    xn_ref[:, xl_ref.shape[1] :] = xh_ref[...]
    out_ref[...] = jnp.zeros_like(out_ref)

    def run(shards):
        for block in range(out_ref.shape[0]):
            source = source_ref[block]
            own = other = 0.0
            for step, shard in enumerate(shards):
                piece = source * PLACES + jnp.bitwise_xor(mine, step)
                here = pl.multiple_of((piece * 2 + half) * seg, seg)
                there = pl.multiple_of(piece * seg, seg)
                rows = shard[block]
                own += jnp.dot(x_ref[:, pl.ds(here, seg)], rows, preferred_element_type=jnp.float32)
                other += jnp.dot(
                    xn_ref[:, pl.ds(there, seg)], rows, preferred_element_type=jnp.float32
                )
            out_ref[block, half, :columns] = own
            out_ref[block, 1 - half, :columns] = other

    inner = (mine == 1) | (mine == 2)

    @pl.when(inner)
    def _():
        run((v0, v1, v2, v3))

    @pl.when(jnp.logical_not(inner))
    def _():
        run((v0, v1, v2, v4))

    send_ref[...] = out_ref[...].astype(send_ref.dtype)


def place_columns(value, offset, store):
    width = value.shape[-1]
    shift = lax.rem(offset, width)
    turned = pltpu.roll(value, shift, value.ndim - 1)
    lane = lax.broadcasted_iota(jnp.int32, value.shape, value.ndim - 1)
    store(offset // width, jnp.where(lane >= shift, turned, 0.0))
    store(offset // width + 1, jnp.where(lane < shift, turned, 0.0))


def squeeze_body(offset_ref, used_ref, u_ref, *refs):
    *out_refs, acc = refs
    acc[...] = jnp.zeros_like(acc)
    for slot in range(u_ref.shape[0]):
        value = u_ref[slot].astype(jnp.float32)
        lane = lax.broadcasted_iota(jnp.int32, value.shape, 1)

        def store(tile, part):
            acc[tile] += part

        place_columns(jnp.where(lane < used_ref[slot], value, 0.0), offset_ref[slot], store)
    packed = acc[...].astype(u_ref.dtype)
    for out_ref in out_refs:
        out_ref[...] = packed[: out_ref.shape[0]]


def land_body(index_ref, target_ref, offset_ref, comp_ref, rows_ref):
    rows_ref[...] = jnp.zeros_like(rows_ref)
    last = rows_ref.shape[0] - 1
    for slot in range(index_ref.shape[0]):
        block, target = index_ref[slot], target_ref[slot]
        value = comp_ref[jnp.maximum(block, 0)].astype(jnp.float32)
        value = jnp.where(block >= 0, value, 0.0).reshape(rows_ref.shape[2:])

        def store(tile, part):
            rows_ref[jnp.minimum(tile, last), target] += part.astype(rows_ref.dtype)

        place_columns(value, offset_ref[slot], store)


def lined_up(ref, rows):
    return jnp.concatenate([ref[tile].reshape(rows, ref.shape[-1]) for tile in range(ref.shape[0])], axis=1)


def expand_body(seg, columns, pos_ref, rows_ref, *refs):
    own_ref, other_ref, acc = refs[-3:]
    half, mine = pos_ref[0], pos_ref[1]
    clusters, sides, padded = acc.shape[:3]

    def run(shard):
        product = lax.dot_general(
            lined_up(rows_ref, clusters * sides * padded),
            lined_up(shard, seg),
            (((1,), (1,)), ((), ())),
            preferred_element_type=jnp.float32,
        )
        acc[...] = product.reshape(acc.shape)

    if len(refs) == 4:
        run(refs[0])
    else:
        inner = (mine == 1) | (mine == 2)

        @pl.when(inner)
        def _():
            run(refs[0])

        @pl.when(jnp.logical_not(inner))
        def _():
            run(refs[1])

    for target in range(clusters):
        span = slice(target * seg, (target + 1) * seg)
        own_ref[:, span] = acc[target, half, :columns].astype(own_ref.dtype)
        other_ref[:, span] = acc[target, 1 - half, :columns].astype(other_ref.dtype)


def expand_own_body(seg, columns, pos_ref, rows_ref, u_ref, side_ref, out_ref, acc):
    half = pos_ref[0]
    clusters, padded = acc.shape[:2]
    start = pl.multiple_of(half * padded, padded)
    tiles = [
        rows_ref[tile, :, pl.ds(start, padded)].reshape(clusters * padded, rows_ref.shape[3])
        for tile in range(rows_ref.shape[0])
    ]
    rows = jnp.concatenate(tiles, axis=1)
    for shard, place in ((u_ref, half), (side_ref, 1 - half)):
        product = lax.dot_general(
            rows,
            lined_up(shard, seg),
            (((1,), (1,)), ((), ())),
            preferred_element_type=jnp.float32,
        )
        acc[...] = product.reshape(acc.shape)
        for target in range(clusters):
            start = pl.multiple_of((2 * target + place) * seg, seg)
            out_ref[:, pl.ds(start, seg)] = acc[target, :columns].astype(out_ref.dtype)


def join_body(seg, clusters, pos_ref, first_ref, *refs):
    out_ref = refs[-1]
    half, mine = pos_ref[0], pos_ref[1]
    for target in range(clusters):
        start = pl.multiple_of((target * PLACES + mine) * 2 * seg, 2 * seg)
        span = slice(2 * target * seg, 2 * (target + 1) * seg)
        out_ref[:, pl.ds(start, 2 * seg)] = first_ref[:, span]
    for step in range(1, PLACES):
        place = jnp.bitwise_xor(mine, step)
        for target in range(clusters):
            span = slice(target * seg, (target + 1) * seg)
            base = (target * PLACES + place) * 2
            here = pl.multiple_of((base + half) * seg, seg)
            there = pl.multiple_of((base + 1 - half) * seg, seg)
            out_ref[:, pl.ds(here, seg)] = refs[step - 1][:, span]
            out_ref[:, pl.ds(there, seg)] = refs[PLACES + step - 2][:, span]


def after(value, *first):
    return lax.optimization_barrier((value, *first))[0]


PLACES = 4


def paired(incident, v_factors, u_factors, block_source, block_rank, block_slot, slot_target):
    columns, width = incident.shape
    padded = -(-columns // 16) * 16
    blocks, seg, rank_max = v_factors.shape
    capacity = u_factors.shape[0]
    owners = lax.axis_size("clus")
    clusters = width // (seg * 2 * PLACES)
    me, owner = lax.axis_index("rhs"), lax.axis_index("clus")
    position = jnp.stack([me % 2, me // 2]).astype(jnp.int32)

    def move(array, pairs):
        return lax.ppermute(array, "rhs", [(2 * a + i, 2 * b + i) for a, b in pairs for i in (0, 1)])

    def across(array):
        return lax.ppermute(array, "rhs", [(p, p ^ 1) for p in range(2 * PLACES)])

    far = [(p, p ^ 2) for p in range(PLACES)]
    near = [(p, p ^ 1) for p in range(PLACES)]
    middle = [(1, 2), (2, 1)]
    ends = [(1, 0), (2, 3)]

    stages = [1 << bit for bit in reversed(range((owners - 1).bit_length()))]

    def swapped(array, stage):
        return lax.ppermute(array, "clus", [(p, p ^ stage) for p in range(owners)])

    def double(array, stage):
        return jnp.concatenate([array, swapped(array, stage)], axis=0)

    v_far, v_near = move(v_factors, far), move(v_factors, near)
    packed = call(
        functools.partial(pack_body, seg),
        [
            jax.ShapeDtypeStruct((columns, count * PLACES * seg), incident.dtype)
            for count in (clusters // 2, clusters - clusters // 2)
        ],
        [SMEM, VMEM],
        "pack",
        moved=3 * columns * width,
    )(position, incident)
    table = jnp.stack([block_slot, block_rank], axis=1)
    for stage in stages:
        table = double(table, stage)
    slots, ranks = table[:, 0], table[:, 1]
    wanted = owner * capacity + lax.broadcasted_iota(jnp.int32, (capacity, slots.shape[0]), 0)
    order = lax.broadcasted_iota(jnp.int32, (capacity, slots.shape[0]), 1)
    found = wanted == slots[None, :]
    feeding = jnp.max(jnp.where(found, order, -1), axis=1)
    used = jnp.sum(jnp.where(found, ranks[None, :], 0), axis=1)
    earlier = lax.broadcasted_iota(jnp.int32, (capacity, capacity), 1)
    earlier = earlier < lax.broadcasted_iota(jnp.int32, (capacity, capacity), 0)
    offset = jnp.sum(jnp.where(earlier, used[None, :], 0), axis=1)
    place = lax.broadcasted_iota(jnp.int32, (owners, slots.shape[0]), 0)
    held = (slots[None, :] >= place * capacity) & (slots[None, :] < (place + 1) * capacity)
    fullest = jnp.max(jnp.sum(jnp.where(held, ranks[None, :], 0), axis=1))
    tiles = sorted({-(-capacity * part // 10) for part in (5, 6, 7, 8, 10)})
    level = sum((fullest > count * rank_max).astype(jnp.int32) for count in tiles[:-1])
    squeezed = call(
        squeeze_body,
        [jax.ShapeDtypeStruct((count, seg, rank_max), u_factors.dtype) for count in tiles],
        [SMEM, SMEM, VMEM],
        "squeeze",
        moved=4 * u_factors.size,
        scratch=[pltpu.VMEM((capacity + 2, seg, rank_max), jnp.float32)],
    )(offset, used, u_factors)

    x_low, x_high = [across(part) for part in packed]
    v_ends = move(after(v_far, *packed), ends)
    v_middle = move(v_factors, middle)
    arrived = lax.optimization_barrier(
        (x_low, x_high, v_near, v_far, v_middle, v_ends, squeezed, level)
    )

    def rest(count, x_low, x_high, v_near, v_far, v_middle, v_ends, squeezed):
        target_factors = squeezed[tiles.index(count)]
        u_far, u_near = move(target_factors, far), move(target_factors, near)
        partial, sent = call(
            functools.partial(compress_body, seg),
            [
                jax.ShapeDtypeStruct((blocks, 2, padded, rank_max), jnp.float32),
                jax.ShapeDtypeStruct((blocks, 2, padded, rank_max), jnp.bfloat16),
            ],
            [SMEM, SMEM] + [VMEM] * 8,
            "compress",
            flops=4 * blocks * columns * seg * PLACES * rank_max,
            moved=3 * columns * width + 2 * PLACES * v_factors.size,
            scratch=[pltpu.VMEM((columns, width // 2), incident.dtype)],
        )(
            position, block_source, incident, x_low, x_high,
            v_factors, v_near, v_far, v_middle, v_ends,
        )
        received = across(sent)
        u_side = across(after(target_factors, received))
        rank_index = lax.broadcasted_iota(jnp.int32, (blocks, 1, 1, rank_max), 3)
        rows = jnp.where(
            rank_index < block_rank[:, None, None, None],
            partial + received.astype(jnp.float32),
            0.0,
        ).astype(jnp.bfloat16)

        rounds, gathered = 1 + jnp.minimum(me, 0), rows
        for stage in stages:
            other = lax.fori_loop(
                0, rounds, lambda _, array, stage=stage: swapped(array, stage), gathered
            )
            gathered = jnp.concatenate([gathered, other], axis=0)
        slot_rows = call(
            land_body,
            jax.ShapeDtypeStruct((count, clusters, 2 * padded, rank_max), jnp.bfloat16),
            [SMEM, SMEM, SMEM, VMEM],
            "land",
            moved=2 * gathered.size * (1 + clusters),
        )(feeding, slot_target, offset, gathered)

        chunk = jax.ShapeDtypeStruct((columns, clusters * seg), jnp.bfloat16)
        own_parts, other_parts = [None] * PLACES, [None] * PLACES
        work = 4 * clusters * count * columns * seg * rank_max
        first = call(
            functools.partial(expand_own_body, seg, columns),
            jax.ShapeDtypeStruct((columns, 2 * clusters * seg), jnp.bfloat16),
            [SMEM] + [VMEM] * 3,
            "expand_own",
            flops=work,
            moved=4 * target_factors.size + 2 * slot_rows.size + 4 * columns * clusters * seg,
            scratch=[pltpu.VMEM((clusters, padded, seg), jnp.float32)],
        )(position, slot_rows, target_factors, u_side)
        finished = []
        for step in range(1, PLACES):
            if step == 2:
                u_far = after(u_far, own_parts[1])
                u_ends = move(u_far, ends)
                u_middle = move(after(target_factors, u_far), middle)
            shards = [u_near] if step == 1 else [u_far] if step == 2 else [u_middle, u_ends]
            if finished:
                slot_rows = after(slot_rows, own_parts[finished[-1]])
            if len(finished) == 2:
                slot_rows = after(slot_rows, first, other_parts[finished[0]])
            own, other = call(
                functools.partial(expand_body, seg, columns),
                [chunk, chunk],
                [SMEM, VMEM] + [VMEM] * len(shards),
                "expand",
                flops=work,
                moved=2 * target_factors.size + 2 * slot_rows.size + 4 * columns * clusters * seg,
                scratch=[pltpu.VMEM((clusters, 2, padded, seg), jnp.float32)],
            )(position, slot_rows, *shards)
            own_parts[step], other_parts[step] = own, across(other)
            finished.append(step)
        return call(
            functools.partial(join_body, seg, clusters),
            jax.ShapeDtypeStruct((columns, width), jnp.bfloat16),
            [SMEM] + [VMEM] * (2 * PLACES - 1),
            "join",
            moved=4 * columns * width,
        )(position, first, *own_parts[1:], *other_parts[1:])

    return lax.switch(
        arrived[-1], [functools.partial(rest, count) for count in tiles], *arrived[:-1]
    )


def gathered_plan(
    incident, v_factors, u_factors, block_source, block_rank, block_slot, slot_target
):
    columns = incident.shape[0]
    blocks = v_factors.shape[0]
    rank_max = v_factors.shape[2]
    capacity = u_factors.shape[0]
    devices = lax.axis_size("clus")
    cluster_len = v_factors.shape[1] * lax.axis_size("rhs")
    local_clusters = incident.shape[1] // cluster_len
    per_peer = max(1, (2 * blocks + devices - 1) // devices)
    sources = jnp.take(incident.reshape(columns, local_clusters, cluster_len), block_source, axis=1)
    compressed = jnp.einsum(
        "cbr,brk->bck",
        sources,
        lax.all_gather(v_factors, "rhs", axis=1, tiled=True),
        preferred_element_type=jnp.float32,
    )
    rank_index = lax.broadcasted_iota(jnp.int32, (blocks, 1, rank_max), 2)
    compressed = jnp.where(rank_index < block_rank[:, None, None], compressed, 0.0).astype(
        jnp.bfloat16
    )
    target_dev = block_slot // capacity
    target_pos = block_slot % capacity
    later_index = lax.broadcasted_iota(jnp.int32, (blocks, blocks), 0)
    earlier_index = lax.broadcasted_iota(jnp.int32, (blocks, blocks), 1)
    same_target = target_dev[None, :] == target_dev[:, None]
    before = jnp.sum((same_target & (earlier_index < later_index)).astype(jnp.int32), axis=1)
    position = target_dev * per_peer + before
    places = lax.broadcasted_iota(jnp.int32, (blocks, devices * per_peer), 1)
    placed = position[:, None] == places
    outgoing = jnp.einsum(
        "bp,bck->pck", placed.astype(jnp.bfloat16), compressed, preferred_element_type=jnp.float32
    ).astype(jnp.bfloat16)
    labels = jnp.sum(jnp.where(placed, target_pos[:, None] + 1, 0), axis=0) - 1
    arrived, arrived_labels = (
        lax.all_to_all(outgoing, "clus", split_axis=0, concat_axis=0, tiled=True),
        lax.all_to_all(labels, "clus", split_axis=0, concat_axis=0, tiled=True),
    )
    slot_ids = lax.broadcasted_iota(jnp.int32, (devices * per_peer, capacity), 1)
    landing = (arrived_labels[:, None] == slot_ids).astype(jnp.bfloat16)
    slot_rows = jnp.einsum(
        "pj,pck->jck", landing, arrived, preferred_element_type=jnp.float32
    ).astype(jnp.bfloat16)
    cluster_ids = lax.broadcasted_iota(jnp.int32, (capacity, local_clusters), 1)
    owners = (slot_target[:, None] == cluster_ids).astype(jnp.float32)
    products = jnp.einsum(
        "jck,jrk->jcr",
        slot_rows,
        lax.all_gather(u_factors, "rhs", axis=1, tiled=True),
        preferred_element_type=jnp.float32,
    )
    summed = jnp.einsum("jt,jcr->ctr", owners, products, precision=lax.Precision.HIGHEST)
    return summed.reshape(columns, local_clusters * cluster_len).astype(jnp.bfloat16)


def local(incident, v_factors, *rest):
    owners = lax.axis_size("clus")
    fits = (
        lax.axis_size("rhs") == 2 * PLACES
        and v_factors.shape[1] % 128 == 0
        and owners > 1
        and incident.shape[1] > v_factors.shape[1] * 2 * PLACES
        and owners & (owners - 1) == 0
    )
    return (paired if fits else gathered_plan)(incident, v_factors, *rest)


def solution(mesh):
    placed = (
        P("rhs", "clus"),
        P("clus", "rhs", None),
        P("clus", "rhs", None),
        P("clus"),
        P("clus"),
        P("clus"),
        P("clus"),
    )
    return jax.shard_map(
        local, mesh=mesh, in_specs=placed, out_specs=P("rhs", "clus"), check_vma=False
    )
```

```python
import functools

import jax
import jax.numpy as jnp
from jax import lax
from jax.experimental import pallas as pl
from jax.experimental.pallas import tpu as pltpu
from jax.sharding import PartitionSpec as P

VMEM = pl.BlockSpec(memory_space=pltpu.VMEM)
SMEM = pl.BlockSpec(memory_space=pltpu.SMEM)
LIMIT = 10 * 1024 * 1024


def call(body, out_shape, in_specs, name, flops=0, moved=0, scratch=()):
    out_specs = [VMEM] * len(out_shape) if isinstance(out_shape, list) else VMEM
    return pl.pallas_call(
        body,
        out_shape=out_shape,
        in_specs=in_specs,
        out_specs=out_specs,
        scratch_shapes=list(scratch),
        compiler_params=pltpu.CompilerParams(vmem_limit_bytes=LIMIT),
        cost_estimate=pl.CostEstimate(flops=flops, bytes_accessed=moved, transcendentals=0),
        name=name,
    )


def pack_body(seg, pos_ref, x_ref, *out_refs):
    half, piece = 1 - pos_ref[0], 0
    for out_ref in out_refs:
        for place in range(0, out_ref.shape[1], seg):
            start = pl.multiple_of((2 * piece + half) * seg, seg)
            out_ref[:, place : place + seg] = x_ref[:, pl.ds(start, seg)]
            piece += 1


def compress_body(seg, pos_ref, source_ref, x_ref, xl_ref, xh_ref, *refs):
    v0, v1, v2, v3, v4, out_ref, send_ref, xn_ref = refs
    half, mine = pos_ref[0], pos_ref[1]
    columns = x_ref.shape[0]
    xn_ref[:, : xl_ref.shape[1]] = xl_ref[...]
    xn_ref[:, xl_ref.shape[1] :] = xh_ref[...]
    out_ref[...] = jnp.zeros_like(out_ref)

    def run(shards):
        for block in range(out_ref.shape[0]):
            source = source_ref[block]
            own = other = 0.0
            for step, shard in enumerate(shards):
                piece = source * PLACES + jnp.bitwise_xor(mine, step)
                here = pl.multiple_of((piece * 2 + half) * seg, seg)
                there = pl.multiple_of(piece * seg, seg)
                rows = shard[block]
                own += jnp.dot(x_ref[:, pl.ds(here, seg)], rows, preferred_element_type=jnp.float32)
                other += jnp.dot(
                    xn_ref[:, pl.ds(there, seg)], rows, preferred_element_type=jnp.float32
                )
            out_ref[block, half, :columns] = own
            out_ref[block, 1 - half, :columns] = other

    inner = (mine == 1) | (mine == 2)

    @pl.when(inner)
    def _():
        run((v0, v1, v2, v3))

    @pl.when(jnp.logical_not(inner))
    def _():
        run((v0, v1, v2, v4))

    send_ref[...] = out_ref[...].astype(send_ref.dtype)


def place_columns(value, offset, store):
    width = value.shape[-1]
    shift = lax.rem(offset, width)
    turned = pltpu.roll(value, shift, value.ndim - 1)
    lane = lax.broadcasted_iota(jnp.int32, value.shape, value.ndim - 1)
    store(offset // width, jnp.where(lane >= shift, turned, 0.0))
    store(offset // width + 1, jnp.where(lane < shift, turned, 0.0))


def squeeze_body(offset_ref, used_ref, u_ref, out_ref, acc):
    acc[...] = jnp.zeros_like(acc)
    for slot in range(u_ref.shape[0]):
        value = u_ref[slot].astype(jnp.float32)
        lane = lax.broadcasted_iota(jnp.int32, value.shape, 1)

        def store(tile, part):
            acc[tile] += part

        place_columns(jnp.where(lane < used_ref[slot], value, 0.0), offset_ref[slot], store)
    out_ref[...] = acc[: out_ref.shape[0]].astype(out_ref.dtype)


def land_body(index_ref, target_ref, offset_ref, comp_ref, rows_ref):
    rows_ref[...] = jnp.zeros_like(rows_ref)
    last = rows_ref.shape[0] - 1
    for slot in range(index_ref.shape[0]):
        block, target = index_ref[slot], target_ref[slot]
        value = comp_ref[jnp.maximum(block, 0)].astype(jnp.float32)
        value = jnp.where(block >= 0, value, 0.0).reshape(rows_ref.shape[2:])

        def store(tile, part):
            rows_ref[jnp.minimum(tile, last), target] += part.astype(rows_ref.dtype)

        place_columns(value, offset_ref[slot], store)


def lined_up(ref, rows):
    return jnp.concatenate([ref[tile].reshape(rows, ref.shape[-1]) for tile in range(ref.shape[0])], axis=1)


def expand_body(seg, columns, pos_ref, rows_ref, *refs):
    own_ref, other_ref, acc = refs[-3:]
    half, mine = pos_ref[0], pos_ref[1]
    clusters, sides, padded = acc.shape[:3]

    def run(shard):
        product = lax.dot_general(
            lined_up(rows_ref, clusters * sides * padded),
            lined_up(shard, seg),
            (((1,), (1,)), ((), ())),
            preferred_element_type=jnp.float32,
        )
        acc[...] = product.reshape(acc.shape)

    if len(refs) == 4:
        run(refs[0])
    else:
        inner = (mine == 1) | (mine == 2)

        @pl.when(inner)
        def _():
            run(refs[0])

        @pl.when(jnp.logical_not(inner))
        def _():
            run(refs[1])

    for target in range(clusters):
        span = slice(target * seg, (target + 1) * seg)
        own_ref[:, span] = acc[target, half, :columns].astype(own_ref.dtype)
        other_ref[:, span] = acc[target, 1 - half, :columns].astype(other_ref.dtype)


def expand_own_body(seg, columns, pos_ref, rows_ref, u_ref, side_ref, out_ref, acc):
    half = pos_ref[0]
    clusters, padded = acc.shape[:2]
    start = pl.multiple_of(half * padded, padded)
    tiles = [
        rows_ref[tile, :, pl.ds(start, padded)].reshape(clusters * padded, rows_ref.shape[3])
        for tile in range(rows_ref.shape[0])
    ]
    rows = jnp.concatenate(tiles, axis=1)
    for shard, place in ((u_ref, half), (side_ref, 1 - half)):
        product = lax.dot_general(
            rows,
            lined_up(shard, seg),
            (((1,), (1,)), ((), ())),
            preferred_element_type=jnp.float32,
        )
        acc[...] = product.reshape(acc.shape)
        for target in range(clusters):
            start = pl.multiple_of((2 * target + place) * seg, seg)
            out_ref[:, pl.ds(start, seg)] = acc[target, :columns].astype(out_ref.dtype)


def join_body(seg, clusters, pos_ref, first_ref, *refs):
    out_ref = refs[-1]
    half, mine = pos_ref[0], pos_ref[1]
    for target in range(clusters):
        start = pl.multiple_of((target * PLACES + mine) * 2 * seg, 2 * seg)
        span = slice(2 * target * seg, 2 * (target + 1) * seg)
        out_ref[:, pl.ds(start, 2 * seg)] = first_ref[:, span]
    for step in range(1, PLACES):
        place = jnp.bitwise_xor(mine, step)
        for target in range(clusters):
            span = slice(target * seg, (target + 1) * seg)
            base = (target * PLACES + place) * 2
            here = pl.multiple_of((base + half) * seg, seg)
            there = pl.multiple_of((base + 1 - half) * seg, seg)
            out_ref[:, pl.ds(here, seg)] = refs[step - 1][:, span]
            out_ref[:, pl.ds(there, seg)] = refs[PLACES + step - 2][:, span]


def after(value, *first):
    return lax.optimization_barrier((value, *first))[0]


PLACES = 4


def paired(incident, v_factors, u_factors, block_source, block_rank, block_slot, slot_target):
    columns, width = incident.shape
    padded = -(-columns // 16) * 16
    blocks, seg, rank_max = v_factors.shape
    capacity = u_factors.shape[0]
    owners = lax.axis_size("clus")
    clusters = width // (seg * 2 * PLACES)
    me, owner = lax.axis_index("rhs"), lax.axis_index("clus")
    position = jnp.stack([me % 2, me // 2]).astype(jnp.int32)

    def move(array, pairs):
        return lax.ppermute(array, "rhs", [(2 * a + i, 2 * b + i) for a, b in pairs for i in (0, 1)])

    def across(array):
        return lax.ppermute(array, "rhs", [(p, p ^ 1) for p in range(2 * PLACES)])

    far = [(p, p ^ 2) for p in range(PLACES)]
    near = [(p, p ^ 1) for p in range(PLACES)]
    middle = [(1, 2), (2, 1)]
    ends = [(1, 0), (2, 3)]

    stages = [1 << bit for bit in reversed(range((owners - 1).bit_length()))]

    def swapped(array, stage):
        return lax.ppermute(array, "clus", [(p, p ^ stage) for p in range(owners)])

    def double(array, stage):
        return jnp.concatenate([array, swapped(array, stage)], axis=0)

    v_far, v_near = move(v_factors, far), move(v_factors, near)
    packed = call(
        functools.partial(pack_body, seg),
        [
            jax.ShapeDtypeStruct((columns, count * PLACES * seg), incident.dtype)
            for count in (clusters // 2, clusters - clusters // 2)
        ],
        [SMEM, VMEM],
        "pack",
        moved=3 * columns * width,
    )(position, incident)
    table = jnp.stack([block_slot, block_rank], axis=1)
    for stage in stages:
        table = double(table, stage)
    slots, ranks = table[:, 0], table[:, 1]
    wanted = owner * capacity + lax.broadcasted_iota(jnp.int32, (capacity, slots.shape[0]), 0)
    order = lax.broadcasted_iota(jnp.int32, (capacity, slots.shape[0]), 1)
    found = wanted == slots[None, :]
    feeding = jnp.max(jnp.where(found, order, -1), axis=1)
    used = jnp.sum(jnp.where(found, ranks[None, :], 0), axis=1)
    earlier = lax.broadcasted_iota(jnp.int32, (capacity, capacity), 1)
    earlier = earlier < lax.broadcasted_iota(jnp.int32, (capacity, capacity), 0)
    offset = jnp.sum(jnp.where(earlier, used[None, :], 0), axis=1)
    place = lax.broadcasted_iota(jnp.int32, (owners, slots.shape[0]), 0)
    held = (slots[None, :] >= place * capacity) & (slots[None, :] < (place + 1) * capacity)
    fullest = jnp.max(jnp.sum(jnp.where(held, ranks[None, :], 0), axis=1))
    tiles = sorted({-(-capacity * part // 10) for part in (5, 6, 7, 8, 10)})
    level = sum((fullest > count * rank_max).astype(jnp.int32) for count in tiles[:-1])
    squeezed = call(
        squeeze_body,
        jax.ShapeDtypeStruct(u_factors.shape, u_factors.dtype),
        [SMEM, SMEM, VMEM],
        "squeeze",
        moved=4 * u_factors.size,
        scratch=[pltpu.VMEM((capacity + 2, seg, rank_max), jnp.float32)],
    )(offset, used, u_factors)

    x_low, x_high = [across(part) for part in packed]
    v_ends = move(after(v_far, *packed), ends)
    v_middle = move(v_factors, middle)
    arrived = lax.optimization_barrier(
        (x_low, x_high, v_near, v_far, v_middle, v_ends, squeezed, level)
    )

    def rest(count, x_low, x_high, v_near, v_far, v_middle, v_ends, squeezed):
        partial, sent = call(
            functools.partial(compress_body, seg),
            [
                jax.ShapeDtypeStruct((blocks, 2, padded, rank_max), jnp.float32),
                jax.ShapeDtypeStruct((blocks, 2, padded, rank_max), jnp.bfloat16),
            ],
            [SMEM, SMEM] + [VMEM] * 8,
            "compress",
            flops=4 * blocks * columns * seg * PLACES * rank_max,
            moved=3 * columns * width + 2 * PLACES * v_factors.size,
            scratch=[pltpu.VMEM((columns, width // 2), incident.dtype)],
        )(
            position, block_source, incident, x_low, x_high,
            v_factors, v_near, v_far, v_middle, v_ends,
        )
        received = across(sent)
        target_factors = after(squeezed, sent)[:count]
        u_far, u_near = move(target_factors, far), move(target_factors, near)
        u_side = across(after(target_factors, received))
        rank_index = lax.broadcasted_iota(jnp.int32, (blocks, 1, 1, rank_max), 3)
        rows = jnp.where(
            rank_index < block_rank[:, None, None, None],
            partial + received.astype(jnp.float32),
            0.0,
        ).astype(jnp.bfloat16)

        rounds, gathered = 1 + jnp.minimum(me, 0), rows
        for stage in stages:
            other = lax.fori_loop(
                0, rounds, lambda _, array, stage=stage: swapped(array, stage), gathered
            )
            gathered = jnp.concatenate([gathered, other], axis=0)
        slot_rows = call(
            land_body,
            jax.ShapeDtypeStruct((count, clusters, 2 * padded, rank_max), jnp.bfloat16),
            [SMEM, SMEM, SMEM, VMEM],
            "land",
            moved=2 * gathered.size * (1 + clusters),
        )(feeding, slot_target, offset, gathered)

        chunk = jax.ShapeDtypeStruct((columns, clusters * seg), jnp.bfloat16)
        own_parts, other_parts = [None] * PLACES, [None] * PLACES
        work = 4 * clusters * count * columns * seg * rank_max
        first = call(
            functools.partial(expand_own_body, seg, columns),
            jax.ShapeDtypeStruct((columns, 2 * clusters * seg), jnp.bfloat16),
            [SMEM] + [VMEM] * 3,
            "expand_own",
            flops=work,
            moved=4 * target_factors.size + 2 * slot_rows.size + 4 * columns * clusters * seg,
            scratch=[pltpu.VMEM((clusters, padded, seg), jnp.float32)],
        )(position, slot_rows, target_factors, u_side)
        finished = []
        for step in range(1, PLACES):
            if step == 2:
                u_far = after(u_far, own_parts[1])
                u_ends = move(u_far, ends)
                u_middle = move(after(target_factors, u_far), middle)
            shards = [u_near] if step == 1 else [u_far] if step == 2 else [u_middle, u_ends]
            if finished:
                slot_rows = after(slot_rows, own_parts[finished[-1]])
            if len(finished) == 2:
                slot_rows = after(slot_rows, first, other_parts[finished[0]])
            own, other = call(
                functools.partial(expand_body, seg, columns),
                [chunk, chunk],
                [SMEM, VMEM] + [VMEM] * len(shards),
                "expand",
                flops=work,
                moved=2 * target_factors.size + 2 * slot_rows.size + 4 * columns * clusters * seg,
                scratch=[pltpu.VMEM((clusters, 2, padded, seg), jnp.float32)],
            )(position, slot_rows, *shards)
            own_parts[step], other_parts[step] = own, across(other)
            finished.append(step)
        return call(
            functools.partial(join_body, seg, clusters),
            jax.ShapeDtypeStruct((columns, width), jnp.bfloat16),
            [SMEM] + [VMEM] * (2 * PLACES - 1),
            "join",
            moved=4 * columns * width,
        )(position, first, *own_parts[1:], *other_parts[1:])

    return lax.switch(
        arrived[-1], [functools.partial(rest, count) for count in tiles], *arrived[:-1]
    )


def gathered_plan(
    incident, v_factors, u_factors, block_source, block_rank, block_slot, slot_target
):
    columns = incident.shape[0]
    blocks = v_factors.shape[0]
    rank_max = v_factors.shape[2]
    capacity = u_factors.shape[0]
    devices = lax.axis_size("clus")
    cluster_len = v_factors.shape[1] * lax.axis_size("rhs")
    local_clusters = incident.shape[1] // cluster_len
    per_peer = max(1, (2 * blocks + devices - 1) // devices)
    sources = jnp.take(incident.reshape(columns, local_clusters, cluster_len), block_source, axis=1)
    compressed = jnp.einsum(
        "cbr,brk->bck",
        sources,
        lax.all_gather(v_factors, "rhs", axis=1, tiled=True),
        preferred_element_type=jnp.float32,
    )
    rank_index = lax.broadcasted_iota(jnp.int32, (blocks, 1, rank_max), 2)
    compressed = jnp.where(rank_index < block_rank[:, None, None], compressed, 0.0).astype(
        jnp.bfloat16
    )
    target_dev = block_slot // capacity
    target_pos = block_slot % capacity
    later_index = lax.broadcasted_iota(jnp.int32, (blocks, blocks), 0)
    earlier_index = lax.broadcasted_iota(jnp.int32, (blocks, blocks), 1)
    same_target = target_dev[None, :] == target_dev[:, None]
    before = jnp.sum((same_target & (earlier_index < later_index)).astype(jnp.int32), axis=1)
    position = target_dev * per_peer + before
    places = lax.broadcasted_iota(jnp.int32, (blocks, devices * per_peer), 1)
    placed = position[:, None] == places
    outgoing = jnp.einsum(
        "bp,bck->pck", placed.astype(jnp.bfloat16), compressed, preferred_element_type=jnp.float32
    ).astype(jnp.bfloat16)
    labels = jnp.sum(jnp.where(placed, target_pos[:, None] + 1, 0), axis=0) - 1
    arrived, arrived_labels = (
        lax.all_to_all(outgoing, "clus", split_axis=0, concat_axis=0, tiled=True),
        lax.all_to_all(labels, "clus", split_axis=0, concat_axis=0, tiled=True),
    )
    slot_ids = lax.broadcasted_iota(jnp.int32, (devices * per_peer, capacity), 1)
    landing = (arrived_labels[:, None] == slot_ids).astype(jnp.bfloat16)
    slot_rows = jnp.einsum(
        "pj,pck->jck", landing, arrived, preferred_element_type=jnp.float32
    ).astype(jnp.bfloat16)
    cluster_ids = lax.broadcasted_iota(jnp.int32, (capacity, local_clusters), 1)
    owners = (slot_target[:, None] == cluster_ids).astype(jnp.float32)
    products = jnp.einsum(
        "jck,jrk->jcr",
        slot_rows,
        lax.all_gather(u_factors, "rhs", axis=1, tiled=True),
        preferred_element_type=jnp.float32,
    )
    summed = jnp.einsum("jt,jcr->ctr", owners, products, precision=lax.Precision.HIGHEST)
    return summed.reshape(columns, local_clusters * cluster_len).astype(jnp.bfloat16)


def local(incident, v_factors, *rest):
    owners = lax.axis_size("clus")
    fits = (
        lax.axis_size("rhs") == 2 * PLACES
        and v_factors.shape[1] % 128 == 0
        and owners > 1
        and incident.shape[1] > v_factors.shape[1] * 2 * PLACES
        and owners & (owners - 1) == 0
    )
    return (paired if fits else gathered_plan)(incident, v_factors, *rest)


def solution(mesh):
    placed = (
        P("rhs", "clus"),
        P("clus", "rhs", None),
        P("clus", "rhs", None),
        P("clus"),
        P("clus"),
        P("clus"),
        P("clus"),
    )
    return jax.shard_map(
        local, mesh=mesh, in_specs=placed, out_specs=P("rhs", "clus"), check_vma=False
    )
```

```python
import functools

import jax
import jax.numpy as jnp
from jax import lax
from jax.experimental import pallas as pl
from jax.experimental.pallas import tpu as pltpu
from jax.sharding import PartitionSpec as P

VMEM = pl.BlockSpec(memory_space=pltpu.VMEM)
SMEM = pl.BlockSpec(memory_space=pltpu.SMEM)
LIMIT = 10 * 1024 * 1024


def call(
    body, out_shape, in_specs, name, flops=0, moved=0, scratch=(), grid=(), out_specs=None
):
    if out_specs is None:
        out_specs = [VMEM] * len(out_shape) if isinstance(out_shape, list) else VMEM
    return pl.pallas_call(
        body,
        grid=grid,
        out_shape=out_shape,
        in_specs=in_specs,
        out_specs=out_specs,
        scratch_shapes=list(scratch),
        compiler_params=pltpu.CompilerParams(vmem_limit_bytes=LIMIT),
        cost_estimate=pl.CostEstimate(flops=flops, bytes_accessed=moved, transcendentals=0),
        name=name,
    )


def pack_body(seg, pos_ref, x_ref, *out_refs):
    half, piece = 1 - pos_ref[0], 0
    for out_ref in out_refs:
        for place in range(0, out_ref.shape[1], seg):
            start = pl.multiple_of((2 * piece + half) * seg, seg)
            out_ref[:, place : place + seg] = x_ref[:, pl.ds(start, seg)]
            piece += 1


def compress_body(seg, pos_ref, source_ref, x_ref, xl_ref, xh_ref, *refs):
    v0, v1, v2, v3, v4, out_ref, send_ref, xn_ref = refs
    half, mine = pos_ref[0], pos_ref[1]
    columns = x_ref.shape[0]
    xn_ref[:, : xl_ref.shape[1]] = xl_ref[...]
    xn_ref[:, xl_ref.shape[1] :] = xh_ref[...]
    out_ref[...] = jnp.zeros_like(out_ref)

    def run(shards):
        for block in range(out_ref.shape[0]):
            source = source_ref[block]
            own = other = 0.0
            for step, shard in enumerate(shards):
                piece = source * PLACES + jnp.bitwise_xor(mine, step)
                here = pl.multiple_of((piece * 2 + half) * seg, seg)
                there = pl.multiple_of(piece * seg, seg)
                rows = shard[block]
                own += jnp.dot(x_ref[:, pl.ds(here, seg)], rows, preferred_element_type=jnp.float32)
                other += jnp.dot(
                    xn_ref[:, pl.ds(there, seg)], rows, preferred_element_type=jnp.float32
                )
            out_ref[block, half, :columns] = own
            out_ref[block, 1 - half, :columns] = other

    inner = (mine == 1) | (mine == 2)

    @pl.when(inner)
    def _():
        run((v0, v1, v2, v3))

    @pl.when(jnp.logical_not(inner))
    def _():
        run((v0, v1, v2, v4))

    send_ref[...] = out_ref[...].astype(send_ref.dtype)


def place_columns(value, offset, store):
    width = value.shape[-1]
    shift = lax.rem(offset, width)
    turned = pltpu.roll(value, shift, value.ndim - 1)
    lane = lax.broadcasted_iota(jnp.int32, value.shape, value.ndim - 1)
    store(offset // width, jnp.where(lane >= shift, turned, 0.0))
    store(offset // width + 1, jnp.where(lane < shift, turned, 0.0))


def squeeze_body(offset_ref, used_ref, u_ref, out_ref, acc):
    acc[...] = jnp.zeros_like(acc)
    for slot in range(u_ref.shape[0]):
        value = u_ref[slot].astype(jnp.float32)
        lane = lax.broadcasted_iota(jnp.int32, value.shape, 1)

        def store(tile, part):
            acc[tile] += part

        place_columns(jnp.where(lane < used_ref[slot], value, 0.0), offset_ref[slot], store)
    out_ref[...] = acc[: out_ref.shape[0]].astype(out_ref.dtype)


def land_body(index_ref, target_ref, offset_ref, comp_ref, rows_ref):
    rows_ref[...] = jnp.zeros_like(rows_ref)
    last = rows_ref.shape[0] - 1
    for slot in range(index_ref.shape[0]):
        block, target = index_ref[slot], target_ref[slot]
        value = comp_ref[jnp.maximum(block, 0)].astype(jnp.float32)
        value = jnp.where(block >= 0, value, 0.0).reshape(rows_ref.shape[2:])

        def store(tile, part):
            rows_ref[jnp.minimum(tile, last), target] += part.astype(rows_ref.dtype)

        place_columns(value, offset_ref[slot], store)


def lined_up(ref, rows):
    return jnp.concatenate([ref[tile].reshape(rows, ref.shape[-1]) for tile in range(ref.shape[0])], axis=1)


def expand_body(seg, columns, pos_ref, rows_ref, *refs):
    own_ref, other_ref, acc = refs[-3:]
    half, mine = pos_ref[0], pos_ref[1]
    clusters, sides, padded = acc.shape[:3]

    def run(shard):
        product = lax.dot_general(
            lined_up(rows_ref, clusters * sides * padded),
            lined_up(shard, seg),
            (((1,), (1,)), ((), ())),
            preferred_element_type=jnp.float32,
        )
        acc[...] = product.reshape(acc.shape)

    if len(refs) == 4:
        run(refs[0])
    else:
        inner = (mine == 1) | (mine == 2)

        @pl.when(inner)
        def _():
            run(refs[0])

        @pl.when(jnp.logical_not(inner))
        def _():
            run(refs[1])

    for target in range(clusters):
        span = slice(target * seg, (target + 1) * seg)
        own_ref[:, span] = acc[target, half, :columns].astype(own_ref.dtype)
        other_ref[:, span] = acc[target, 1 - half, :columns].astype(other_ref.dtype)


def expand_own_body(seg, columns, pos_ref, rows_ref, u_ref, side_ref, out_ref, acc):
    half = pos_ref[0]
    clusters, padded = acc.shape[:2]
    start = pl.multiple_of(half * padded, padded)
    tiles = [
        rows_ref[tile, :, pl.ds(start, padded)].reshape(clusters * padded, rows_ref.shape[3])
        for tile in range(rows_ref.shape[0])
    ]
    rows = jnp.concatenate(tiles, axis=1)
    for shard, place in ((u_ref, half), (side_ref, 1 - half)):
        product = lax.dot_general(
            rows,
            lined_up(shard, seg),
            (((1,), (1,)), ((), ())),
            preferred_element_type=jnp.float32,
        )
        acc[...] = product.reshape(acc.shape)
        for target in range(clusters):
            start = pl.multiple_of((2 * target + place) * seg, seg)
            out_ref[:, pl.ds(start, seg)] = acc[target, :columns].astype(out_ref.dtype)


def join_body(seg, pos_ref, first_ref, *refs):
    out_ref = refs[-1]
    half, mine, target = pos_ref[0], pos_ref[1], pl.program_id(0)
    pair = pl.ds(pl.multiple_of(2 * target * seg, 2 * seg), 2 * seg)
    span = pl.ds(pl.multiple_of(target * seg, seg), seg)
    start = pl.multiple_of(mine * 2 * seg, 2 * seg)
    out_ref[:, pl.ds(start, 2 * seg)] = first_ref[:, pair]
    for step in range(1, PLACES):
        base = jnp.bitwise_xor(mine, step) * 2
        here = pl.multiple_of((base + half) * seg, seg)
        there = pl.multiple_of((base + 1 - half) * seg, seg)
        out_ref[:, pl.ds(here, seg)] = refs[step - 1][:, span]
        out_ref[:, pl.ds(there, seg)] = refs[PLACES + step - 2][:, span]


def after(value, *first):
    return lax.optimization_barrier((value, *first))[0]


PLACES = 4


def paired(incident, v_factors, u_factors, block_source, block_rank, block_slot, slot_target):
    columns, width = incident.shape
    padded = -(-columns // 16) * 16
    blocks, seg, rank_max = v_factors.shape
    capacity = u_factors.shape[0]
    owners = lax.axis_size("clus")
    clusters = width // (seg * 2 * PLACES)
    me, owner = lax.axis_index("rhs"), lax.axis_index("clus")
    position = jnp.stack([me % 2, me // 2]).astype(jnp.int32)

    def move(array, pairs):
        return lax.ppermute(array, "rhs", [(2 * a + i, 2 * b + i) for a, b in pairs for i in (0, 1)])

    def across(array):
        return lax.ppermute(array, "rhs", [(p, p ^ 1) for p in range(2 * PLACES)])

    far = [(p, p ^ 2) for p in range(PLACES)]
    near = [(p, p ^ 1) for p in range(PLACES)]
    middle = [(1, 2), (2, 1)]
    ends = [(1, 0), (2, 3)]

    stages = [1 << bit for bit in reversed(range((owners - 1).bit_length()))]

    def swapped(array, stage):
        return lax.ppermute(array, "clus", [(p, p ^ stage) for p in range(owners)])

    def double(array, stage):
        return jnp.concatenate([array, swapped(array, stage)], axis=0)

    v_far, v_near = move(v_factors, far), move(v_factors, near)
    packed = call(
        functools.partial(pack_body, seg),
        [
            jax.ShapeDtypeStruct((columns, count * PLACES * seg), incident.dtype)
            for count in (clusters // 2, clusters - clusters // 2)
        ],
        [SMEM, VMEM],
        "pack",
        moved=3 * columns * width,
    )(position, incident)
    table = jnp.stack([block_slot, block_rank], axis=1)
    for stage in stages:
        table = double(table, stage)
    slots, ranks = table[:, 0], table[:, 1]
    wanted = owner * capacity + lax.broadcasted_iota(jnp.int32, (capacity, slots.shape[0]), 0)
    order = lax.broadcasted_iota(jnp.int32, (capacity, slots.shape[0]), 1)
    found = wanted == slots[None, :]
    feeding = jnp.max(jnp.where(found, order, -1), axis=1)
    used = jnp.sum(jnp.where(found, ranks[None, :], 0), axis=1)
    earlier = lax.broadcasted_iota(jnp.int32, (capacity, capacity), 1)
    earlier = earlier < lax.broadcasted_iota(jnp.int32, (capacity, capacity), 0)
    offset = jnp.sum(jnp.where(earlier, used[None, :], 0), axis=1)
    place = lax.broadcasted_iota(jnp.int32, (owners, slots.shape[0]), 0)
    held = (slots[None, :] >= place * capacity) & (slots[None, :] < (place + 1) * capacity)
    fullest = jnp.max(jnp.sum(jnp.where(held, ranks[None, :], 0), axis=1))
    tiles = sorted({-(-capacity * part // 10) for part in (5, 6, 7, 8, 10)})
    level = sum((fullest > count * rank_max).astype(jnp.int32) for count in tiles[:-1])
    squeezed = call(
        squeeze_body,
        jax.ShapeDtypeStruct(u_factors.shape, u_factors.dtype),
        [SMEM, SMEM, VMEM],
        "squeeze",
        moved=4 * u_factors.size,
        scratch=[pltpu.VMEM((capacity + 2, seg, rank_max), jnp.float32)],
    )(offset, used, u_factors)

    x_low, x_high = [across(part) for part in packed]
    v_ends = move(after(v_far, *packed), ends)
    v_middle = move(v_factors, middle)
    arrived = lax.optimization_barrier(
        (x_low, x_high, v_near, v_far, v_middle, v_ends, squeezed, level)
    )

    def rest(count, x_low, x_high, v_near, v_far, v_middle, v_ends, squeezed):
        partial, sent = call(
            functools.partial(compress_body, seg),
            [
                jax.ShapeDtypeStruct((blocks, 2, padded, rank_max), jnp.float32),
                jax.ShapeDtypeStruct((blocks, 2, padded, rank_max), jnp.bfloat16),
            ],
            [SMEM, SMEM] + [VMEM] * 8,
            "compress",
            flops=4 * blocks * columns * seg * PLACES * rank_max,
            moved=3 * columns * width + 2 * PLACES * v_factors.size,
            scratch=[pltpu.VMEM((columns, width // 2), incident.dtype)],
        )(
            position, block_source, incident, x_low, x_high,
            v_factors, v_near, v_far, v_middle, v_ends,
        )
        received = across(sent)
        target_factors = after(squeezed, sent)[:count]
        u_far, u_near = move(target_factors, far), move(target_factors, near)
        u_side = across(after(target_factors, received))
        rank_index = lax.broadcasted_iota(jnp.int32, (blocks, 1, 1, rank_max), 3)
        rows = jnp.where(
            rank_index < block_rank[:, None, None, None],
            partial + received.astype(jnp.float32),
            0.0,
        ).astype(jnp.bfloat16)

        rounds, gathered = 1 + jnp.minimum(me, 0), rows
        for stage in stages:
            other = lax.fori_loop(
                0, rounds, lambda _, array, stage=stage: swapped(array, stage), gathered
            )
            gathered = jnp.concatenate([gathered, other], axis=0)
        slot_rows = call(
            land_body,
            jax.ShapeDtypeStruct((count, clusters, 2 * padded, rank_max), jnp.bfloat16),
            [SMEM, SMEM, SMEM, VMEM],
            "land",
            moved=2 * gathered.size * (1 + clusters),
        )(feeding, slot_target, offset, gathered)

        chunk = jax.ShapeDtypeStruct((columns, clusters * seg), jnp.bfloat16)
        own_parts, other_parts = [None] * PLACES, [None] * PLACES
        work = 4 * clusters * count * columns * seg * rank_max
        first = call(
            functools.partial(expand_own_body, seg, columns),
            jax.ShapeDtypeStruct((columns, 2 * clusters * seg), jnp.bfloat16),
            [SMEM] + [VMEM] * 3,
            "expand_own",
            flops=work,
            moved=4 * target_factors.size + 2 * slot_rows.size + 4 * columns * clusters * seg,
            scratch=[pltpu.VMEM((clusters, padded, seg), jnp.float32)],
        )(position, slot_rows, target_factors, u_side)
        finished = []
        for step in range(1, PLACES):
            if step == 2:
                u_far = after(u_far, own_parts[1])
                u_ends = move(u_far, ends)
                u_middle = move(after(target_factors, u_far), middle)
            shards = [u_near] if step == 1 else [u_far] if step == 2 else [u_middle, u_ends]
            if finished:
                slot_rows = after(slot_rows, own_parts[finished[-1]])
            if len(finished) == 2:
                slot_rows = after(slot_rows, first, other_parts[finished[0]])
            own, other = call(
                functools.partial(expand_body, seg, columns),
                [chunk, chunk],
                [SMEM, VMEM] + [VMEM] * len(shards),
                "expand",
                flops=work,
                moved=2 * target_factors.size + 2 * slot_rows.size + 4 * columns * clusters * seg,
                scratch=[pltpu.VMEM((clusters, 2, padded, seg), jnp.float32)],
            )(position, slot_rows, *shards)
            own_parts[step], other_parts[step] = own, across(other)
            finished.append(step)
        return call(
            functools.partial(join_body, seg),
            jax.ShapeDtypeStruct((columns, width), jnp.bfloat16),
            [SMEM] + [VMEM] * (2 * PLACES - 1),
            "join",
            moved=4 * columns * width,
            grid=(clusters,),
            out_specs=pl.BlockSpec((columns, width // clusters), lambda target: (0, target)),
        )(position, first, *own_parts[1:], *other_parts[1:])

    return lax.switch(
        arrived[-1], [functools.partial(rest, count) for count in tiles], *arrived[:-1]
    )


def gathered_plan(
    incident, v_factors, u_factors, block_source, block_rank, block_slot, slot_target
):
    columns = incident.shape[0]
    blocks = v_factors.shape[0]
    rank_max = v_factors.shape[2]
    capacity = u_factors.shape[0]
    devices = lax.axis_size("clus")
    cluster_len = v_factors.shape[1] * lax.axis_size("rhs")
    local_clusters = incident.shape[1] // cluster_len
    per_peer = max(1, (2 * blocks + devices - 1) // devices)
    sources = jnp.take(incident.reshape(columns, local_clusters, cluster_len), block_source, axis=1)
    compressed = jnp.einsum(
        "cbr,brk->bck",
        sources,
        lax.all_gather(v_factors, "rhs", axis=1, tiled=True),
        preferred_element_type=jnp.float32,
    )
    rank_index = lax.broadcasted_iota(jnp.int32, (blocks, 1, rank_max), 2)
    compressed = jnp.where(rank_index < block_rank[:, None, None], compressed, 0.0).astype(
        jnp.bfloat16
    )
    target_dev = block_slot // capacity
    target_pos = block_slot % capacity
    later_index = lax.broadcasted_iota(jnp.int32, (blocks, blocks), 0)
    earlier_index = lax.broadcasted_iota(jnp.int32, (blocks, blocks), 1)
    same_target = target_dev[None, :] == target_dev[:, None]
    before = jnp.sum((same_target & (earlier_index < later_index)).astype(jnp.int32), axis=1)
    position = target_dev * per_peer + before
    places = lax.broadcasted_iota(jnp.int32, (blocks, devices * per_peer), 1)
    placed = position[:, None] == places
    outgoing = jnp.einsum(
        "bp,bck->pck", placed.astype(jnp.bfloat16), compressed, preferred_element_type=jnp.float32
    ).astype(jnp.bfloat16)
    labels = jnp.sum(jnp.where(placed, target_pos[:, None] + 1, 0), axis=0) - 1
    arrived, arrived_labels = (
        lax.all_to_all(outgoing, "clus", split_axis=0, concat_axis=0, tiled=True),
        lax.all_to_all(labels, "clus", split_axis=0, concat_axis=0, tiled=True),
    )
    slot_ids = lax.broadcasted_iota(jnp.int32, (devices * per_peer, capacity), 1)
    landing = (arrived_labels[:, None] == slot_ids).astype(jnp.bfloat16)
    slot_rows = jnp.einsum(
        "pj,pck->jck", landing, arrived, preferred_element_type=jnp.float32
    ).astype(jnp.bfloat16)
    cluster_ids = lax.broadcasted_iota(jnp.int32, (capacity, local_clusters), 1)
    owners = (slot_target[:, None] == cluster_ids).astype(jnp.float32)
    products = jnp.einsum(
        "jck,jrk->jcr",
        slot_rows,
        lax.all_gather(u_factors, "rhs", axis=1, tiled=True),
        preferred_element_type=jnp.float32,
    )
    summed = jnp.einsum("jt,jcr->ctr", owners, products, precision=lax.Precision.HIGHEST)
    return summed.reshape(columns, local_clusters * cluster_len).astype(jnp.bfloat16)


def local(incident, v_factors, *rest):
    owners = lax.axis_size("clus")
    fits = (
        lax.axis_size("rhs") == 2 * PLACES
        and v_factors.shape[1] % 128 == 0
        and owners > 1
        and incident.shape[1] > v_factors.shape[1] * 2 * PLACES
        and owners & (owners - 1) == 0
    )
    return (paired if fits else gathered_plan)(incident, v_factors, *rest)


def solution(mesh):
    placed = (
        P("rhs", "clus"),
        P("clus", "rhs", None),
        P("clus", "rhs", None),
        P("clus"),
        P("clus"),
        P("clus"),
        P("clus"),
    )
    return jax.shard_map(
        local, mesh=mesh, in_specs=placed, out_specs=P("rhs", "clus"), check_vma=False
    )
```

```python
import functools

import jax
import jax.numpy as jnp
from jax import lax
from jax.experimental import pallas as pl
from jax.experimental.pallas import tpu as pltpu
from jax.sharding import PartitionSpec as P

VMEM = pl.BlockSpec(memory_space=pltpu.VMEM)
SMEM = pl.BlockSpec(memory_space=pltpu.SMEM)
LIMIT = 10 * 1024 * 1024


def call(body, out_shape, in_specs, name, flops=0, moved=0, scratch=()):
    out_specs = [VMEM] * len(out_shape) if isinstance(out_shape, list) else VMEM
    return pl.pallas_call(
        body,
        out_shape=out_shape,
        in_specs=in_specs,
        out_specs=out_specs,
        scratch_shapes=list(scratch),
        compiler_params=pltpu.CompilerParams(vmem_limit_bytes=LIMIT),
        cost_estimate=pl.CostEstimate(flops=flops, bytes_accessed=moved, transcendentals=0),
        name=name,
    )


def pack_body(seg, pos_ref, x_ref, *refs):
    *out_refs, own_ref = refs
    half, piece = pos_ref[0], 0
    for out_ref in out_refs:
        for place in range(0, out_ref.shape[1], seg):
            there = pl.multiple_of((2 * piece + 1 - half) * seg, seg)
            here = pl.multiple_of((2 * piece + half) * seg, seg)
            out_ref[:, place : place + seg] = x_ref[:, pl.ds(there, seg)]
            own_ref[:, piece * seg : (piece + 1) * seg] = x_ref[:, pl.ds(here, seg)]
            piece += 1


def compress_body(seg, pos_ref, source_ref, x_ref, xl_ref, xh_ref, *refs):
    v0, v1, v2, v3, v4, out_ref, send_ref, xn_ref = refs
    half, mine = pos_ref[0], pos_ref[1]
    columns = x_ref.shape[0]
    xn_ref[:, : xl_ref.shape[1]] = xl_ref[...]
    xn_ref[:, xl_ref.shape[1] :] = xh_ref[...]
    out_ref[...] = jnp.zeros_like(out_ref)

    def run(shards):
        for block in range(out_ref.shape[0]):
            source = source_ref[block]
            own = other = 0.0
            for step, shard in enumerate(shards):
                piece = source * PLACES + jnp.bitwise_xor(mine, step)
                span = pl.ds(pl.multiple_of(piece * seg, seg), seg)
                rows = shard[block]
                own += jnp.dot(x_ref[:, span], rows, preferred_element_type=jnp.float32)
                other += jnp.dot(xn_ref[:, span], rows, preferred_element_type=jnp.float32)
            out_ref[block, half, :columns] = own
            out_ref[block, 1 - half, :columns] = other

    inner = (mine == 1) | (mine == 2)

    @pl.when(inner)
    def _():
        run((v0, v1, v2, v3))

    @pl.when(jnp.logical_not(inner))
    def _():
        run((v0, v1, v2, v4))

    send_ref[...] = out_ref[...].astype(send_ref.dtype)


def place_columns(value, offset, store):
    width = value.shape[-1]
    shift = lax.rem(offset, width)
    turned = pltpu.roll(value, shift, value.ndim - 1)
    lane = lax.broadcasted_iota(jnp.int32, value.shape, value.ndim - 1)
    store(offset // width, jnp.where(lane >= shift, turned, 0.0))
    store(offset // width + 1, jnp.where(lane < shift, turned, 0.0))


def squeeze_body(offset_ref, used_ref, u_ref, out_ref, acc):
    acc[...] = jnp.zeros_like(acc)
    for slot in range(u_ref.shape[0]):
        value = u_ref[slot].astype(jnp.float32)
        lane = lax.broadcasted_iota(jnp.int32, value.shape, 1)

        def store(tile, part):
            acc[tile] += part

        place_columns(jnp.where(lane < used_ref[slot], value, 0.0), offset_ref[slot], store)
    out_ref[...] = acc[: out_ref.shape[0]].astype(out_ref.dtype)


def land_body(index_ref, target_ref, offset_ref, comp_ref, rows_ref):
    rows_ref[...] = jnp.zeros_like(rows_ref)
    last = rows_ref.shape[0] - 1
    for slot in range(index_ref.shape[0]):
        block, target = index_ref[slot], target_ref[slot]
        value = comp_ref[jnp.maximum(block, 0)].astype(jnp.float32)
        value = jnp.where(block >= 0, value, 0.0).reshape(rows_ref.shape[2:])

        def store(tile, part):
            rows_ref[jnp.minimum(tile, last), target] += part.astype(rows_ref.dtype)

        place_columns(value, offset_ref[slot], store)


def lined_up(ref, rows):
    return jnp.concatenate([ref[tile].reshape(rows, ref.shape[-1]) for tile in range(ref.shape[0])], axis=1)


def expand_body(seg, columns, pos_ref, rows_ref, *refs):
    own_ref, other_ref, acc = refs[-3:]
    half, mine = pos_ref[0], pos_ref[1]
    clusters, sides, padded = acc.shape[:3]

    def run(shard):
        product = lax.dot_general(
            lined_up(rows_ref, clusters * sides * padded),
            lined_up(shard, seg),
            (((1,), (1,)), ((), ())),
            preferred_element_type=jnp.float32,
        )
        acc[...] = product.reshape(acc.shape)

    if len(refs) == 4:
        run(refs[0])
    else:
        inner = (mine == 1) | (mine == 2)

        @pl.when(inner)
        def _():
            run(refs[0])

        @pl.when(jnp.logical_not(inner))
        def _():
            run(refs[1])

    for target in range(clusters):
        span = slice(target * seg, (target + 1) * seg)
        own_ref[:, span] = acc[target, half, :columns].astype(own_ref.dtype)
        other_ref[:, span] = acc[target, 1 - half, :columns].astype(other_ref.dtype)


def expand_own_body(seg, columns, pos_ref, rows_ref, u_ref, side_ref, out_ref, acc):
    half = pos_ref[0]
    clusters, padded = acc.shape[:2]
    start = pl.multiple_of(half * padded, padded)
    tiles = [
        rows_ref[tile, :, pl.ds(start, padded)].reshape(clusters * padded, rows_ref.shape[3])
        for tile in range(rows_ref.shape[0])
    ]
    rows = jnp.concatenate(tiles, axis=1)
    for shard, place in ((u_ref, half), (side_ref, 1 - half)):
        product = lax.dot_general(
            rows,
            lined_up(shard, seg),
            (((1,), (1,)), ((), ())),
            preferred_element_type=jnp.float32,
        )
        acc[...] = product.reshape(acc.shape)
        for target in range(clusters):
            start = pl.multiple_of((2 * target + place) * seg, seg)
            out_ref[:, pl.ds(start, seg)] = acc[target, :columns].astype(out_ref.dtype)


def join_body(seg, clusters, pos_ref, first_ref, *refs):
    out_ref = refs[-1]
    half, mine = pos_ref[0], pos_ref[1]
    for target in range(clusters):
        start = pl.multiple_of((target * PLACES + mine) * 2 * seg, 2 * seg)
        span = slice(2 * target * seg, 2 * (target + 1) * seg)
        out_ref[:, pl.ds(start, 2 * seg)] = first_ref[:, span]
    for step in range(1, PLACES):
        place = jnp.bitwise_xor(mine, step)
        for target in range(clusters):
            span = slice(target * seg, (target + 1) * seg)
            base = (target * PLACES + place) * 2
            here = pl.multiple_of((base + half) * seg, seg)
            there = pl.multiple_of((base + 1 - half) * seg, seg)
            out_ref[:, pl.ds(here, seg)] = refs[step - 1][:, span]
            out_ref[:, pl.ds(there, seg)] = refs[PLACES + step - 2][:, span]


def after(value, *first):
    return lax.optimization_barrier((value, *first))[0]


PLACES = 4


def paired(incident, v_factors, u_factors, block_source, block_rank, block_slot, slot_target):
    columns, width = incident.shape
    padded = -(-columns // 16) * 16
    blocks, seg, rank_max = v_factors.shape
    capacity = u_factors.shape[0]
    owners = lax.axis_size("clus")
    clusters = width // (seg * 2 * PLACES)
    me, owner = lax.axis_index("rhs"), lax.axis_index("clus")
    position = jnp.stack([me % 2, me // 2]).astype(jnp.int32)

    def move(array, pairs):
        return lax.ppermute(array, "rhs", [(2 * a + i, 2 * b + i) for a, b in pairs for i in (0, 1)])

    def across(array):
        return lax.ppermute(array, "rhs", [(p, p ^ 1) for p in range(2 * PLACES)])

    far = [(p, p ^ 2) for p in range(PLACES)]
    near = [(p, p ^ 1) for p in range(PLACES)]
    middle = [(1, 2), (2, 1)]
    ends = [(1, 0), (2, 3)]

    stages = [1 << bit for bit in reversed(range((owners - 1).bit_length()))]

    def swapped(array, stage):
        return lax.ppermute(array, "clus", [(p, p ^ stage) for p in range(owners)])

    def double(array, stage):
        return jnp.concatenate([array, swapped(array, stage)], axis=0)

    v_far, v_near = move(v_factors, far), move(v_factors, near)
    *packed, own_half = call(
        functools.partial(pack_body, seg),
        [
            jax.ShapeDtypeStruct((columns, count * PLACES * seg), incident.dtype)
            for count in (clusters // 2, clusters - clusters // 2, clusters)
        ],
        [SMEM, VMEM],
        "pack",
        moved=3 * columns * width,
    )(position, incident)
    table = jnp.stack([block_slot, block_rank], axis=1)
    for stage in stages:
        table = double(table, stage)
    slots, ranks = table[:, 0], table[:, 1]
    wanted = owner * capacity + lax.broadcasted_iota(jnp.int32, (capacity, slots.shape[0]), 0)
    order = lax.broadcasted_iota(jnp.int32, (capacity, slots.shape[0]), 1)
    found = wanted == slots[None, :]
    feeding = jnp.max(jnp.where(found, order, -1), axis=1)
    used = jnp.sum(jnp.where(found, ranks[None, :], 0), axis=1)
    earlier = lax.broadcasted_iota(jnp.int32, (capacity, capacity), 1)
    earlier = earlier < lax.broadcasted_iota(jnp.int32, (capacity, capacity), 0)
    offset = jnp.sum(jnp.where(earlier, used[None, :], 0), axis=1)
    place = lax.broadcasted_iota(jnp.int32, (owners, slots.shape[0]), 0)
    held = (slots[None, :] >= place * capacity) & (slots[None, :] < (place + 1) * capacity)
    fullest = jnp.max(jnp.sum(jnp.where(held, ranks[None, :], 0), axis=1))
    tiles = sorted({-(-capacity * part // 10) for part in (5, 6, 7, 8, 10)})
    level = sum((fullest > count * rank_max).astype(jnp.int32) for count in tiles[:-1])
    squeezed = call(
        squeeze_body,
        jax.ShapeDtypeStruct(u_factors.shape, u_factors.dtype),
        [SMEM, SMEM, VMEM],
        "squeeze",
        moved=4 * u_factors.size,
        scratch=[pltpu.VMEM((capacity + 2, seg, rank_max), jnp.float32)],
    )(offset, used, u_factors)

    x_low, x_high = [across(part) for part in packed]
    v_ends = move(after(v_far, *packed), ends)
    v_middle = move(v_factors, middle)
    arrived = lax.optimization_barrier(
        (x_low, x_high, v_near, v_far, v_middle, v_ends, squeezed, level)
    )

    def rest(count, x_low, x_high, v_near, v_far, v_middle, v_ends, squeezed):
        partial, sent = call(
            functools.partial(compress_body, seg),
            [
                jax.ShapeDtypeStruct((blocks, 2, padded, rank_max), jnp.float32),
                jax.ShapeDtypeStruct((blocks, 2, padded, rank_max), jnp.bfloat16),
            ],
            [SMEM, SMEM] + [VMEM] * 8,
            "compress",
            flops=4 * blocks * columns * seg * PLACES * rank_max,
            moved=3 * columns * width + 2 * PLACES * v_factors.size,
            scratch=[pltpu.VMEM((columns, width // 2), incident.dtype)],
        )(
            position, block_source, own_half, x_low, x_high,
            v_factors, v_near, v_far, v_middle, v_ends,
        )
        received = across(sent)
        target_factors = after(squeezed, sent)[:count]
        u_far, u_near = move(target_factors, far), move(target_factors, near)
        u_side = across(after(target_factors, received))
        rank_index = lax.broadcasted_iota(jnp.int32, (blocks, 1, 1, rank_max), 3)
        rows = jnp.where(
            rank_index < block_rank[:, None, None, None],
            partial + received.astype(jnp.float32),
            0.0,
        ).astype(jnp.bfloat16)

        rounds, gathered = 1 + jnp.minimum(me, 0), rows
        for stage in stages:
            other = lax.fori_loop(
                0, rounds, lambda _, array, stage=stage: swapped(array, stage), gathered
            )
            gathered = jnp.concatenate([gathered, other], axis=0)
        slot_rows = call(
            land_body,
            jax.ShapeDtypeStruct((count, clusters, 2 * padded, rank_max), jnp.bfloat16),
            [SMEM, SMEM, SMEM, VMEM],
            "land",
            moved=2 * gathered.size * (1 + clusters),
        )(feeding, slot_target, offset, gathered)

        chunk = jax.ShapeDtypeStruct((columns, clusters * seg), jnp.bfloat16)
        own_parts, other_parts = [None] * PLACES, [None] * PLACES
        work = 4 * clusters * count * columns * seg * rank_max
        first = call(
            functools.partial(expand_own_body, seg, columns),
            jax.ShapeDtypeStruct((columns, 2 * clusters * seg), jnp.bfloat16),
            [SMEM] + [VMEM] * 3,
            "expand_own",
            flops=work,
            moved=4 * target_factors.size + 2 * slot_rows.size + 4 * columns * clusters * seg,
            scratch=[pltpu.VMEM((clusters, padded, seg), jnp.float32)],
        )(position, slot_rows, target_factors, u_side)
        finished = []
        for step in range(1, PLACES):
            if step == 2:
                u_far = after(u_far, own_parts[1])
                u_ends = move(u_far, ends)
                u_middle = move(after(target_factors, u_far), middle)
            shards = [u_near] if step == 1 else [u_far] if step == 2 else [u_middle, u_ends]
            if finished:
                slot_rows = after(slot_rows, own_parts[finished[-1]])
            if len(finished) == 2:
                slot_rows = after(slot_rows, first, other_parts[finished[0]])
            own, other = call(
                functools.partial(expand_body, seg, columns),
                [chunk, chunk],
                [SMEM, VMEM] + [VMEM] * len(shards),
                "expand",
                flops=work,
                moved=2 * target_factors.size + 2 * slot_rows.size + 4 * columns * clusters * seg,
                scratch=[pltpu.VMEM((clusters, 2, padded, seg), jnp.float32)],
            )(position, slot_rows, *shards)
            own_parts[step], other_parts[step] = own, across(other)
            finished.append(step)
        return call(
            functools.partial(join_body, seg, clusters),
            jax.ShapeDtypeStruct((columns, width), jnp.bfloat16),
            [SMEM] + [VMEM] * (2 * PLACES - 1),
            "join",
            moved=4 * columns * width,
        )(position, first, *own_parts[1:], *other_parts[1:])

    return lax.switch(
        arrived[-1], [functools.partial(rest, count) for count in tiles], *arrived[:-1]
    )


def gathered_plan(
    incident, v_factors, u_factors, block_source, block_rank, block_slot, slot_target
):
    columns = incident.shape[0]
    blocks = v_factors.shape[0]
    rank_max = v_factors.shape[2]
    capacity = u_factors.shape[0]
    devices = lax.axis_size("clus")
    cluster_len = v_factors.shape[1] * lax.axis_size("rhs")
    local_clusters = incident.shape[1] // cluster_len
    per_peer = max(1, (2 * blocks + devices - 1) // devices)
    sources = jnp.take(incident.reshape(columns, local_clusters, cluster_len), block_source, axis=1)
    compressed = jnp.einsum(
        "cbr,brk->bck",
        sources,
        lax.all_gather(v_factors, "rhs", axis=1, tiled=True),
        preferred_element_type=jnp.float32,
    )
    rank_index = lax.broadcasted_iota(jnp.int32, (blocks, 1, rank_max), 2)
    compressed = jnp.where(rank_index < block_rank[:, None, None], compressed, 0.0).astype(
        jnp.bfloat16
    )
    target_dev = block_slot // capacity
    target_pos = block_slot % capacity
    later_index = lax.broadcasted_iota(jnp.int32, (blocks, blocks), 0)
    earlier_index = lax.broadcasted_iota(jnp.int32, (blocks, blocks), 1)
    same_target = target_dev[None, :] == target_dev[:, None]
    before = jnp.sum((same_target & (earlier_index < later_index)).astype(jnp.int32), axis=1)
    position = target_dev * per_peer + before
    places = lax.broadcasted_iota(jnp.int32, (blocks, devices * per_peer), 1)
    placed = position[:, None] == places
    outgoing = jnp.einsum(
        "bp,bck->pck", placed.astype(jnp.bfloat16), compressed, preferred_element_type=jnp.float32
    ).astype(jnp.bfloat16)
    labels = jnp.sum(jnp.where(placed, target_pos[:, None] + 1, 0), axis=0) - 1
    arrived, arrived_labels = (
        lax.all_to_all(outgoing, "clus", split_axis=0, concat_axis=0, tiled=True),
        lax.all_to_all(labels, "clus", split_axis=0, concat_axis=0, tiled=True),
    )
    slot_ids = lax.broadcasted_iota(jnp.int32, (devices * per_peer, capacity), 1)
    landing = (arrived_labels[:, None] == slot_ids).astype(jnp.bfloat16)
    slot_rows = jnp.einsum(
        "pj,pck->jck", landing, arrived, preferred_element_type=jnp.float32
    ).astype(jnp.bfloat16)
    cluster_ids = lax.broadcasted_iota(jnp.int32, (capacity, local_clusters), 1)
    owners = (slot_target[:, None] == cluster_ids).astype(jnp.float32)
    products = jnp.einsum(
        "jck,jrk->jcr",
        slot_rows,
        lax.all_gather(u_factors, "rhs", axis=1, tiled=True),
        preferred_element_type=jnp.float32,
    )
    summed = jnp.einsum("jt,jcr->ctr", owners, products, precision=lax.Precision.HIGHEST)
    return summed.reshape(columns, local_clusters * cluster_len).astype(jnp.bfloat16)


def local(incident, v_factors, *rest):
    owners = lax.axis_size("clus")
    fits = (
        lax.axis_size("rhs") == 2 * PLACES
        and v_factors.shape[1] % 128 == 0
        and owners > 1
        and incident.shape[1] > v_factors.shape[1] * 2 * PLACES
        and owners & (owners - 1) == 0
    )
    return (paired if fits else gathered_plan)(incident, v_factors, *rest)


def solution(mesh):
    placed = (
        P("rhs", "clus"),
        P("clus", "rhs", None),
        P("clus", "rhs", None),
        P("clus"),
        P("clus"),
        P("clus"),
        P("clus"),
    )
    return jax.shard_map(
        local, mesh=mesh, in_specs=placed, out_specs=P("rhs", "clus"), check_vma=False
    )
```
